512 devices in a mesh: lon: 64 (over z_lo, x, core), lat: 8 (over z_hi, y).
Axes of the slice: x: 4, y: 4, z: 16 (z_hi: 2, z_lo: 8; z = z_hi * 8 + z_lo), core: 2. Of those that a mesh axis runs over, the one named last changes fastest.
Arguments:
- fields: bfloat16 [2, 96, 1536, 192], P(None, 'lat', 'lon'), may hold values from -50 to 50
- fine_bias: float32 [16, 1, 6, 23, 144], P('lat'), may hold values from -4 to 304
- fine_qkv: bfloat16 [192, 576], replicated, may hold values from -0.4375 to 0.4375
- fine_proj: bfloat16 [192, 192], replicated, may hold values from -0.4375 to 0.4375
- fine_up: bfloat16 [192, 768], replicated, may hold values from -0.4375 to 0.4375
- fine_down: bfloat16 [768, 192], replicated, may hold values from -0.21875 to 0.21875
- merge_weight: bfloat16 [768, 384], replicated, may hold values from -0.21875 to 0.21875
- coarse_bias: float32 [8, 1, 12, 23, 144], P('lat'), may hold values from -4 to 304
- coarse_qkv: bfloat16 [384, 1152], replicated, may hold values from -0.3125 to 0.3125
- coarse_proj: bfloat16 [384, 384], replicated, may hold values from -0.3125 to 0.3125
- coarse_up: bfloat16 [384, 1536], replicated, may hold values from -0.3125 to 0.3125
- coarse_down: bfloat16 [1536, 384], replicated, may hold values from -0.15625 to 0.15625
Outputs:
- coarse_fields: bfloat16 [2, 48, 768, 384], P(None, 'lat', 'lon')
The draws below stay inside these ranges and needn't reach their ends.
All inputs are finite; a program needn't handle non-finite values.
Results may differ from the reference program's by a relative error of at most 0.024.
Values may be sent and summed in bfloat16 or wider, within the bound.
No kernel may reach another device: no remote copies, remote signals or barrier semaphores. Data moves between devices by JAX's collectives and lax.ppermute only.
A program may use at most 128 MiB of HBM per device.

```python
import jax
import jax.numpy as jnp
from jax import lax

C1 = 192
C2 = 384
HEADS1 = 6
HEADS2 = 12
FF1 = 768
FF2 = 1536
HD = 32
WZ = 2
WLAT = 6
WLON = 12
PLEV = 2
LAT = 96
LON = 1536


def drawn_table(key, extent):
    return jnp.clip(jax.random.normal(key, extent, jnp.float32), -4.0, 4.0)


def draw_fine_bias(key, part):
    key = jax.random.fold_in(key, 11)
    extent = (LAT // WLAT, PLEV // WZ, HEADS1, 2 * WLON - 1, 4 * WLAT * WLAT)
    return drawn_table(key, extent)


def draw_coarse_bias(key, part):
    key = jax.random.fold_in(key, 23)
    extent = (LAT // (2 * WLAT), PLEV // WZ, HEADS2, 2 * WLON - 1, 4 * WLAT * WLAT)
    return drawn_table(key, extent)


def draw_fields(key, part):
    key = jax.random.fold_in(key, 5)
    extent = (PLEV, LAT, LON, C1)
    return jnp.clip(jax.random.normal(key, extent, jnp.float32), -6.0, 6.0).astype(jnp.bfloat16)


def bell_draw(stream_key, shape, width, most, held_as=jnp.bfloat16):
    values = width * jax.random.normal(stream_key, shape, jnp.float32)
    return jnp.clip(values, min=-most, max=most).astype(held_as)


def setup_inputs(seed: int = 0) -> dict:
    key_list = jax.random.split(jax.random.key(seed), 13)
    return {
        "fields": draw_fields(jax.random.fold_in(key_list[12], 71), 0),
        "fine_bias": draw_fine_bias(jax.random.fold_in(key_list[12], 71), 0),
        "fine_qkv": bell_draw(key_list[2], (C1, 3 * C1), C1 ** -0.5, 0.4375),
        "fine_proj": bell_draw(key_list[3], (C1, C1), C1 ** -0.5, 0.4375),
        "fine_up": bell_draw(key_list[4], (C1, FF1), C1 ** -0.5, 0.4375),
        "fine_down": bell_draw(key_list[5], (FF1, C1), FF1 ** -0.5, 0.21875),
        "merge_weight": bell_draw(key_list[6], (4 * C1, C2), (4 * C1) ** -0.5, 0.21875),
        "coarse_bias": draw_coarse_bias(jax.random.fold_in(key_list[12], 71), 0),
        "coarse_qkv": bell_draw(key_list[8], (C2, 3 * C2), C2 ** -0.5, 0.3125),
        "coarse_proj": bell_draw(key_list[9], (C2, C2), C2 ** -0.5, 0.3125),
        "coarse_up": bell_draw(key_list[10], (C2, FF2), C2 ** -0.5, 0.3125),
        "coarse_down": bell_draw(key_list[11], (FF2, C2), FF2 ** -0.5, 0.15625),
    }


EPSILON = 1e-05

def layer_norm(values):
    centred = values - lax.optimization_barrier(jnp.mean(values, axis=-1, keepdims=True))
    variance = lax.optimization_barrier(jnp.mean(centred * centred, axis=-1, keepdims=True))
    return centred * lax.rsqrt(variance + EPSILON)

def expand_bias(bias_table):
    offsets = jnp.arange(WLON, dtype=jnp.int32)
    distance = jnp.arange(2 * WLON - 1, dtype=jnp.int32)
    one_hot = (offsets[:, None, None] - offsets[None, :, None] + WLON - 1 == distance[None, None, :]).astype(jnp.float32)
    expanded = jnp.einsum('lzhdc,qkd->lzhcqk', bias_table, one_hot, precision=lax.Precision.HIGHEST)
    row_windows = bias_table.shape[0]
    level_windows = bias_table.shape[1]
    head_count = bias_table.shape[2]
    expanded = expanded.reshape(row_windows, level_windows, head_count, WZ, WZ, WLAT, WLAT, WLON, WLON)
    expanded = expanded.transpose(1, 0, 2, 3, 5, 7, 4, 6, 8)
    return expanded.reshape(level_windows, row_windows, head_count, WZ * WLAT * WLON, WZ * WLAT * WLON)

def window_valid(level_count, row_count, row_offset, row_total):
    level_wrap = (jnp.arange(level_count, dtype=jnp.int32) == level_count - 1).astype(jnp.int32)
    row_wrap = (row_offset + jnp.arange(row_count, dtype=jnp.int32) >= row_total - WLAT // 2).astype(jnp.int32)
    region = level_wrap[:, None] * 2 + row_wrap[None, :]
    region = region.reshape(level_count // WZ, WZ, row_count // WLAT, WLAT).transpose(0, 2, 1, 3)
    region = jnp.broadcast_to(region[..., None], region.shape + (WLON,))
    region = region.reshape(level_count // WZ, row_count // WLAT, WZ * WLAT * WLON)
    return region[..., :, None] == region[..., None, :]

def attend(tokens, w_qkv, w_proj, full_bias, pair_valid):
    level_count, row_count, column_count, feature_width = tokens.shape
    head_count = feature_width // HD
    normed = layer_norm(tokens.astype(jnp.float32)).astype(jnp.bfloat16)
    projected = jnp.dot(normed.reshape(-1, feature_width), w_qkv, preferred_element_type=jnp.float32).astype(jnp.bfloat16)
    projected = projected.reshape(level_count // WZ, WZ, row_count // WLAT, WLAT, column_count // WLON, WLON, 3, head_count, HD)
    projected = projected.transpose(6, 0, 2, 4, 7, 1, 3, 5, 8)
    projected = projected.reshape(3, level_count // WZ, row_count // WLAT, column_count // WLON, head_count, WZ * WLAT * WLON, HD)
    queries = projected[0].astype(jnp.float32)
    key_rows = projected[1].astype(jnp.float32)
    value_rows = projected[2].astype(jnp.float32)
    scores = jnp.einsum('zlohqd,zlohkd->zlohqk', queries, key_rows) * HD ** (-0.5) + full_bias[:, :, None]
    scores = jnp.where(pair_valid[:, :, None, None], scores, -1e+30)
    weights_soft = jax.nn.softmax(scores, axis=-1).astype(jnp.bfloat16)
    mixed = jnp.einsum('zlohqk,zlohkd->zlohqd', weights_soft.astype(jnp.float32), value_rows).astype(jnp.bfloat16)
    mixed = mixed.reshape(level_count // WZ, row_count // WLAT, column_count // WLON, head_count, WZ, WLAT, WLON, HD)
    mixed = mixed.transpose(0, 4, 1, 5, 2, 6, 3, 7).reshape(-1, feature_width)
    output = jnp.dot(mixed, w_proj, preferred_element_type=jnp.float32)
    return output.reshape(level_count, row_count, column_count, feature_width)

def feed_forward(tokens, w_up, w_down):
    feature_width = tokens.shape[-1]
    normed = layer_norm(tokens.astype(jnp.float32)).astype(jnp.bfloat16).reshape(-1, feature_width)
    hidden = jax.nn.gelu(jnp.dot(normed, w_up, preferred_element_type=jnp.float32), approximate=False).astype(jnp.bfloat16)
    output = tokens.astype(jnp.float32).reshape(-1, feature_width) + jnp.dot(hidden, w_down, preferred_element_type=jnp.float32)
    return output.astype(jnp.bfloat16).reshape(tokens.shape)

def swin_block(tokens, w_qkv, w_proj, w_up, w_down, bias_table):
    level_count, row_count, column_count, feature_width = tokens.shape
    rolled = jnp.roll(tokens, (-1, -(WLAT // 2), -(WLON // 2)), axis=(0, 1, 2))
    full_bias = expand_bias(bias_table)
    pair_valid = window_valid(level_count, row_count, 0, row_count)

    def one_column(portion):
        attended = (portion.astype(jnp.float32) + attend(portion, w_qkv, w_proj, full_bias, pair_valid)).astype(jnp.bfloat16)
        return feed_forward(attended, w_up, w_down)
    stacked = rolled.reshape(level_count, row_count, column_count // WLON, WLON, feature_width).transpose(2, 0, 1, 3, 4)
    result = lax.map(one_column, stacked)
    result = result.transpose(1, 2, 0, 3, 4).reshape(level_count, row_count, column_count, feature_width)
    return jnp.roll(result, (1, WLAT // 2, WLON // 2), axis=(0, 1, 2))

def patch_merge(tokens, merge_matrix):
    level_count, row_count, column_count, feature_width = tokens.shape
    grouped = tokens.reshape(level_count, row_count // 2, 2, column_count // 2, 2, feature_width).transpose(0, 1, 3, 2, 4, 5)
    grouped = grouped.reshape(-1, 4 * feature_width)
    normed = layer_norm(grouped.astype(jnp.float32)).astype(jnp.bfloat16)
    merged = jnp.dot(normed, merge_matrix, preferred_element_type=jnp.float32).astype(jnp.bfloat16)
    return merged.reshape(level_count, row_count // 2, column_count // 2, merge_matrix.shape[1])

def reference(fields, fine_bias, fine_qkv, fine_proj, fine_up, fine_down, merge_weight, coarse_bias, coarse_qkv, coarse_proj, coarse_up, coarse_down):
    fine_field = swin_block(fields, fine_qkv, fine_proj, fine_up, fine_down, fine_bias)
    merged = patch_merge(fine_field, merge_weight)
    return swin_block(merged, coarse_qkv, coarse_proj, coarse_up, coarse_down, coarse_bias)
```

```python
import functools

import jax
import jax.numpy as jnp
from jax import lax
from jax.experimental import pallas as pl
from jax.experimental.pallas import tpu as pltpu
from jax.sharding import PartitionSpec as P

HD = 32
WZ = 2
WLAT = 6
WLON = 12
CELLS = WZ * WLAT * WLON
LINES = WZ * WLAT
SPAN = 2 * WLON - 1
EPSILON = 1e-05
MASKED = -1e30
VMEM_LIMIT = 40 * 1024 * 1024

f32 = jnp.float32
bf16 = jnp.bfloat16


def from_behind(shard, axis, by):
    peers = lax.axis_size(axis)
    return lax.ppermute(shard, axis, [(i, (i + by) % peers) for i in range(peers)])


def normalise(values):
    centred = values - jnp.mean(values, axis=-1, keepdims=True)
    variance = jnp.mean(centred * centred, axis=-1, keepdims=True)
    return (centred * lax.rsqrt(variance + EPSILON)).astype(bf16)


def dot(a, b):
    return jnp.dot(a, b, preferred_element_type=f32)


def dot_nt(a, b):
    return lax.dot_general(a, b, (((1,), (1,)), ((), ())), preferred_element_type=f32)


def gelu(x):
    return 0.5 * x * (1.0 + lax.erf(x * (2.0**-0.5)))


def feed_forward(x, up_ref, down_ref):
    hidden = gelu(dot(normalise(x), up_ref[...])).astype(bf16)
    return (x + dot(hidden, down_ref[...])).astype(bf16).astype(f32)


def three_parts(x):
    high = x.astype(bf16)
    rest = x - high.astype(f32)
    middle = rest.astype(bf16)
    low = (rest - middle.astype(f32)).astype(bf16)
    return high, middle, low


def iota(shape, axis):
    return lax.broadcasted_iota(jnp.int32, shape, axis)


def bias_kernel(last_ref, fine_ref, coarse_ref, fine_out, coarse_out, stacked, spread_from):
    stacked[...] = jnp.zeros_like(stacked)
    spread_from[...] = jnp.zeros_like(spread_from)
    row = iota((CELLS, CELLS), 0)
    key, query = row // LINES, row % LINES
    column = ((query // WLAT * WZ + key // WLAT) * WLAT + query % WLAT) * WLAT + key % WLAT
    pick = (iota((CELLS, CELLS), 1) == column).astype(f32).astype(bf16)
    row = iota((LINES * 32, 384), 0)
    lane = iota((LINES * 32, 384), 1)
    spread = (lane == (SPAN - 1 - row % 32) * LINES + row // 32) & (row % 32 < SPAN)
    spread = spread.astype(f32).astype(bf16)
    row, lane = iota((6 * LINES, 384), 0) % LINES, iota((6 * LINES, 384), 1) % LINES
    levels_differ = row // WLAT != lane // WLAT
    rows_differ = (row % WLAT >= WLAT // 2) != (lane % WLAT >= WLAT // 2)

    def expand(table_of, out_of, last):
        for head in range(6):
            stacked[head * 24 : head * 24 + SPAN, :] = table_of(head)
        picked = sum(dot_nt(pick, part) for part in three_parts(stacked[...]))
        for head in range(6):
            for key in range(LINES):
                spread_from[head * LINES : (head + 1) * LINES, key * 32 : key * 32 + 24] = picked[
                    key * LINES : (key + 1) * LINES, head * 24 : (head + 1) * 24
                ]
        flat = sum(dot(part, spread) for part in three_parts(spread_from[...]))
        if last is None:
            apart = levels_differ
        else:
            apart = levels_differ | (rows_differ & (last > 0))
        flat = jnp.where(apart, MASKED, flat)
        for o in range(WLON):
            start = (WLON - 1 - o) * LINES
            piece = flat[:, start : start + CELLS]
            for head in range(6):
                out_of(head, o * LINES, piece[head * LINES : (head + 1) * LINES])

    def put_fine(n):
        def put(head, at, piece):
            fine_out[n, head, at : at + LINES, :] = piece

        return put

    def put_coarse(base):
        def put(head, at, piece):
            coarse_out[base + head, at : at + LINES, :] = piece

        return put

    last = last_ref[0]
    expand(lambda head: fine_ref[0, 0, head], put_fine(0), None)
    expand(lambda head: fine_ref[1, 0, head], put_fine(1), last)
    expand(lambda head: coarse_ref[0, 0, head], put_coarse(0), last)
    expand(lambda head: coarse_ref[0, 0, 6 + head], put_coarse(6), last)


def attend_group(q, k, v, bias, heads):
    queries, width = q.shape
    of_head = iota((queries, width), 1) // HD
    big = jnp.concatenate([jnp.where(of_head == h, q, 0.0) for h in range(heads)], axis=0)
    scores = dot_nt(big.astype(bf16), k) * HD ** (-0.5) + bias.reshape(heads * queries, CELLS)
    top = jnp.max(scores, axis=-1, keepdims=True)
    weights = jnp.exp(scores - top)
    total = jnp.sum(weights, axis=-1, keepdims=True)
    mixed = dot(weights.astype(bf16), v) * (1.0 / total)
    out = jnp.zeros((queries, width), f32)
    for h in range(heads):
        out = jnp.where(of_head == h, mixed[h * queries : (h + 1) * queries], out)
    return out


def tiles_of(rows, width):
    return ((-(-width // 128), rows, 128), f32)


def put(ref, at, rows, stride, values):
    width = values.shape[-1]
    for t in range(ref.shape[0]):
        piece = values[:, t * 128 : min((t + 1) * 128, width)]
        if piece.shape[-1] < 128:
            piece = jnp.concatenate([piece, jnp.zeros((rows, 128 - piece.shape[-1]), f32)], axis=-1)
        ref[t, pl.ds(at, rows, stride=stride), :] = piece


def get(ref, at, rows, stride, width):
    pieces = [ref[t, pl.ds(at, rows, stride=stride), :] for t in range(ref.shape[0])]
    return jnp.concatenate(pieces, axis=-1)[:, :width]


def fine_attention_kernel(
    own_ref, below_ref, right_ref, bias_ref, qkv_ref, proj_ref, out_ref, send_ref, x_ref, a_ref, w_ref, s_ref
):
    for z in range(WZ):
        for rho in range(2 * WLAT):
            n, a = divmod(rho, WLAT)
            line = own_ref[1 - z, 3 + rho] if rho < 9 else below_ref[1 - z, rho - 9]
            put(x_ref, n * 576 + z * WLAT + a, 24, LINES, line.astype(f32))
            put(x_ref, n * 576 + 288 + z * WLAT + a, 24, LINES, right_ref[1 - z, rho].astype(f32))
    for n in range(2):
        normed = normalise(get(x_ref, n * 576 + 72, 432, 1, 192))
        q = dot(normed, qkv_ref[:, 0:192]).astype(bf16).astype(f32)
        k = dot(normed, qkv_ref[:, 192:384]).astype(bf16)
        v = dot(normed, qkv_ref[:, 384:576]).astype(bf16)
        left, right = [], []
        for window, start, stop in ((0, 72, 144), (1, 0, 144), (2, 0, 72)):
            at = window * CELLS
            q_rows = q[at + start : at + stop]
            k_rows, v_rows = k[at : at + CELLS], v[at : at + CELLS]
            bias = bias_ref[n, :, start:stop, :]
            left.append(attend_group(q_rows[:, :128], k_rows[:, :128], v_rows[:, :128], bias[:4], 4))
            right.append(attend_group(q_rows[:, 128:], k_rows[:, 128:], v_rows[:, 128:], bias[4:], 2))
        left = jnp.concatenate(left, axis=0).astype(bf16)
        right = jnp.concatenate(right, axis=0).astype(bf16)
        product = dot(left, proj_ref[0:128, :]) + dot(right, proj_ref[128:192, :])
        attended = (get(x_ref, n * 576 + 144, 288, 1, 192) + product).astype(bf16).astype(f32)
        put(a_ref, n * 288, 288, 1, attended)
    for t in range(2):
        for pb in range(2):
            for z in range(WZ):
                for rho in range(12):
                    n, a = divmod(rho, WLAT)
                    line = a_ref[t, pl.ds(n * 288 + pb * LINES + z * WLAT + a, 12, stride=24), :]
                    if rho < 3:
                        at = (z * 3 + rho) * 24 + pb * 12
                        s_ref[t, at : at + 12, :] = line
                        line = jnp.zeros((12, 128), f32)
                        rho += 12
                    w_ref[t, pl.ds(pb * 288 + z * 12 + rho - 3, 12, stride=24), :] = line
    out_ref[...] = get(w_ref, 0, 576, 1, 192).astype(bf16)
    send_ref[...] = get(s_ref, 0, 144, 1, 192).astype(bf16)


def fine_feed_forward_kernel(a_ref, up_ref, down_ref, out_ref):
    for i in range(4):
        rows = slice(i * 144, (i + 1) * 144)
        out_ref[rows, :] = feed_forward(a_ref[rows, :].astype(f32), up_ref, down_ref).astype(bf16)


def coarse_kernel(
    y_ref, got_ref, fine_up_ref, fine_down_ref, merge_ref, bias_ref, qkv_ref, proj_ref, up_ref, down_ref,
    keep_ref, send_ref, w_ref, r_ref, o_ref,
):
    put(r_ref, 0, 144, 1, feed_forward(got_ref[...].astype(f32), fine_up_ref, fine_down_ref))
    put(w_ref, 0, 576, 1, y_ref[...].astype(f32))
    for t in range(2):
        for pb in range(2):
            for z in range(WZ):
                for rho in range(3):
                    at = (z * 3 + rho) * 24 + pb * 12
                    w_ref[t, pl.ds(pb * 288 + z * 12 + 9 + rho, 12, stride=24), :] = r_ref[t, at : at + 12, :]
    parts = [get(w_ref, pb * 288 + pa, CELLS, 2, 192) for pa in range(2) for pb in range(2)]
    mean = sum(jnp.sum(part, axis=-1, keepdims=True) for part in parts) * (1.0 / 768)
    parts = [part - mean for part in parts]
    variance = sum(jnp.sum(part * part, axis=-1, keepdims=True) for part in parts) * (1.0 / 768)
    scale = lax.rsqrt(variance + EPSILON)
    merged = sum(
        dot((part * scale).astype(bf16), merge_ref[i * 192 : (i + 1) * 192, :]) for i, part in enumerate(parts)
    )
    merged = merged.astype(bf16).astype(f32)
    normed = normalise(merged)
    qkv = dot(normed, qkv_ref[...]).astype(bf16)
    product = merged
    for g in range(3):
        q = qkv[:, g * 128 : (g + 1) * 128].astype(f32)
        k = qkv[:, 384 + g * 128 : 384 + (g + 1) * 128]
        v = qkv[:, 768 + g * 128 : 768 + (g + 1) * 128]
        mixed = attend_group(q, k, v, bias_ref[g * 4 : (g + 1) * 4], 4)
        product = product + dot(mixed.astype(bf16), proj_ref[g * 128 : (g + 1) * 128, :])
    attended = product.astype(bf16).astype(f32)
    put(o_ref, 0, CELLS, 1, feed_forward(attended, up_ref, down_ref))
    for z in range(WZ):
        for i in range(3):
            keep_ref[1 - z, i] = get(o_ref, z * WLAT + i, WLON, LINES, 384).astype(bf16)
            send_ref[1 - z, i] = get(o_ref, z * WLAT + 3 + i, WLON, LINES, 384).astype(bf16)


def call(kernel, outs, scratch, operands, flops, smem=0):
    specs = [pl.BlockSpec(memory_space=pltpu.SMEM)] * smem
    specs += [pl.BlockSpec(memory_space=pltpu.VMEM)] * (len(operands) - smem)
    return pl.pallas_call(
        kernel,
        out_shape=[jax.ShapeDtypeStruct(shape, dtype) for shape, dtype in outs],
        in_specs=specs,
        out_specs=[pl.BlockSpec(memory_space=pltpu.VMEM)] * len(outs),
        scratch_shapes=[pltpu.VMEM(shape, dtype) for shape, dtype in scratch],
        compiler_params=pltpu.CompilerParams(vmem_limit_bytes=VMEM_LIMIT),
        cost_estimate=pl.CostEstimate(
            flops=flops,
            bytes_accessed=sum(a.size * a.dtype.itemsize for a in operands),
            transcendentals=0,
        ),
    )(*operands)


def body(
    fields,
    fine_bias,
    fine_qkv,
    fine_proj,
    fine_up,
    fine_down,
    merge_weight,
    coarse_bias,
    coarse_qkv,
    coarse_proj,
    coarse_up,
    coarse_down,
):
    last = (lax.axis_index("lat") == lax.axis_size("lat") - 1).astype(jnp.int32).reshape(1)
    below = from_behind(fields[:, :3], "lat", -1)
    right = from_behind(jnp.concatenate([fields[:, 3:], below], axis=1), "lon", -1)
    bias1, bias2 = call(
        bias_kernel,
        [((2, 6, CELLS, CELLS), f32), ((12, CELLS, CELLS), f32)],
        [((CELLS, CELLS), f32), ((6 * LINES, LINES * 32), f32)],
        [last, fine_bias, coarse_bias],
        3_000_000_000,
        smem=1,
    )
    attended, edge = call(
        fine_attention_kernel,
        [((576, 192), bf16), ((144, 192), bf16)],
        [tiles_of(1152, 192), tiles_of(576, 192), tiles_of(576, 192), tiles_of(144, 192)],
        [fields, below, right, bias1, fine_qkv, fine_proj],
        2_000_000_000,
    )
    got = from_behind(edge, "lat", -1)
    (finished,) = call(
        fine_feed_forward_kernel, [((576, 192), bf16)], [], [attended, fine_up, fine_down], 3_000_000_000
    )
    keep, send = call(
        coarse_kernel,
        [((2, 3, 12, 384), bf16), ((2, 3, 12, 384), bf16)],
        [tiles_of(576, 192), tiles_of(144, 192), tiles_of(CELLS, 384)],
        [finished, got, fine_up, fine_down, merge_weight, bias2, coarse_qkv, coarse_proj, coarse_up, coarse_down],
        4_000_000_000,
    )
    above = from_behind(send, "lat", 1)
    rows = jnp.concatenate([above, keep], axis=1)
    arrived = from_behind(rows[:, :, 6:], "lon", 1)
    return jnp.concatenate([arrived, rows[:, :, :6]], axis=2)


def solution(mesh):
    return jax.shard_map(
        body,
        mesh=mesh,
        in_specs=(
            P(None, "lat", "lon", None),
            P("lat", None, None, None, None),
            P(),
            P(),
            P(),
            P(),
            P(),
            P("lat", None, None, None, None),
            P(),
            P(),
            P(),
            P(),
        ),
        out_specs=P(None, "lat", "lon", None),
        check_vma=False,
    )
```

```python
import functools

import jax
import jax.numpy as jnp
from jax import lax
from jax.experimental import pallas as pl
from jax.experimental.pallas import tpu as pltpu
from jax.sharding import PartitionSpec as P

HD = 32
WZ = 2
WLAT = 6
WLON = 12
CELLS = WZ * WLAT * WLON
LINES = WZ * WLAT
SPAN = 2 * WLON - 1
EPSILON = 1e-05
MASKED = -1e30
VMEM_LIMIT = 40 * 1024 * 1024

f32 = jnp.float32
bf16 = jnp.bfloat16


def from_behind(shard, lon, lat):
    lons, lats = lax.axis_size("lon"), lax.axis_size("lat")
    pairs = [
        (o * lats + a, (o + lon) % lons * lats + (a + lat) % lats) for o in range(lons) for a in range(lats)
    ]
    return lax.ppermute(shard, ("lon", "lat"), pairs)


def normalise(values):
    centred = values - jnp.mean(values, axis=-1, keepdims=True)
    variance = jnp.mean(centred * centred, axis=-1, keepdims=True)
    return (centred * lax.rsqrt(variance + EPSILON)).astype(bf16)


def dot(a, b):
    return jnp.dot(a, b, preferred_element_type=f32)


def dot_nt(a, b):
    return lax.dot_general(a, b, (((1,), (1,)), ((), ())), preferred_element_type=f32)


def gelu(x):
    return 0.5 * x * (1.0 + lax.erf(x * (2.0**-0.5)))


def feed_forward(x, up_ref, down_ref):
    hidden = gelu(dot(normalise(x), up_ref[...])).astype(bf16)
    return (x + dot(hidden, down_ref[...])).astype(bf16).astype(f32)


def three_parts(x):
    high = x.astype(bf16)
    rest = x - high.astype(f32)
    middle = rest.astype(bf16)
    low = (rest - middle.astype(f32)).astype(bf16)
    return high, middle, low


def iota(shape, axis):
    return lax.broadcasted_iota(jnp.int32, shape, axis)


def bias_kernel(last_ref, fine_ref, coarse_ref, fine_out, coarse_out, stacked, spread_from):
    stacked[...] = jnp.zeros_like(stacked)
    spread_from[...] = jnp.zeros_like(spread_from)
    row = iota((CELLS, CELLS), 0)
    key, query = row // LINES, row % LINES
    column = ((query // WLAT * WZ + key // WLAT) * WLAT + query % WLAT) * WLAT + key % WLAT
    pick = (iota((CELLS, CELLS), 1) == column).astype(f32).astype(bf16)
    row = iota((LINES * 32, 384), 0)
    lane = iota((LINES * 32, 384), 1)
    spread = (lane == (SPAN - 1 - row % 32) * LINES + row // 32) & (row % 32 < SPAN)
    spread = spread.astype(f32).astype(bf16)
    row, lane = iota((6 * LINES, 384), 0) % LINES, iota((6 * LINES, 384), 1) % LINES
    levels_differ = row // WLAT != lane // WLAT
    rows_differ = (row % WLAT >= WLAT // 2) != (lane % WLAT >= WLAT // 2)

    def expand(table_of, out_of, last):
        for head in range(6):
            stacked[head * 24 : head * 24 + SPAN, :] = table_of(head)
        picked = sum(dot_nt(pick, part) for part in three_parts(stacked[...]))
        for head in range(6):
            for key in range(LINES):
                spread_from[head * LINES : (head + 1) * LINES, key * 32 : key * 32 + 24] = picked[
                    key * LINES : (key + 1) * LINES, head * 24 : (head + 1) * 24
                ]
        flat = sum(dot(part, spread) for part in three_parts(spread_from[...]))
        if last is None:
            apart = levels_differ
        else:
            apart = levels_differ | (rows_differ & (last > 0))
        flat = jnp.where(apart, MASKED, flat)
        for o in range(WLON):
            start = (WLON - 1 - o) * LINES
            piece = flat[:, start : start + CELLS]
            for head in range(6):
                out_of(head, o * LINES, piece[head * LINES : (head + 1) * LINES])

    def put_fine(n):
        def put(head, at, piece):
            fine_out[n, head, at : at + LINES, :] = piece

        return put

    def put_coarse(base):
        def put(head, at, piece):
            coarse_out[base + head, at : at + LINES, :] = piece

        return put

    last = last_ref[0]
    expand(lambda head: fine_ref[0, 0, head], put_fine(0), None)
    expand(lambda head: fine_ref[1, 0, head], put_fine(1), last)
    expand(lambda head: coarse_ref[0, 0, head], put_coarse(0), last)
    expand(lambda head: coarse_ref[0, 0, 6 + head], put_coarse(6), last)


def attend_group(q, k, v, bias, heads):
    queries, width = q.shape
    of_head = iota((queries, width), 1) // HD
    big = jnp.concatenate([jnp.where(of_head == h, q, 0.0) for h in range(heads)], axis=0)
    scores = dot_nt(big.astype(bf16), k) * HD ** (-0.5) + bias.reshape(heads * queries, CELLS)
    top = jnp.max(scores, axis=-1, keepdims=True)
    weights = jnp.exp(scores - top)
    total = jnp.sum(weights, axis=-1, keepdims=True)
    mixed = dot(weights.astype(bf16), v) * (1.0 / total)
    out = jnp.zeros((queries, width), f32)
    for h in range(heads):
        out = jnp.where(of_head == h, mixed[h * queries : (h + 1) * queries], out)
    return out


def tiles_of(rows, width):
    return ((-(-width // 128), rows, 128), f32)


def put(ref, at, rows, stride, values):
    width = values.shape[-1]
    for t in range(ref.shape[0]):
        piece = values[:, t * 128 : min((t + 1) * 128, width)]
        if piece.shape[-1] < 128:
            piece = jnp.concatenate([piece, jnp.zeros((rows, 128 - piece.shape[-1]), f32)], axis=-1)
        ref[t, pl.ds(at, rows, stride=stride), :] = piece


def get(ref, at, rows, stride, width):
    pieces = [ref[t, pl.ds(at, rows, stride=stride), :] for t in range(ref.shape[0])]
    return jnp.concatenate(pieces, axis=-1)[:, :width]


def attend_fine(n, x_ref, bias_ref, qkv_ref, proj_ref):
    normed = normalise(get(x_ref, 72, 432, 1, 192))
    q = dot(normed, qkv_ref[:, 0:192]).astype(bf16).astype(f32)
    k = dot(normed, qkv_ref[:, 192:384]).astype(bf16)
    v = dot(normed, qkv_ref[:, 384:576]).astype(bf16)
    left, right = [], []
    for window, start, stop in ((0, 72, 144), (1, 0, 144), (2, 0, 72)):
        at = window * CELLS
        q_rows = q[at + start : at + stop]
        k_rows, v_rows = k[at : at + CELLS], v[at : at + CELLS]
        bias = bias_ref[n, :, start:stop, :]
        left.append(attend_group(q_rows[:, :128], k_rows[:, :128], v_rows[:, :128], bias[:4], 4))
        right.append(attend_group(q_rows[:, 128:], k_rows[:, 128:], v_rows[:, 128:], bias[4:], 2))
    left = jnp.concatenate(left, axis=0).astype(bf16)
    right = jnp.concatenate(right, axis=0).astype(bf16)
    product = dot(left, proj_ref[0:128, :]) + dot(right, proj_ref[128:192, :])
    return (get(x_ref, 144, 288, 1, 192) + product).astype(bf16)


def first_rows_kernel(own_ref, right_ref, bias_ref, qkv_ref, proj_ref, out_ref, send_ref, x_ref, a_ref, s_ref):
    for z in range(WZ):
        for a in range(WLAT):
            put(x_ref, z * WLAT + a, 24, LINES, own_ref[1 - z, 3 + a].astype(f32))
            put(x_ref, 288 + z * WLAT + a, 24, LINES, right_ref[1 - z, 3 + a].astype(f32))
    attended = attend_fine(0, x_ref, bias_ref, qkv_ref, proj_ref)
    out_ref[...] = attended
    put(a_ref, 0, 288, 1, attended.astype(f32))
    for t in range(2):
        for pb in range(2):
            for z in range(WZ):
                for a in range(3):
                    at = (z * 3 + a) * 24 + pb * 12
                    line = a_ref[t, pl.ds(pb * LINES + z * WLAT + a, 12, stride=24), :]
                    s_ref[t, at : at + 12, :] = line
    send_ref[...] = get(s_ref, 0, 144, 1, 192).astype(bf16)


def second_rows_kernel(
    own_ref, right_ref, below_ref, corner_ref, first_ref, bias_ref, qkv_ref, proj_ref, up_ref, down_ref,
    out_ref, x_ref, a_ref, w_ref,
):
    for z in range(WZ):
        for a in range(WLAT):
            near = own_ref[1 - z, 9 + a] if a < 3 else below_ref[1 - z, a - 3]
            far = right_ref[1 - z, 9 + a] if a < 3 else corner_ref[1 - z, a - 3]
            put(x_ref, z * WLAT + a, 24, LINES, near.astype(f32))
            put(x_ref, 288 + z * WLAT + a, 24, LINES, far.astype(f32))
    put(a_ref, 0, 288, 1, first_ref[...].astype(f32))
    put(a_ref, 288, 288, 1, attend_fine(1, x_ref, bias_ref, qkv_ref, proj_ref).astype(f32))
    for t in range(2):
        for pb in range(2):
            for z in range(WZ):
                for rho in range(3, 15):
                    n, a = divmod(rho, WLAT)
                    if rho < 12:
                        line = a_ref[t, pl.ds(n * 288 + pb * LINES + z * WLAT + a, 12, stride=24), :]
                    else:
                        line = jnp.zeros((12, 128), f32)
                    w_ref[t, pl.ds(pb * 288 + z * 12 + rho - 3, 12, stride=24), :] = line
    for i in range(4):
        x = get(w_ref, i * 144, 144, 1, 192)
        out_ref[i * 144 : (i + 1) * 144, :] = feed_forward(x, up_ref, down_ref).astype(bf16)


def coarse_kernel(
    y_ref, got_ref, fine_up_ref, fine_down_ref, merge_ref, bias_ref, qkv_ref, proj_ref, up_ref, down_ref,
    keep_ref, down_row_ref, right_column_ref, corner_ref, w_ref, r_ref, o_ref,
):
    put(r_ref, 0, 144, 1, feed_forward(got_ref[...].astype(f32), fine_up_ref, fine_down_ref))
    put(w_ref, 0, 576, 1, y_ref[...].astype(f32))
    for t in range(2):
        for pb in range(2):
            for z in range(WZ):
                for rho in range(3):
                    at = (z * 3 + rho) * 24 + pb * 12
                    w_ref[t, pl.ds(pb * 288 + z * 12 + 9 + rho, 12, stride=24), :] = r_ref[t, at : at + 12, :]
    parts = [get(w_ref, pb * 288 + pa, CELLS, 2, 192) for pa in range(2) for pb in range(2)]
    mean = sum(jnp.sum(part, axis=-1, keepdims=True) for part in parts) * (1.0 / 768)
    parts = [part - mean for part in parts]
    variance = sum(jnp.sum(part * part, axis=-1, keepdims=True) for part in parts) * (1.0 / 768)
    scale = lax.rsqrt(variance + EPSILON)
    merged = sum(
        dot((part * scale).astype(bf16), merge_ref[i * 192 : (i + 1) * 192, :]) for i, part in enumerate(parts)
    )
    merged = merged.astype(bf16).astype(f32)
    normed = normalise(merged)
    qkv = dot(normed, qkv_ref[...]).astype(bf16)
    product = merged
    for g in range(3):
        q = qkv[:, g * 128 : (g + 1) * 128].astype(f32)
        k = qkv[:, 384 + g * 128 : 384 + (g + 1) * 128]
        v = qkv[:, 768 + g * 128 : 768 + (g + 1) * 128]
        mixed = attend_group(q, k, v, bias_ref[g * 4 : (g + 1) * 4], 4)
        product = product + dot(mixed.astype(bf16), proj_ref[g * 128 : (g + 1) * 128, :])
    attended = product.astype(bf16).astype(f32)
    put(o_ref, 0, CELLS, 1, feed_forward(attended, up_ref, down_ref))
    for z in range(WZ):
        for i in range(3):
            upper = get(o_ref, z * WLAT + i, WLON, LINES, 384)
            lower = get(o_ref, z * WLAT + 3 + i, WLON, LINES, 384)
            keep_ref[1 - z, i] = upper[:6].astype(bf16)
            right_column_ref[1 - z, i] = upper[6:].astype(bf16)
            down_row_ref[1 - z, i] = lower[:6].astype(bf16)
            corner_ref[1 - z, i] = lower[6:].astype(bf16)


def assemble_kernel(keep_ref, above_ref, left_ref, corner_ref, out_ref):
    for z in range(WZ):
        for i in range(3):
            upper = [corner_ref[z, i].astype(f32), above_ref[z, i].astype(f32)]
            lower = [left_ref[z, i].astype(f32), keep_ref[z, i].astype(f32)]
            out_ref[z, i] = jnp.concatenate(upper, axis=0).astype(bf16)
            out_ref[z, 3 + i] = jnp.concatenate(lower, axis=0).astype(bf16)


def call(kernel, outs, scratch, operands, flops, smem=0):
    specs = [pl.BlockSpec(memory_space=pltpu.SMEM)] * smem
    specs += [pl.BlockSpec(memory_space=pltpu.VMEM)] * (len(operands) - smem)
    return pl.pallas_call(
        kernel,
        out_shape=[jax.ShapeDtypeStruct(shape, dtype) for shape, dtype in outs],
        in_specs=specs,
        out_specs=[pl.BlockSpec(memory_space=pltpu.VMEM)] * len(outs),
        scratch_shapes=[pltpu.VMEM(shape, dtype) for shape, dtype in scratch],
        compiler_params=pltpu.CompilerParams(vmem_limit_bytes=VMEM_LIMIT),
        cost_estimate=pl.CostEstimate(
            flops=flops,
            bytes_accessed=sum(a.size * a.dtype.itemsize for a in operands),
            transcendentals=0,
        ),
    )(*operands)


def body(
    fields,
    fine_bias,
    fine_qkv,
    fine_proj,
    fine_up,
    fine_down,
    merge_weight,
    coarse_bias,
    coarse_qkv,
    coarse_proj,
    coarse_up,
    coarse_down,
):
    last = (lax.axis_index("lat") == lax.axis_size("lat") - 1).astype(jnp.int32).reshape(1)
    right = from_behind(fields, -1, 0)
    top = fields[:, :3]
    below = from_behind(top, 0, -1)
    corner = from_behind(top, -1, -1)
    bias1, bias2 = call(
        bias_kernel,
        [((2, 6, CELLS, CELLS), f32), ((12, CELLS, CELLS), f32)],
        [((CELLS, CELLS), f32), ((6 * LINES, LINES * 32), f32)],
        [last, fine_bias, coarse_bias],
        3_000_000_000,
        smem=1,
    )
    first, edge = call(
        first_rows_kernel,
        [((288, 192), bf16), ((144, 192), bf16)],
        [tiles_of(576, 192), tiles_of(288, 192), tiles_of(144, 192)],
        [fields, right, bias1, fine_qkv, fine_proj],
        1_000_000_000,
    )
    got = from_behind(edge, 0, -1)
    (finished,) = call(
        second_rows_kernel,
        [((576, 192), bf16)],
        [tiles_of(576, 192), tiles_of(576, 192), tiles_of(576, 192)],
        [fields, right, below, corner, first, bias1, fine_qkv, fine_proj, fine_up, fine_down],
        3_000_000_000,
    )
    quarter = ((2, 3, 6, 384), bf16)
    keep, down_row, right_column, far_corner = call(
        coarse_kernel,
        [quarter] * 4,
        [tiles_of(576, 192), tiles_of(144, 192), tiles_of(CELLS, 384)],
        [finished, got, fine_up, fine_down, merge_weight, bias2, coarse_qkv, coarse_proj, coarse_up, coarse_down],
        4_000_000_000,
    )
    above = from_behind(down_row, 0, 1)
    corner = from_behind(far_corner, 1, 1)
    left = from_behind(right_column, 1, 0)
    return pl.pallas_call(
        assemble_kernel,
        out_shape=jax.ShapeDtypeStruct((2, 6, 12, 384), bf16),
        grid=(1,),
        in_specs=[pl.BlockSpec((2, 3, 6, 384), lambda i: (0, 0, 0, 0))] * 4,
        out_specs=pl.BlockSpec((2, 6, 12, 384), lambda i: (0, 0, 0, 0)),
    )(keep, above, left, corner)


def solution(mesh):
    return jax.shard_map(
        body,
        mesh=mesh,
        in_specs=(
            P(None, "lat", "lon", None),
            P("lat", None, None, None, None),
            P(),
            P(),
            P(),
            P(),
            P(),
            P("lat", None, None, None, None),
            P(),
            P(),
            P(),
            P(),
        ),
        out_specs=P(None, "lat", "lon", None),
        check_vma=False,
    )
```

```python
import functools

import jax
import jax.numpy as jnp
from jax import lax
from jax.experimental import pallas as pl
from jax.experimental.pallas import tpu as pltpu
from jax.sharding import PartitionSpec as P

HD = 32
WZ = 2
WLAT = 6
WLON = 12
CELLS = WZ * WLAT * WLON
LINES = WZ * WLAT
SPAN = 2 * WLON - 1
EPSILON = 1e-05
MASKED = -1e30
VMEM_LIMIT = 40 * 1024 * 1024

f32 = jnp.float32
bf16 = jnp.bfloat16


def from_behind(shard, lon, lat):
    lons, lats = lax.axis_size("lon"), lax.axis_size("lat")
    pairs = [
        (o * lats + a, (o + lon) % lons * lats + (a + lat) % lats) for o in range(lons) for a in range(lats)
    ]
    return lax.ppermute(shard, ("lon", "lat"), pairs)


def normalise(values):
    centred = values - jnp.mean(values, axis=-1, keepdims=True)
    variance = jnp.mean(centred * centred, axis=-1, keepdims=True)
    return (centred * lax.rsqrt(variance + EPSILON)).astype(bf16)


def dot(a, b):
    return jnp.dot(a, b, preferred_element_type=f32)


def dot_nt(a, b):
    return lax.dot_general(a, b, (((1,), (1,)), ((), ())), preferred_element_type=f32)


def gelu(x):
    return 0.5 * x * (1.0 + lax.erf(x * (2.0**-0.5)))


def feed_forward(x, up_ref, down_ref):
    hidden = gelu(dot(normalise(x), up_ref[...])).astype(bf16)
    return (x + dot(hidden, down_ref[...])).astype(bf16).astype(f32)


def fine_feed_forward(x, up_ref, down_ref):
    hidden = gelu(dot(normalise(x), up_ref[...])).astype(bf16)
    return (x + dot_nt(hidden, down_ref[...])).astype(bf16).astype(f32)


def three_parts(x):
    high = x.astype(bf16)
    rest = x - high.astype(f32)
    middle = rest.astype(bf16)
    low = (rest - middle.astype(f32)).astype(bf16)
    return high, middle, low


def iota(shape, axis):
    return lax.broadcasted_iota(jnp.int32, shape, axis)


def expand_bias(tables, outs, stacked, spread_from):
    stacked[...] = jnp.zeros_like(stacked)
    spread_from[...] = jnp.zeros_like(spread_from)
    row = iota((CELLS, CELLS), 0)
    key, query = row // LINES, row % LINES
    column = ((query // WLAT * WZ + key // WLAT) * WLAT + query % WLAT) * WLAT + key % WLAT
    pick = (iota((CELLS, CELLS), 1) == column).astype(f32).astype(bf16)
    row = iota((LINES * 32, 384), 0)
    lane = iota((LINES * 32, 384), 1)
    spread = (lane == (SPAN - 1 - row % 32) * LINES + row // 32) & (row % 32 < SPAN)
    spread = spread.astype(f32).astype(bf16)
    row, lane = iota((6 * LINES, 384), 0) % LINES, iota((6 * LINES, 384), 1) % LINES
    levels_differ = row // WLAT != lane // WLAT
    rows_differ = (row % WLAT >= WLAT // 2) != (lane % WLAT >= WLAT // 2)
    for (table_of, last), out_of in zip(tables, outs, strict=True):
        for head in range(6):
            stacked[head * 24 : head * 24 + SPAN, :] = table_of(head)
        picked = sum(dot_nt(pick, part) for part in three_parts(stacked[...]))
        for head in range(6):
            for key in range(LINES):
                spread_from[head * LINES : (head + 1) * LINES, key * 32 : key * 32 + 24] = picked[
                    key * LINES : (key + 1) * LINES, head * 24 : (head + 1) * 24
                ]
        flat = sum(dot(part, spread) for part in three_parts(spread_from[...]))
        apart = levels_differ if last is None else levels_differ | (rows_differ & (last > 0))
        flat = jnp.where(apart, MASKED, flat)
        for o in range(WLON):
            start = (WLON - 1 - o) * LINES
            piece = flat[:, start : start + CELLS]
            for head in range(6):
                out_of(head, o * LINES, piece[head * LINES : (head + 1) * LINES])


def writer(out_ref, base):
    def write(head, at, piece):
        out_ref[base + head, at : at + LINES, :] = piece

    return write


def reader(table_ref, row, base):
    return lambda head: table_ref[row, base + head, :, 0, :]


def first_bias_kernel(fine_ref, out_ref, stacked, spread_from):
    expand_bias([(reader(fine_ref, 0, 0), None)], [writer(out_ref, 0)], stacked, spread_from)


def other_bias_kernel(last_ref, fine_ref, coarse_ref, after_ref, fine_out, coarse_out, stacked, spread_from):
    last = last_ref[0]
    tables = [(reader(fine_ref, 1, 0), last), (reader(coarse_ref, 0, 0), last), (reader(coarse_ref, 0, 6), last)]
    expand_bias(tables, [writer(fine_out, 0), writer(coarse_out, 0), writer(coarse_out, 6)], stacked, spread_from)


def attend_group(q, k, v, bias, heads):
    queries, width = q.shape
    of_head = iota((queries, width), 1) // HD
    big = jnp.concatenate([jnp.where(of_head == h, q, 0.0) for h in range(heads)], axis=0)
    scores = dot_nt(big.astype(bf16), k) * HD ** (-0.5) + bias.reshape(heads * queries, CELLS)
    top = jnp.max(scores, axis=-1, keepdims=True)
    weights = jnp.exp(scores - top)
    total = jnp.sum(weights, axis=-1, keepdims=True)
    mixed = dot(weights.astype(bf16), v) * (1.0 / total)
    out = jnp.zeros((queries, width), f32)
    for h in range(heads):
        out = jnp.where(of_head == h, mixed[h * queries : (h + 1) * queries], out)
    return out


def tiles_of(rows, width):
    return ((-(-width // 128), rows, 128), f32)


def put(ref, at, rows, stride, values):
    width = values.shape[-1]
    for t in range(ref.shape[0]):
        piece = values[:, t * 128 : min((t + 1) * 128, width)]
        if piece.shape[-1] < 128:
            piece = jnp.concatenate([piece, jnp.zeros((rows, 128 - piece.shape[-1]), f32)], axis=-1)
        ref[t, pl.ds(at, rows, stride=stride), :] = piece


def get(ref, at, rows, stride, width):
    pieces = [ref[t, pl.ds(at, rows, stride=stride), :] for t in range(ref.shape[0])]
    return jnp.concatenate(pieces, axis=-1)[:, :width]


def pack_lines(first, second):
    return jnp.concatenate(first + [jnp.concatenate([second[i], second[3 + i]], axis=-1) for i in range(3)], axis=0)


def unpack_line(packed, i, size):
    first = packed[i * size : (i + 1) * size]
    at = (6 + i % 3) * size
    second = packed[at : at + size, i // 3 * 64 : i // 3 * 64 + 64]
    return jnp.concatenate([first, second], axis=-1)


def pack_top_kernel(top_ref, below_ref, corner_ref, line_ref):
    lines = [top_ref[z, a].astype(f32) for z in range(WZ) for a in range(3)]
    packed = pack_lines([line[:, :128] for line in lines], [line[:, 128:] for line in lines])
    below_ref[...] = packed.astype(bf16)
    for i in range(9):
        line_ref[i * 18 : (i + 1) * 18, :] = packed[i * 24 + 6 : (i + 1) * 24]
    corner_ref[...] = line_ref[...].astype(bf16)


def attend_fine(x_ref, bias_ref, qkv_ref, proj_ref):
    normed = normalise(get(x_ref, 72, 432, 1, 192))
    q = dot(normed, qkv_ref[:, 0:192]).astype(bf16).astype(f32)
    k = dot(normed, qkv_ref[:, 192:384]).astype(bf16)
    v = dot(normed, qkv_ref[:, 384:576]).astype(bf16)
    left, right = [], []
    for window, start, stop in ((0, 72, 144), (1, 0, 144), (2, 0, 72)):
        at = window * CELLS
        q_rows = q[at + start : at + stop]
        k_rows, v_rows = k[at : at + CELLS], v[at : at + CELLS]
        bias = bias_ref[:, start:stop, :]
        left.append(attend_group(q_rows[:, :128], k_rows[:, :128], v_rows[:, :128], bias[:4], 4))
        right.append(attend_group(q_rows[:, 128:], k_rows[:, 128:], v_rows[:, 128:], bias[4:], 2))
    left = jnp.concatenate(left, axis=0).astype(bf16)
    right = jnp.concatenate(right, axis=0).astype(bf16)
    product = dot(left, proj_ref[0:128, :]) + dot(right, proj_ref[128:192, :])
    return (get(x_ref, 144, 288, 1, 192) + product).astype(bf16)


def first_rows_kernel(left_ref, own_ref, bias_ref, qkv_ref, proj_ref, out_ref, send_ref, x_ref, a_ref):
    for z in range(WZ):
        for a in range(WLAT):
            put(x_ref, z * WLAT + a, 24, LINES, left_ref[1 - z, 3 + a].astype(f32))
            put(x_ref, 288 + z * WLAT + a, 24, LINES, own_ref[1 - z, 3 + a].astype(f32))
    attended = attend_fine(x_ref, bias_ref, qkv_ref, proj_ref)
    out_ref[...] = attended
    put(a_ref, 0, 288, 1, attended.astype(f32))
    lines = [
        jnp.concatenate([a_ref[t, pl.ds(pb * LINES + z * WLAT + a, 12, stride=24), :] for pb in range(2)], axis=0)
        for t in range(2)
        for z in range(WZ)
        for a in range(3)
    ]
    send_ref[...] = pack_lines(lines[:6], [line[:, :64] for line in lines[6:]]).astype(bf16)


def second_rows_kernel(
    left_ref, own_ref, corner_ref, below_ref, first_ref, bias_ref, qkv_ref, proj_ref, up_ref, down_ref,
    out_ref, x_ref, a_ref, w_ref,
):
    below, corner = below_ref[...].astype(f32), corner_ref[...].astype(f32)
    for z in range(WZ):
        for a in range(WLAT):
            at = z * WLAT + a
            if a < 3:
                put(x_ref, at, 24, LINES, left_ref[1 - z, 9 + a].astype(f32))
                put(x_ref, 288 + at, 24, LINES, own_ref[1 - z, 9 + a].astype(f32))
            else:
                line = (1 - z) * 3 + a - 3
                put(x_ref, 72 + at, 18, LINES, unpack_line(corner, line, 18))
                put(x_ref, 288 + at, 24, LINES, unpack_line(below, line, 24))
    put(a_ref, 0, 288, 1, first_ref[...].astype(f32))
    put(a_ref, 288, 288, 1, attend_fine(x_ref, bias_ref, qkv_ref, proj_ref).astype(f32))
    for t in range(2):
        for pb in range(2):
            for z in range(WZ):
                for rho in range(3, 15):
                    n, a = divmod(rho, WLAT)
                    if rho < 12:
                        line = a_ref[t, pl.ds(n * 288 + pb * LINES + z * WLAT + a, 12, stride=24), :]
                    else:
                        line = jnp.zeros((12, 128), f32)
                    w_ref[t, pl.ds(pb * 288 + z * 12 + rho - 3, 12, stride=24), :] = line
    for i in range(4):
        x = get(w_ref, i * 144, 144, 1, 192)
        out_ref[i * 144 : (i + 1) * 144, :] = fine_feed_forward(x, up_ref, down_ref).astype(bf16)


def coarse_kernel(
    y_ref, got_ref, fine_up_ref, fine_down_ref, merge_ref, bias_ref, qkv_ref, proj_ref, up_ref, down_ref,
    keep_ref, lower_ref, corner_ref, left_ref, w_ref, r_ref, o_ref,
):
    got = got_ref[...].astype(f32)
    got = jnp.concatenate([unpack_line(got, i, 24) for i in range(6)], axis=0)
    put(r_ref, 0, 144, 1, fine_feed_forward(got, fine_up_ref, fine_down_ref))
    put(w_ref, 0, 576, 1, y_ref[...].astype(f32))
    for t in range(2):
        for pb in range(2):
            for z in range(WZ):
                for rho in range(3):
                    at = (z * 3 + rho) * 24 + pb * 12
                    w_ref[t, pl.ds(pb * 288 + z * 12 + 9 + rho, 12, stride=24), :] = r_ref[t, at : at + 12, :]
    parts = [get(w_ref, pb * 288 + pa, CELLS, 2, 192) for pa in range(2) for pb in range(2)]
    mean = sum(jnp.sum(part, axis=-1, keepdims=True) for part in parts) * (1.0 / 768)
    parts = [part - mean for part in parts]
    variance = sum(jnp.sum(part * part, axis=-1, keepdims=True) for part in parts) * (1.0 / 768)
    scale = lax.rsqrt(variance + EPSILON)
    merged = sum(
        dot((part * scale).astype(bf16), merge_ref[i * 192 : (i + 1) * 192, :]) for i, part in enumerate(parts)
    )
    merged = merged.astype(bf16).astype(f32)
    normed = normalise(merged)
    qkv = dot(normed, qkv_ref[...]).astype(bf16)
    product = merged
    for g in range(3):
        q = qkv[:, g * 128 : (g + 1) * 128].astype(f32)
        k = qkv[:, 384 + g * 128 : 384 + (g + 1) * 128]
        v = qkv[:, 768 + g * 128 : 768 + (g + 1) * 128]
        mixed = attend_group(q, k, v, bias_ref[g * 4 : (g + 1) * 4], 4)
        product = product + dot(mixed.astype(bf16), proj_ref[g * 128 : (g + 1) * 128, :])
    attended = product.astype(bf16).astype(f32)
    put(o_ref, 0, CELLS, 1, feed_forward(attended, up_ref, down_ref))
    for z in range(WZ):
        for i in range(3):
            upper = get(o_ref, z * WLAT + i, WLON, LINES, 384)
            lower = get(o_ref, z * WLAT + 3 + i, WLON, LINES, 384)
            keep_ref[1 - z, i] = upper[6:].astype(bf16)
            left_ref[1 - z, i] = upper[:6].astype(bf16)
            lower_ref[1 - z, i] = lower[6:].astype(bf16)
            corner_ref[1 - z, i] = lower[:6].astype(bf16)


def call(kernel, outs, scratch, operands, flops, smem=0):
    specs = [pl.BlockSpec(memory_space=pltpu.SMEM)] * smem
    specs += [pl.BlockSpec(memory_space=pltpu.VMEM)] * (len(operands) - smem)
    return pl.pallas_call(
        kernel,
        out_shape=[jax.ShapeDtypeStruct(shape, dtype) for shape, dtype in outs],
        in_specs=specs,
        out_specs=[pl.BlockSpec(memory_space=pltpu.VMEM)] * len(outs),
        scratch_shapes=[pltpu.VMEM(shape, dtype) for shape, dtype in scratch],
        compiler_params=pltpu.CompilerParams(vmem_limit_bytes=VMEM_LIMIT),
        cost_estimate=pl.CostEstimate(
            flops=flops,
            bytes_accessed=sum(a.size * a.dtype.itemsize for a in operands),
            transcendentals=0,
        ),
    )(*operands)


def body(
    fields,
    fine_bias,
    fine_qkv,
    fine_proj,
    fine_up,
    fine_down,
    merge_weight,
    coarse_bias,
    coarse_qkv,
    coarse_proj,
    coarse_up,
    coarse_down,
):
    last = (lax.axis_index("lat") == lax.axis_size("lat") - 1).astype(jnp.int32).reshape(1)
    fine_tables = fine_bias.transpose(0, 2, 3, 1, 4)
    coarse_tables = coarse_bias.transpose(0, 2, 3, 1, 4)
    fine_down = fine_down.T
    expansion = [((CELLS, CELLS), f32), ((6 * LINES, LINES * 32), f32)]
    left = from_behind(fields, 1, 0)
    below, corner = pl.pallas_call(
        pack_top_kernel,
        out_shape=[jax.ShapeDtypeStruct((216, 128), bf16), jax.ShapeDtypeStruct((162, 128), bf16)],
        grid=(1,),
        in_specs=[pl.BlockSpec((2, 3, 24, 192), lambda i: (0, 0, 0, 0))],
        out_specs=[pl.BlockSpec(memory_space=pltpu.VMEM)] * 2,
        scratch_shapes=[pltpu.VMEM((162, 128), f32)],
    )(fields)
    below = from_behind(below, 0, -1)
    corner = from_behind(corner, 1, -1)
    (bias0,) = call(first_bias_kernel, [((6, CELLS, CELLS), f32)], expansion, [fine_tables], 1_000_000_000)
    first, edge = call(
        first_rows_kernel,
        [((288, 192), bf16), ((216, 128), bf16)],
        [tiles_of(576, 192), tiles_of(288, 192)],
        [left, fields, bias0, fine_qkv, fine_proj],
        1_000_000_000,
    )
    got = from_behind(edge, 0, -1)
    bias1, bias2 = call(
        other_bias_kernel,
        [((6, CELLS, CELLS), f32), ((12, CELLS, CELLS), f32)],
        expansion,
        [last, fine_tables, coarse_tables, first],
        3_000_000_000,
        smem=1,
    )
    (finished,) = call(
        second_rows_kernel,
        [((576, 192), bf16)],
        [tiles_of(576, 192), tiles_of(576, 192), tiles_of(576, 192)],
        [left, fields, corner, below, first, bias1, fine_qkv, fine_proj, fine_up, fine_down],
        3_000_000_000,
    )
    quarter = ((2, 3, 6, 384), bf16)
    keep, lower, far_corner, upper_left = call(
        coarse_kernel,
        [quarter] * 4,
        [tiles_of(576, 192), tiles_of(144, 192), tiles_of(CELLS, 384)],
        [finished, got, fine_up, fine_down, merge_weight, bias2, coarse_qkv, coarse_proj, coarse_up, coarse_down],
        4_000_000_000,
    )
    above = from_behind(lower, 0, 1)
    corner = from_behind(far_corner, -1, 1)
    right = from_behind(upper_left, -1, 0)
    rows = [jnp.concatenate([above, corner], axis=2), jnp.concatenate([keep, right], axis=2)]
    return jnp.concatenate(rows, axis=1)


def solution(mesh):
    return jax.shard_map(
        body,
        mesh=mesh,
        in_specs=(
            P(None, "lat", "lon", None),
            P("lat", None, None, None, None),
            P(),
            P(),
            P(),
            P(),
            P(),
            P("lat", None, None, None, None),
            P(),
            P(),
            P(),
            P(),
        ),
        out_specs=P(None, "lat", "lon", None),
        check_vma=False,
    )
```

```python
import functools

import jax
import jax.numpy as jnp
from jax import lax
from jax.experimental import pallas as pl
from jax.experimental.pallas import tpu as pltpu
from jax.sharding import PartitionSpec as P

HD = 32
WZ = 2
WLAT = 6
WLON = 12
CELLS = WZ * WLAT * WLON
LINES = WZ * WLAT
SPAN = 2 * WLON - 1
EPSILON = 1e-05
MASKED = -1e30
VMEM_LIMIT = 40 * 1024 * 1024

f32 = jnp.float32
bf16 = jnp.bfloat16


def from_behind(shard, lon, lat):
    lons, lats = lax.axis_size("lon"), lax.axis_size("lat")
    pairs = [
        (o * lats + a, (o + lon) % lons * lats + (a + lat) % lats) for o in range(lons) for a in range(lats)
    ]
    return lax.ppermute(shard, ("lon", "lat"), pairs)


def normalise(values):
    centred = values - jnp.mean(values, axis=-1, keepdims=True)
    variance = jnp.mean(centred * centred, axis=-1, keepdims=True)
    return (centred * lax.rsqrt(variance + EPSILON)).astype(bf16)


def dot(a, b):
    return jnp.dot(a, b, preferred_element_type=f32)


def dot_nt(a, b):
    return lax.dot_general(a, b, (((1,), (1,)), ((), ())), preferred_element_type=f32)


def gelu(x):
    return 0.5 * x * (1.0 + lax.erf(x * (2.0**-0.5)))


def feed_forward(x, up_ref, down_ref):
    hidden = gelu(dot(normalise(x), up_ref[...])).astype(bf16)
    return (x + dot(hidden, down_ref[...])).astype(bf16).astype(f32)


def fine_feed_forward(x, up_ref, down_ref):
    hidden = gelu(dot(normalise(x), up_ref[...])).astype(bf16)
    return (x + dot_nt(hidden, down_ref[...])).astype(bf16).astype(f32)


def three_parts(x):
    high = x.astype(bf16)
    rest = x - high.astype(f32)
    middle = rest.astype(bf16)
    low = (rest - middle.astype(f32)).astype(bf16)
    return high, middle, low


def iota(shape, axis):
    return lax.broadcasted_iota(jnp.int32, shape, axis)


def expand_bias(tables, outs, stacked, spread_from):
    stacked[...] = jnp.zeros_like(stacked)
    spread_from[...] = jnp.zeros_like(spread_from)
    row = iota((CELLS, CELLS), 0)
    key, query = row // LINES, row % LINES
    z_key, z_query = 1 - key // WLAT, 1 - query // WLAT
    column = ((z_query * WZ + z_key) * WLAT + query % WLAT) * WLAT + key % WLAT
    pick = (iota((CELLS, CELLS), 1) == column).astype(f32).astype(bf16)
    row = iota((LINES * 32, 384), 0)
    lane = iota((LINES * 32, 384), 1)
    spread = (lane == (SPAN - 1 - row % 32) * LINES + row // 32) & (row % 32 < SPAN)
    spread = spread.astype(f32).astype(bf16)
    row, lane = iota((6 * LINES, 384), 0) % LINES, iota((6 * LINES, 384), 1) % LINES
    levels_differ = row // WLAT != lane // WLAT
    rows_differ = (row % WLAT >= WLAT // 2) != (lane % WLAT >= WLAT // 2)
    for (table_of, last), out_of in zip(tables, outs, strict=True):
        for head in range(6):
            stacked[head * 24 : head * 24 + SPAN, :] = table_of(head)
        picked = sum(dot_nt(pick, part) for part in three_parts(stacked[...]))
        for head in range(6):
            for key in range(LINES):
                spread_from[head * LINES : (head + 1) * LINES, key * 32 : key * 32 + 24] = picked[
                    key * LINES : (key + 1) * LINES, head * 24 : (head + 1) * 24
                ]
        flat = sum(dot(part, spread) for part in three_parts(spread_from[...]))
        apart = levels_differ if last is None else levels_differ | (rows_differ & (last > 0))
        flat = jnp.where(apart, MASKED, flat)
        for o in range(WLON):
            start = (WLON - 1 - o) * LINES
            piece = flat[:, start : start + CELLS]
            for head in range(6):
                out_of(head, o * LINES, piece[head * LINES : (head + 1) * LINES])


def writer(out_ref, base):
    def write(head, at, piece):
        out_ref[base + head, at : at + LINES, :] = piece

    return write


def reader(table_ref, row, base):
    return lambda head: table_ref[row, base + head, :, 0, :]


def expand_first(fine_ref, bias0_ref, stacked, spread_from):
    expand_bias([(reader(fine_ref, 0, 0), None)], [writer(bias0_ref, 0)], stacked, spread_from)


def expand_others(last, fine_ref, coarse_ref, bias1_ref, bias2_ref, stacked, spread_from):
    tables = [(reader(fine_ref, 1, 0), last), (reader(coarse_ref, 0, 0), last), (reader(coarse_ref, 0, 6), last)]
    expand_bias(tables, [writer(bias1_ref, 0), writer(bias2_ref, 0), writer(bias2_ref, 6)], stacked, spread_from)


def attend_group(q, k, v, bias, heads):
    queries, width = q.shape
    of_head = iota((queries, width), 1) // HD
    big = jnp.concatenate([jnp.where(of_head == h, q, 0.0) for h in range(heads)], axis=0)
    scores = dot_nt(big.astype(bf16), k) * HD ** (-0.5) + bias.reshape(heads * queries, CELLS)
    top = jnp.max(scores, axis=-1, keepdims=True)
    weights = jnp.exp(scores - top)
    total = jnp.sum(weights, axis=-1, keepdims=True)
    mixed = dot(weights.astype(bf16), v) * (1.0 / total)
    out = jnp.zeros((queries, width), f32)
    for h in range(heads):
        out = jnp.where(of_head == h, mixed[h * queries : (h + 1) * queries], out)
    return out


def tiles_of(rows, width):
    return ((-(-width // 128), rows, 128), f32)


def put(ref, at, rows, stride, values):
    width = values.shape[-1]
    for t in range(ref.shape[0]):
        piece = values[:, t * 128 : min((t + 1) * 128, width)]
        if piece.shape[-1] < 128:
            piece = jnp.concatenate([piece, jnp.zeros((rows, 128 - piece.shape[-1]), f32)], axis=-1)
        ref[t, pl.ds(at, rows, stride=stride), :] = piece


def get(ref, at, rows, stride, width):
    pieces = [ref[t, pl.ds(at, rows, stride=stride), :] for t in range(ref.shape[0])]
    return jnp.concatenate(pieces, axis=-1)[:, :width]


def pack_lines(first, second):
    return jnp.concatenate(first + [jnp.concatenate([second[i], second[3 + i]], axis=-1) for i in range(3)], axis=0)


def unpack_line(packed, i, size):
    first = packed[i * size : (i + 1) * size]
    at = (6 + i % 3) * size
    second = packed[at : at + size, i // 3 * 64 : i // 3 * 64 + 64]
    return jnp.concatenate([first, second], axis=-1)


def prepare_kernel(
    flags_ref, fields_ref, fine_ref, coarse_ref, below_ref, corner_ref, bias0_ref, bias1_ref, bias2_ref,
    line_ref, stacked, spread_from,
):
    lines = [fields_ref[z, a].astype(f32) for z in range(WZ) for a in range(3)]
    packed = pack_lines([line[:, :128] for line in lines], [line[:, 128:] for line in lines])
    for ref, start in ((below_ref, 0), (corner_ref, 6)):
        for i in range(9):
            line_ref[i * 18 : (i + 1) * 18, :] = packed[i * 24 + start : i * 24 + start + 18]
        ref[...] = line_ref[...].astype(bf16)
    expand_first(fine_ref, bias0_ref, stacked, spread_from)

    @pl.when(flags_ref[1] > 0)
    def _():
        expand_others(flags_ref[0], fine_ref, coarse_ref, bias1_ref, bias2_ref, stacked, spread_from)


def attend_fine(x_ref, bias_ref, qkv_ref, proj_ref):
    normed = normalise(get(x_ref, 72, 432, 1, 192))
    q = dot(normed, qkv_ref[:, 0:192]).astype(bf16).astype(f32)
    k = dot(normed, qkv_ref[:, 192:384]).astype(bf16)
    v = dot(normed, qkv_ref[:, 384:576]).astype(bf16)
    left, right = [], []
    for window, start, stop in ((0, 72, 144), (1, 0, 144), (2, 0, 72)):
        at = window * CELLS
        q_rows = q[at + start : at + stop]
        k_rows, v_rows = k[at : at + CELLS], v[at : at + CELLS]
        bias = bias_ref[:, start:stop, :]
        left.append(attend_group(q_rows[:, :128], k_rows[:, :128], v_rows[:, :128], bias[:4], 4))
        right.append(attend_group(q_rows[:, 128:], k_rows[:, 128:], v_rows[:, 128:], bias[4:], 2))
    left = jnp.concatenate(left, axis=0).astype(bf16)
    right = jnp.concatenate(right, axis=0).astype(bf16)
    product = dot(left, proj_ref[0:128, :]) + dot(right, proj_ref[128:192, :])
    return (get(x_ref, 144, 288, 1, 192) + product).astype(bf16)


def first_rows_kernel(left_ref, own_ref, bias_ref, qkv_ref, proj_ref, out_ref, send_ref, x_ref, a_ref):
    for z in range(WZ):
        for a in range(WLAT):
            put(x_ref, z * WLAT + a, 24, LINES, left_ref[z, 3 + a].astype(f32))
            put(x_ref, 288 + z * WLAT + a, 24, LINES, own_ref[z, 3 + a].astype(f32))
    attended = attend_fine(x_ref, bias_ref, qkv_ref, proj_ref)
    out_ref[...] = attended
    put(a_ref, 0, 288, 1, attended.astype(f32))
    lines = [a_ref[t, pl.ds(z * WLAT + a, 24, stride=LINES), :] for t in range(2) for z in range(WZ) for a in range(3)]
    send_ref[...] = pack_lines(lines[:6], [line[:, :64] for line in lines[6:]]).astype(bf16)


def second_rows_kernel(
    flags_ref, left_ref, own_ref, corner_ref, below_ref, first_ref, fine_ref, coarse_ref, old1_ref, old2_ref,
    qkv_ref, proj_ref, up_ref, down_ref, out_ref, bias2_ref, bias1_ref, x_ref, a_ref, w_ref, stacked, spread_from,
):

    @pl.when(flags_ref[1] > 0)
    def _():
        bias1_ref[...] = old1_ref[...]
        bias2_ref[...] = old2_ref[...]

    @pl.when(flags_ref[1] == 0)
    def _():
        expand_others(flags_ref[0], fine_ref, coarse_ref, bias1_ref, bias2_ref, stacked, spread_from)

    below, corner = below_ref[...].astype(f32), corner_ref[...].astype(f32)
    for z in range(WZ):
        for a in range(WLAT):
            at = z * WLAT + a
            if a < 3:
                put(x_ref, at, 24, LINES, left_ref[z, 9 + a].astype(f32))
                put(x_ref, 288 + at, 24, LINES, own_ref[z, 9 + a].astype(f32))
            else:
                put(x_ref, 72 + at, 18, LINES, unpack_line(corner, z * 3 + a - 3, 18))
                put(x_ref, 288 + at, 18, LINES, unpack_line(below, z * 3 + a - 3, 18))
    put(a_ref, 0, 288, 1, first_ref[...].astype(f32))
    put(a_ref, 288, 288, 1, attend_fine(x_ref, bias1_ref, qkv_ref, proj_ref).astype(f32))
    for t in range(2):
        for rho in range(3, 12):
            for z in range(WZ):
                at = rho // WLAT * 288 + z * WLAT + rho % WLAT
                to = ((rho - 3) * WZ + z) * 24
                w_ref[t, to : to + 24, :] = a_ref[t, pl.ds(at, 24, stride=LINES), :]
    for i in range(3):
        x = get(w_ref, i * 144, 144, 1, 192)
        out_ref[i * 144 : (i + 1) * 144, :] = fine_feed_forward(x, up_ref, down_ref).astype(bf16)


def coarse_kernel(
    y_ref, got_ref, fine_up_ref, fine_down_ref, merge_ref, bias_ref, qkv_ref, proj_ref, up_ref, down_ref,
    keep_ref, lower_ref, corner_ref, left_ref, w_ref, p_ref, o_ref,
):
    got = got_ref[...].astype(f32)
    got = jnp.concatenate([unpack_line(got, z * 3 + a, 24) for a in range(3) for z in range(WZ)], axis=0)
    put(w_ref, 0, 432, 1, y_ref[...].astype(f32))
    put(w_ref, 432, 144, 1, fine_feed_forward(got, fine_up_ref, fine_down_ref))
    parts = []
    for pa in range(2):
        for pb in range(2):
            for t in range(2):
                for z in range(WZ):
                    for i in range(WLAT):
                        at = ((2 * i + pa) * WZ + z) * 24 + pb
                        line = w_ref[t, pl.ds(at, WLON, stride=2), :]
                        p_ref[t, pl.ds(len(parts) * CELLS + z * WLAT + i, WLON, stride=LINES), :] = line
            parts.append(get(p_ref, len(parts) * CELLS, CELLS, 1, 192))
    mean = sum(jnp.sum(part, axis=-1, keepdims=True) for part in parts) * (1.0 / 768)
    parts = [part - mean for part in parts]
    variance = sum(jnp.sum(part * part, axis=-1, keepdims=True) for part in parts) * (1.0 / 768)
    scale = lax.rsqrt(variance + EPSILON)
    merged = sum(
        dot((part * scale).astype(bf16), merge_ref[i * 192 : (i + 1) * 192, :]) for i, part in enumerate(parts)
    )
    merged = merged.astype(bf16).astype(f32)
    normed = normalise(merged)
    qkv = dot(normed, qkv_ref[...]).astype(bf16)
    product = merged
    for g in range(3):
        q = qkv[:, g * 128 : (g + 1) * 128].astype(f32)
        k = qkv[:, 384 + g * 128 : 384 + (g + 1) * 128]
        v = qkv[:, 768 + g * 128 : 768 + (g + 1) * 128]
        mixed = attend_group(q, k, v, bias_ref[g * 4 : (g + 1) * 4], 4)
        product = product + dot(mixed.astype(bf16), proj_ref[g * 128 : (g + 1) * 128, :])
    attended = product.astype(bf16).astype(f32)
    put(o_ref, 0, CELLS, 1, feed_forward(attended, up_ref, down_ref))
    for i in range(3):
        for j in range(WLON):
            for ref, row in ((left_ref, i), (corner_ref, 3 + i)) if j < 6 else ((keep_ref, i), (lower_ref, 3 + i)):
                ref[i, j % 6] = get(o_ref, j * LINES + row, WZ, WLAT, 384).astype(bf16)


def call(kernel, outs, scratch, operands, flops, smem=0):
    specs = [pl.BlockSpec(memory_space=pltpu.SMEM)] * smem
    specs += [pl.BlockSpec(memory_space=pltpu.VMEM)] * (len(operands) - smem)
    return pl.pallas_call(
        kernel,
        out_shape=[jax.ShapeDtypeStruct(shape, dtype) for shape, dtype in outs],
        in_specs=specs,
        out_specs=[pl.BlockSpec(memory_space=pltpu.VMEM)] * len(outs),
        scratch_shapes=[pltpu.VMEM(shape, dtype) for shape, dtype in scratch],
        compiler_params=pltpu.CompilerParams(vmem_limit_bytes=VMEM_LIMIT),
        cost_estimate=pl.CostEstimate(
            flops=flops,
            bytes_accessed=sum(a.size * a.dtype.itemsize for a in operands),
            transcendentals=0,
        ),
    )(*operands)


def body(
    fields,
    fine_bias,
    fine_qkv,
    fine_proj,
    fine_up,
    fine_down,
    merge_weight,
    coarse_bias,
    coarse_qkv,
    coarse_proj,
    coarse_up,
    coarse_down,
):
    lat, lats = lax.axis_index("lat"), lax.axis_size("lat")
    lon, lons = lax.axis_index("lon"), lax.axis_size("lon")
    flags = jnp.stack([lat == lats - 1, (lat < lats // 2) & (lon < lons // 2)]).astype(jnp.int32)
    fine_tables = fine_bias.transpose(0, 2, 3, 1, 4)
    coarse_tables = coarse_bias.transpose(0, 2, 3, 1, 4)
    fine_down = fine_down.T
    expansion = [((CELLS, CELLS), f32), ((6 * LINES, LINES * 32), f32)]
    biases = [((6, CELLS, CELLS), f32), ((12, CELLS, CELLS), f32)]
    left = from_behind(fields, 1, 0)
    below, corner, bias0, bias1, bias2 = call(
        prepare_kernel,
        [((162, 128), bf16), ((162, 128), bf16), ((6, CELLS, CELLS), f32)] + biases,
        [((162, 128), f32)] + expansion,
        [flags, fields, fine_tables, coarse_tables],
        1_000_000_000,
        smem=1,
    )
    corner = from_behind(corner, 1, -1)
    below = from_behind(below, 0, -1)
    first, edge = call(
        first_rows_kernel,
        [((288, 192), bf16), ((216, 128), bf16)],
        [tiles_of(576, 192), tiles_of(288, 192)],
        [left, fields, bias0, fine_qkv, fine_proj],
        1_000_000_000,
    )
    got = from_behind(edge, 0, -1)
    finished, bias2 = call(
        second_rows_kernel,
        [((432, 192), bf16), biases[1]],
        [biases[0], tiles_of(576, 192), tiles_of(576, 192), tiles_of(432, 192)] + expansion,
        [flags, left, fields, corner, below, first, fine_tables, coarse_tables, bias1, bias2]
        + [fine_qkv, fine_proj, fine_up, fine_down],
        3_000_000_000,
        smem=1,
    )
    quarter = ((3, 6, WZ, 384), bf16)
    keep, lower, far_corner, upper_left = call(
        coarse_kernel,
        [quarter] * 4,
        [tiles_of(576, 192), tiles_of(576, 192), tiles_of(CELLS, 384)],
        [finished, got, fine_up, fine_down, merge_weight, bias2, coarse_qkv, coarse_proj, coarse_up, coarse_down],
        4_000_000_000,
    )
    above = from_behind(lower, 0, 1)
    corner = from_behind(far_corner, -1, 1)
    right = from_behind(upper_left, -1, 0)
    rows = [jnp.concatenate([above, corner], axis=1), jnp.concatenate([keep, right], axis=1)]
    return jnp.concatenate(rows, axis=0).transpose(2, 0, 1, 3)


def solution(mesh):
    return jax.shard_map(
        body,
        mesh=mesh,
        in_specs=(
            P(None, "lat", "lon", None),
            P("lat", None, None, None, None),
            P(),
            P(),
            P(),
            P(),
            P(),
            P("lat", None, None, None, None),
            P(),
            P(),
            P(),
            P(),
        ),
        out_specs=P(None, "lat", "lon", None),
        check_vma=False,
    )
```

```python
import functools

import jax
import jax.numpy as jnp
from jax import lax
from jax.experimental import pallas as pl
from jax.experimental.pallas import tpu as pltpu
from jax.sharding import PartitionSpec as P

HD = 32
WZ = 2
WLAT = 6
WLON = 12
CELLS = WZ * WLAT * WLON
LINES = WZ * WLAT
SPAN = 2 * WLON - 1
EPSILON = 1e-05
MASKED = -1e30
VMEM_LIMIT = 40 * 1024 * 1024

f32 = jnp.float32
bf16 = jnp.bfloat16


def from_behind(shard, lon, lat):
    lons, lats = lax.axis_size("lon"), lax.axis_size("lat")
    pairs = [
        (o * lats + a, (o + lon) % lons * lats + (a + lat) % lats) for o in range(lons) for a in range(lats)
    ]
    return lax.ppermute(shard, ("lon", "lat"), pairs)


def normalise(values):
    centred = values - jnp.mean(values, axis=-1, keepdims=True)
    variance = jnp.mean(centred * centred, axis=-1, keepdims=True)
    return (centred * lax.rsqrt(variance + EPSILON)).astype(bf16)


def dot(a, b):
    return jnp.dot(a, b, preferred_element_type=f32)


def dot_nt(a, b):
    return lax.dot_general(a, b, (((1,), (1,)), ((), ())), preferred_element_type=f32)


def gelu(x):
    return 0.5 * x * (1.0 + lax.erf(x * (2.0**-0.5)))


def feed_forward(x, up_ref, down_ref):
    hidden = gelu(dot(normalise(x), up_ref[...])).astype(bf16)
    return (x + dot(hidden, down_ref[...])).astype(bf16).astype(f32)


def fine_feed_forward(x, up_ref, down_ref):
    hidden = gelu(dot(normalise(x), up_ref[...])).astype(bf16)
    return (x + dot_nt(hidden, down_ref[...])).astype(bf16).astype(f32)


def three_parts(x):
    high = x.astype(bf16)
    rest = x - high.astype(f32)
    middle = rest.astype(bf16)
    low = (rest - middle.astype(f32)).astype(bf16)
    return high, middle, low


def iota(shape, axis):
    return lax.broadcasted_iota(jnp.int32, shape, axis)


def expand_bias(tables, outs, stacked, spread_from):
    stacked[...] = jnp.zeros_like(stacked)
    spread_from[...] = jnp.zeros_like(spread_from)
    row = iota((CELLS, CELLS), 0)
    key, query = row // LINES, row % LINES
    z_key, z_query = 1 - key // WLAT, 1 - query // WLAT
    column = ((z_query * WZ + z_key) * WLAT + query % WLAT) * WLAT + key % WLAT
    pick = (iota((CELLS, CELLS), 1) == column).astype(f32).astype(bf16)
    row = iota((LINES * 32, 384), 0)
    lane = iota((LINES * 32, 384), 1)
    spread = (lane == (SPAN - 1 - row % 32) * LINES + row // 32) & (row % 32 < SPAN)
    spread = spread.astype(f32).astype(bf16)
    row, lane = iota((6 * LINES, 384), 0) % LINES, iota((6 * LINES, 384), 1) % LINES
    levels_differ = row // WLAT != lane // WLAT
    rows_differ = (row % WLAT >= WLAT // 2) != (lane % WLAT >= WLAT // 2)
    for (table_of, last), out_of in zip(tables, outs, strict=True):
        for head in range(6):
            stacked[head * 24 : head * 24 + SPAN, :] = table_of(head)
        picked = sum(dot_nt(pick, part) for part in three_parts(stacked[...]))
        for head in range(6):
            for key in range(LINES):
                spread_from[head * LINES : (head + 1) * LINES, key * 32 : key * 32 + 24] = picked[
                    key * LINES : (key + 1) * LINES, head * 24 : (head + 1) * 24
                ]
        flat = sum(dot(part, spread) for part in three_parts(spread_from[...]))
        apart = levels_differ if last is None else levels_differ | (rows_differ & (last > 0))
        flat = jnp.where(apart, MASKED, flat)
        for o in range(WLON):
            start = (WLON - 1 - o) * LINES
            piece = flat[:, start : start + CELLS]
            for head in range(6):
                out_of(head, o * LINES, piece[head * LINES : (head + 1) * LINES])


def writer(out_ref, base):
    def write(head, at, piece):
        out_ref[base + head, at : at + LINES, :] = piece

    return write


def reader(table_ref, row, base):
    return lambda head: table_ref[row, base + head, :, 0, :]


def attend_group(q, k, v, bias, heads):
    queries, width = q.shape
    of_head = iota((queries, width), 1) // HD
    big = jnp.concatenate([jnp.where(of_head == h, q, 0.0) for h in range(heads)], axis=0)
    scores = dot_nt(big.astype(bf16), k) * HD ** (-0.5) + bias.reshape(heads * queries, CELLS)
    top = jnp.max(scores, axis=-1, keepdims=True)
    weights = jnp.exp(scores - top)
    total = jnp.sum(weights, axis=-1, keepdims=True)
    mixed = dot(weights.astype(bf16), v) * (1.0 / total)
    out = jnp.zeros((queries, width), f32)
    for h in range(heads):
        out = jnp.where(of_head == h, mixed[h * queries : (h + 1) * queries], out)
    return out


def tiles_of(rows, width):
    return ((-(-width // 128), rows, 128), f32)


def put(ref, at, rows, stride, values):
    width = values.shape[-1]
    for t in range(ref.shape[0]):
        piece = values[:, t * 128 : min((t + 1) * 128, width)]
        if piece.shape[-1] < 128:
            piece = jnp.concatenate([piece, jnp.zeros((rows, 128 - piece.shape[-1]), f32)], axis=-1)
        ref[t, pl.ds(at, rows, stride=stride), :] = piece


def get(ref, at, rows, stride, width):
    pieces = [ref[t, pl.ds(at, rows, stride=stride), :] for t in range(ref.shape[0])]
    return jnp.concatenate(pieces, axis=-1)[:, :width]


def pack_lines(first, second):
    return jnp.concatenate(first + [jnp.concatenate([second[i], second[3 + i]], axis=-1) for i in range(3)], axis=0)


def unpack_line(packed, i, size):
    first = packed[i * size : (i + 1) * size]
    at = (6 + i % 3) * size
    second = packed[at : at + size, i // 3 * 64 : i // 3 * 64 + 64]
    return jnp.concatenate([first, second], axis=-1)


def expand_all(last, fine_ref, coarse_ref, bias0_ref, bias1_ref, bias2_ref, stacked, spread_from):
    tables = [
        (reader(fine_ref, 0, 0), None),
        (reader(fine_ref, 1, 0), last),
        (reader(coarse_ref, 0, 0), last),
        (reader(coarse_ref, 0, 6), last),
    ]
    outs = [writer(bias0_ref, 0), writer(bias1_ref, 0), writer(bias2_ref, 0), writer(bias2_ref, 6)]
    expand_bias(tables, outs, stacked, spread_from)


def prepare_kernel(
    flags_ref, fields_hbm, fine_hbm, coarse_hbm, qkv_hbm, proj_hbm, below_ref, corner_ref, own_ref, fine_ref,
    coarse_ref, qkv_ref, proj_ref, bias0_ref, bias1_ref, bias2_ref, line_ref, stacked, spread_from, sems,
):
    moves = [
        (fields_hbm.at[:, 0:3], own_ref.at[:, 0:3]),
        (fine_hbm, fine_ref),
        (coarse_hbm, coarse_ref),
        (fields_hbm.at[:, 3:12], own_ref.at[:, 3:12]),
        (qkv_hbm, qkv_ref),
        (proj_hbm, proj_ref),
    ]
    copies = [pltpu.make_async_copy(source, to, sems.at[i]) for i, (source, to) in enumerate(moves)]
    for copy in copies:
        copy.start()
    copies[0].wait()
    lines = [own_ref[z, a].astype(f32) for z in range(WZ) for a in range(3)]
    packed = pack_lines([line[:, :128] for line in lines], [line[:, 128:] for line in lines])
    for ref, start in ((below_ref, 0), (corner_ref, 6)):
        for i in range(9):
            line_ref[i * 18 : (i + 1) * 18, :] = packed[i * 24 + start : i * 24 + start + 18]
        ref[...] = line_ref[...].astype(bf16)

    for copy in copies[1:]:
        copy.wait()

    @pl.when(flags_ref[1] > 0)
    def _():
        expand_all(flags_ref[0], fine_ref, coarse_ref, bias0_ref, bias1_ref, bias2_ref, stacked, spread_from)


def attend_fine(x_ref, bias_ref, qkv_ref, proj_ref):
    normed = normalise(get(x_ref, 72, 432, 1, 192))
    q = dot(normed, qkv_ref[:, 0:192]).astype(bf16).astype(f32)
    k = dot(normed, qkv_ref[:, 192:384]).astype(bf16)
    v = dot(normed, qkv_ref[:, 384:576]).astype(bf16)
    left, right = [], []
    for window, start, stop in ((0, 72, 144), (1, 0, 144), (2, 0, 72)):
        at = window * CELLS
        q_rows = q[at + start : at + stop]
        k_rows, v_rows = k[at : at + CELLS], v[at : at + CELLS]
        bias = bias_ref[:, start:stop, :]
        left.append(attend_group(q_rows[:, :128], k_rows[:, :128], v_rows[:, :128], bias[:4], 4))
        right.append(attend_group(q_rows[:, 128:], k_rows[:, 128:], v_rows[:, 128:], bias[4:], 2))
    left = jnp.concatenate(left, axis=0).astype(bf16)
    right = jnp.concatenate(right, axis=0).astype(bf16)
    product = dot(left, proj_ref[0:128, :]) + dot(right, proj_ref[128:192, :])
    return (get(x_ref, 144, 288, 1, 192) + product).astype(bf16)


def first_rows_kernel(
    flags_ref, left_ref, own_ref, fine_ref, coarse_ref, old0_ref, old1_ref, old2_ref, qkv_ref, proj_ref,
    out_ref, send_ref, bias1_ref, bias2_ref, bias0_ref, x_ref, a_ref, stacked, spread_from,
):
    @pl.when(flags_ref[1] > 0)
    def _():
        bias0_ref[...] = old0_ref[...]
        bias1_ref[...] = old1_ref[...]
        bias2_ref[...] = old2_ref[...]

    @pl.when(flags_ref[1] == 0)
    def _():
        expand_all(flags_ref[0], fine_ref, coarse_ref, bias0_ref, bias1_ref, bias2_ref, stacked, spread_from)

    for z in range(WZ):
        for a in range(WLAT):
            put(x_ref, z * WLAT + a, 24, LINES, left_ref[z, 3 + a].astype(f32))
            put(x_ref, 288 + z * WLAT + a, 24, LINES, own_ref[z, 3 + a].astype(f32))
    attended = attend_fine(x_ref, bias0_ref, qkv_ref, proj_ref)
    out_ref[...] = attended
    put(a_ref, 0, 288, 1, attended.astype(f32))
    lines = [a_ref[t, pl.ds(z * WLAT + a, 24, stride=LINES), :] for t in range(2) for z in range(WZ) for a in range(3)]
    send_ref[...] = pack_lines(lines[:6], [line[:, :64] for line in lines[6:]]).astype(bf16)


def second_rows_kernel(
    left_ref, own_ref, corner_ref, below_ref, first_ref, bias1_ref, qkv_ref, proj_ref, up_ref, down_ref,
    out_ref, x_ref, a_ref, w_ref,
):
    below, corner = below_ref[...].astype(f32), corner_ref[...].astype(f32)
    for z in range(WZ):
        for a in range(WLAT):
            at = z * WLAT + a
            if a < 3:
                put(x_ref, at, 24, LINES, left_ref[z, 9 + a].astype(f32))
                put(x_ref, 288 + at, 24, LINES, own_ref[z, 9 + a].astype(f32))
            else:
                put(x_ref, 72 + at, 18, LINES, unpack_line(corner, z * 3 + a - 3, 18))
                put(x_ref, 288 + at, 18, LINES, unpack_line(below, z * 3 + a - 3, 18))
    put(a_ref, 0, 288, 1, first_ref[...].astype(f32))
    put(a_ref, 288, 288, 1, attend_fine(x_ref, bias1_ref, qkv_ref, proj_ref).astype(f32))
    for t in range(2):
        for rho in range(3, 12):
            for z in range(WZ):
                at = rho // WLAT * 288 + z * WLAT + rho % WLAT
                to = ((rho - 3) * WZ + z) * 24
                w_ref[t, to : to + 24, :] = a_ref[t, pl.ds(at, 24, stride=LINES), :]
    for i in range(3):
        x = get(w_ref, i * 144, 144, 1, 192)
        out_ref[i * 144 : (i + 1) * 144, :] = fine_feed_forward(x, up_ref, down_ref).astype(bf16)


def coarse_kernel(
    y_ref, got_ref, fine_up_ref, fine_down_ref, merge_ref, bias_ref, qkv_ref, proj_ref, up_ref, down_ref,
    keep_ref, lower_ref, corner_ref, left_ref, w_ref, p_ref, o_ref,
):
    got = got_ref[...].astype(f32)
    got = jnp.concatenate([unpack_line(got, z * 3 + a, 24) for a in range(3) for z in range(WZ)], axis=0)
    put(w_ref, 0, 432, 1, y_ref[...].astype(f32))
    put(w_ref, 432, 144, 1, fine_feed_forward(got, fine_up_ref, fine_down_ref))
    parts = []
    for pa in range(2):
        for pb in range(2):
            for t in range(2):
                for z in range(WZ):
                    for i in range(WLAT):
                        at = ((2 * i + pa) * WZ + z) * 24 + pb
                        line = w_ref[t, pl.ds(at, WLON, stride=2), :]
                        p_ref[t, pl.ds(len(parts) * CELLS + z * WLAT + i, WLON, stride=LINES), :] = line
            parts.append(get(p_ref, len(parts) * CELLS, CELLS, 1, 192))
    mean = sum(jnp.sum(part, axis=-1, keepdims=True) for part in parts) * (1.0 / 768)
    parts = [part - mean for part in parts]
    variance = sum(jnp.sum(part * part, axis=-1, keepdims=True) for part in parts) * (1.0 / 768)
    scale = lax.rsqrt(variance + EPSILON)
    merged = sum(
        dot((part * scale).astype(bf16), merge_ref[i * 192 : (i + 1) * 192, :]) for i, part in enumerate(parts)
    )
    merged = merged.astype(bf16).astype(f32)
    normed = normalise(merged)
    qkv = dot(normed, qkv_ref[...]).astype(bf16)
    product = merged
    for g in range(3):
        q = qkv[:, g * 128 : (g + 1) * 128].astype(f32)
        k = qkv[:, 384 + g * 128 : 384 + (g + 1) * 128]
        v = qkv[:, 768 + g * 128 : 768 + (g + 1) * 128]
        mixed = attend_group(q, k, v, bias_ref[g * 4 : (g + 1) * 4], 4)
        product = product + dot(mixed.astype(bf16), proj_ref[g * 128 : (g + 1) * 128, :])
    attended = product.astype(bf16).astype(f32)
    put(o_ref, 0, CELLS, 1, feed_forward(attended, up_ref, down_ref))
    for i in range(3):
        for j in range(WLON):
            for ref, row in ((left_ref, i), (corner_ref, 3 + i)) if j < 6 else ((keep_ref, i), (lower_ref, 3 + i)):
                ref[i, j % 6] = get(o_ref, j * LINES + row, WZ, WLAT, 384).astype(bf16)


def call(kernel, outs, scratch, operands, flops, smem=0):
    specs = [pl.BlockSpec(memory_space=pltpu.SMEM)] * smem
    specs += [pl.BlockSpec(memory_space=pltpu.VMEM)] * (len(operands) - smem)
    return pl.pallas_call(
        kernel,
        out_shape=[jax.ShapeDtypeStruct(shape, dtype) for shape, dtype in outs],
        in_specs=specs,
        out_specs=[pl.BlockSpec(memory_space=pltpu.VMEM)] * len(outs),
        scratch_shapes=[pltpu.VMEM(shape, dtype) for shape, dtype in scratch],
        compiler_params=pltpu.CompilerParams(vmem_limit_bytes=VMEM_LIMIT),
        cost_estimate=pl.CostEstimate(
            flops=flops,
            bytes_accessed=sum(a.size * a.dtype.itemsize for a in operands),
            transcendentals=0,
        ),
    )(*operands)


def body(
    fields,
    fine_bias,
    fine_qkv,
    fine_proj,
    fine_up,
    fine_down,
    merge_weight,
    coarse_bias,
    coarse_qkv,
    coarse_proj,
    coarse_up,
    coarse_down,
):
    lat, lats = lax.axis_index("lat"), lax.axis_size("lat")
    lon, lons = lax.axis_index("lon"), lax.axis_size("lon")
    flags = jnp.stack([lat == lats - 1, (lat < lats // 2) & (lon < lons // 2)]).astype(jnp.int32)
    fine_tables = fine_bias.transpose(0, 2, 3, 1, 4)
    coarse_tables = coarse_bias.transpose(0, 2, 3, 1, 4)
    fine_down = fine_down.T
    expansion = [((CELLS, CELLS), f32), ((6 * LINES, LINES * 32), f32)]
    biases = [((6, CELLS, CELLS), f32), ((12, CELLS, CELLS), f32)]
    left = from_behind(fields, 1, 0)
    sources = [fields, fine_tables, coarse_tables, fine_qkv, fine_proj]
    hbm, vmem, smem = (pl.BlockSpec(memory_space=space) for space in (pltpu.HBM, pltpu.VMEM, pltpu.SMEM))
    below, corner, own, fine_tables, coarse_tables, fine_qkv, fine_proj, bias0, bias1, bias2 = pl.pallas_call(
        prepare_kernel,
        out_shape=[jax.ShapeDtypeStruct((162, 128), bf16)] * 2
        + [jax.ShapeDtypeStruct(source.shape, source.dtype) for source in sources]
        + [jax.ShapeDtypeStruct(shape, dtype) for shape, dtype in [((6, CELLS, CELLS), f32)] + biases],
        in_specs=[smem] + [hbm] * 5,
        out_specs=[vmem] * 10,
        scratch_shapes=[pltpu.VMEM((162, 128), f32)]
        + [pltpu.VMEM(shape, dtype) for shape, dtype in expansion]
        + [pltpu.SemaphoreType.DMA((6,))],
        compiler_params=pltpu.CompilerParams(vmem_limit_bytes=VMEM_LIMIT),
    )(flags, *(pltpu.with_memory_space_constraint(source, pltpu.HBM) for source in sources))
    corner = from_behind(corner, 1, -1)
    below = from_behind(below, 0, -1)
    first, edge, bias1, bias2 = call(
        first_rows_kernel,
        [((288, 192), bf16), ((216, 128), bf16)] + biases,
        [((6, CELLS, CELLS), f32), tiles_of(576, 192), tiles_of(288, 192)] + expansion,
        [flags, left, own, fine_tables, coarse_tables, bias0, bias1, bias2, fine_qkv, fine_proj],
        1_000_000_000,
        smem=1,
    )
    got = from_behind(edge, 0, -1)
    (finished,) = call(
        second_rows_kernel,
        [((432, 192), bf16)],
        [tiles_of(576, 192), tiles_of(576, 192), tiles_of(432, 192)],
        [left, own, corner, below, first, bias1, fine_qkv, fine_proj, fine_up, fine_down],
        3_000_000_000,
    )
    quarter = ((3, 6, WZ, 384), bf16)
    keep, lower, far_corner, upper_left = call(
        coarse_kernel,
        [quarter] * 4,
        [tiles_of(576, 192), tiles_of(576, 192), tiles_of(CELLS, 384)],
        [finished, got, fine_up, fine_down, merge_weight, bias2, coarse_qkv, coarse_proj, coarse_up, coarse_down],
        4_000_000_000,
    )
    above = from_behind(lower, 0, 1)
    corner = from_behind(far_corner, -1, 1)
    right = from_behind(upper_left, -1, 0)
    rows = [jnp.concatenate([above, corner], axis=1), jnp.concatenate([keep, right], axis=1)]
    return jnp.concatenate(rows, axis=0).transpose(2, 0, 1, 3)


def solution(mesh):
    return jax.shard_map(
        body,
        mesh=mesh,
        in_specs=(
            P(None, "lat", "lon", None),
            P("lat", None, None, None, None),
            P(),
            P(),
            P(),
            P(),
            P(),
            P("lat", None, None, None, None),
            P(),
            P(),
            P(),
            P(),
        ),
        out_specs=P(None, "lat", "lon", None),
        check_vma=False,
    )
```

```python
import functools

import jax
import jax.numpy as jnp
from jax import lax
from jax.experimental import pallas as pl
from jax.experimental.pallas import tpu as pltpu
from jax.sharding import PartitionSpec as P

HD = 32
WZ = 2
WLAT = 6
WLON = 12
CELLS = WZ * WLAT * WLON
LINES = WZ * WLAT
SPAN = 2 * WLON - 1
EPSILON = 1e-05
MASKED = -1e30
VMEM_LIMIT = 40 * 1024 * 1024

f32 = jnp.float32
bf16 = jnp.bfloat16


def from_behind(shard, lon, lat):
    lons, lats = lax.axis_size("lon"), lax.axis_size("lat")
    pairs = [
        (o * lats + a, (o + lon) % lons * lats + (a + lat) % lats) for o in range(lons) for a in range(lats)
    ]
    return lax.ppermute(shard, ("lon", "lat"), pairs)


def normalise(values):
    centred = values - jnp.mean(values, axis=-1, keepdims=True)
    variance = jnp.mean(centred * centred, axis=-1, keepdims=True)
    return (centred * lax.rsqrt(variance + EPSILON)).astype(bf16)


def dot(a, b):
    return jnp.dot(a, b, preferred_element_type=f32)


def dot_nt(a, b):
    return lax.dot_general(a, b, (((1,), (1,)), ((), ())), preferred_element_type=f32)


def gelu(x):
    return 0.5 * x * (1.0 + lax.erf(x * (2.0**-0.5)))


def feed_forward(x, up_ref, down_ref):
    hidden = gelu(dot(normalise(x), up_ref[...])).astype(bf16)
    return (x + dot(hidden, down_ref[...])).astype(bf16).astype(f32)


def fine_feed_forward(x, up_ref, down_ref):
    hidden = gelu(dot(normalise(x), up_ref[...])).astype(bf16)
    return (x + dot_nt(hidden, down_ref[...])).astype(bf16).astype(f32)


def three_parts(x):
    high = x.astype(bf16)
    rest = x - high.astype(f32)
    middle = rest.astype(bf16)
    low = (rest - middle.astype(f32)).astype(bf16)
    return high, middle, low


def iota(shape, axis):
    return lax.broadcasted_iota(jnp.int32, shape, axis)


def expand_bias(tables, outs, stacked, spread_from):
    stacked[...] = jnp.zeros_like(stacked)
    row = iota((LINES * 16, CELLS), 0)
    key, query = row // 16, row % 16
    z_key, z_query = 1 - key // WLAT, 1 - query // WLAT
    column = ((z_query * WZ + z_key) * WLAT + query % WLAT) * WLAT + key % WLAT
    pick = ((iota((LINES * 16, CELLS), 1) == column) & (query < LINES)).astype(f32).astype(bf16)
    row = iota((LINES * 32, 384), 0)
    lane = iota((LINES * 32, 384), 1)
    spread = (lane == (SPAN - 1 - row % 32) * LINES + row // 32) & (row % 32 < SPAN)
    spread = spread.astype(f32).astype(bf16)
    row, lane = iota((6 * 16, 384), 0) % 16, iota((6 * 16, 384), 1) % LINES
    levels_differ = row // WLAT != lane // WLAT
    rows_differ = (row % WLAT >= WLAT // 2) != (lane % WLAT >= WLAT // 2)
    slot = iota((16, 128), 1) // 32
    for (table_of, last), out_of in zip(tables, outs, strict=True):
        for head in range(6):
            stacked[head * 32 : head * 32 + SPAN, :] = table_of(head)
        picked = sum(dot_nt(pick, part) for part in three_parts(stacked[...]))
        picked = [picked[:, :128], jnp.concatenate([picked[:, 128:], jnp.zeros((LINES * 16, 64), f32)], axis=-1)]
        rolled = [[half] + [pltpu.roll(half, 32 * r, 1) for r in range(1, 4)] for half in picked]
        for head in range(6):
            for group in range(3):
                block = None
                for at in range(4):
                    key = group * 4 + at
                    piece = rolled[head // 4][(at - head) % 4][key * 16 : (key + 1) * 16]
                    block = piece if block is None else jnp.where(slot == at, piece, block)
                spread_from[head * 16 : (head + 1) * 16, group * 128 : (group + 1) * 128] = block
        flat = sum(dot(part, spread) for part in three_parts(spread_from[...]))
        apart = levels_differ if last is None else levels_differ | (rows_differ & (last > 0))
        flat = jnp.where(apart, MASKED, flat)
        for o in range(WLON):
            start = (WLON - 1 - o) * LINES
            piece = flat[:, start : start + CELLS]
            for head in range(6):
                out_of(head, o * LINES, piece[head * 16 : head * 16 + LINES])


def writer(out_ref, base):
    def write(head, at, piece):
        out_ref[base + head, at : at + LINES, :] = piece

    return write


def reader(table_ref, row, base):
    return lambda head: table_ref[row, base + head, :, 0, :]


def attend_group(q, k, v, bias, heads):
    queries, width = q.shape
    of_head = iota((queries, width), 1) // HD
    big = jnp.concatenate([jnp.where(of_head == h, q, 0.0) for h in range(heads)], axis=0)
    scores = dot_nt(big.astype(bf16), k) * HD ** (-0.5) + bias.reshape(heads * queries, CELLS)
    top = jnp.max(scores, axis=-1, keepdims=True)
    weights = jnp.exp(scores - top)
    total = jnp.sum(weights, axis=-1, keepdims=True)
    mixed = dot(weights.astype(bf16), v) * (1.0 / total)
    out = jnp.zeros((queries, width), f32)
    for h in range(heads):
        out = jnp.where(of_head == h, mixed[h * queries : (h + 1) * queries], out)
    return out


def tiles_of(rows, width):
    return ((-(-width // 128), rows, 128), f32)


def put(ref, at, rows, stride, values):
    width = values.shape[-1]
    for t in range(ref.shape[0]):
        piece = values[:, t * 128 : min((t + 1) * 128, width)]
        if piece.shape[-1] < 128:
            piece = jnp.concatenate([piece, jnp.zeros((rows, 128 - piece.shape[-1]), f32)], axis=-1)
        ref[t, pl.ds(at, rows, stride=stride), :] = piece


def get(ref, at, rows, stride, width):
    pieces = [ref[t, pl.ds(at, rows, stride=stride), :] for t in range(ref.shape[0])]
    return jnp.concatenate(pieces, axis=-1)[:, :width]


def pack_lines(first, second):
    return jnp.concatenate(first + [jnp.concatenate([second[i], second[3 + i]], axis=-1) for i in range(3)], axis=0)


def unpack_line(packed, i, size):
    first = packed[i * size : (i + 1) * size]
    at = (6 + i % 3) * size
    second = packed[at : at + size, i // 3 * 64 : i // 3 * 64 + 64]
    return jnp.concatenate([first, second], axis=-1)


def expand_first(fine_ref, bias0_ref, stacked, spread_from):
    expand_bias([(reader(fine_ref, 0, 0), None)], [writer(bias0_ref, 0)], stacked, spread_from)


def expand_others(last, fine_ref, coarse_ref, bias1_ref, bias2_ref, stacked, spread_from):
    tables = [(reader(fine_ref, 1, 0), last), (reader(coarse_ref, 0, 0), last), (reader(coarse_ref, 0, 6), last)]
    expand_bias(tables, [writer(bias1_ref, 0), writer(bias2_ref, 0), writer(bias2_ref, 6)], stacked, spread_from)


def prepare_kernel(
    flags_ref, fields_hbm, fine_hbm, coarse_hbm, qkv_hbm, proj_hbm, below_ref, corner_ref, own_ref, fine_ref,
    coarse_ref, qkv_ref, proj_ref, bias0_ref, bias1_ref, bias2_ref, line_ref, stacked, spread_from, sems,
):
    moves = [
        (fields_hbm.at[:, 0:3], own_ref.at[:, 0:3]),
        (fine_hbm, fine_ref),
        (coarse_hbm, coarse_ref),
        (fields_hbm.at[:, 3:12], own_ref.at[:, 3:12]),
        (qkv_hbm, qkv_ref),
        (proj_hbm, proj_ref),
    ]
    copies = [pltpu.make_async_copy(source, to, sems.at[i]) for i, (source, to) in enumerate(moves)]
    for copy in copies:
        copy.start()
    copies[0].wait()
    lines = [own_ref[z, a].astype(f32) for z in range(WZ) for a in range(3)]
    packed = pack_lines([line[:, :128] for line in lines], [line[:, 128:] for line in lines])
    for ref, start in ((below_ref, 0), (corner_ref, 6)):
        for i in range(9):
            line_ref[i * 18 : (i + 1) * 18, :] = packed[i * 24 + start : i * 24 + start + 18]
        ref[...] = line_ref[...].astype(bf16)

    for copy in copies[1:]:
        copy.wait()

    @pl.when(flags_ref[1] > 0)
    def _():
        expand_first(fine_ref, bias0_ref, stacked, spread_from)
        expand_others(flags_ref[0], fine_ref, coarse_ref, bias1_ref, bias2_ref, stacked, spread_from)


def other_bias_kernel(flags_ref, fine_ref, coarse_ref, after_ref, bias1_ref, bias2_ref, stacked, spread_from):
    @pl.when(flags_ref[1] == 0)
    def _():
        expand_others(flags_ref[0], fine_ref, coarse_ref, bias1_ref, bias2_ref, stacked, spread_from)


def attend_fine(x_ref, bias, qkv_ref, proj_ref):
    normed = normalise(get(x_ref, 72, 432, 1, 192))
    q = dot(normed, qkv_ref[:, 0:192]).astype(bf16).astype(f32)
    k = dot(normed, qkv_ref[:, 192:384]).astype(bf16)
    v = dot(normed, qkv_ref[:, 384:576]).astype(bf16)
    left, right = [], []
    for window, start, stop in ((0, 72, 144), (1, 0, 144), (2, 0, 72)):
        at = window * CELLS
        q_rows = q[at + start : at + stop]
        k_rows, v_rows = k[at : at + CELLS], v[at : at + CELLS]
        left.append(attend_group(q_rows[:, :128], k_rows[:, :128], v_rows[:, :128], bias(0, 4, start, stop), 4))
        right.append(attend_group(q_rows[:, 128:], k_rows[:, 128:], v_rows[:, 128:], bias(4, 6, start, stop), 2))
    left = jnp.concatenate(left, axis=0).astype(bf16)
    right = jnp.concatenate(right, axis=0).astype(bf16)
    product = dot(left, proj_ref[0:128, :]) + dot(right, proj_ref[128:192, :])
    return (get(x_ref, 144, 288, 1, 192) + product).astype(bf16)


def early_or_late(flags_ref, early_ref, late_ref):
    return lambda head, last, start, stop: jnp.where(
        flags_ref[1] > 0, early_ref[head:last, start:stop, :], late_ref[head:last, start:stop, :]
    )


def first_rows_kernel(
    flags_ref, left_ref, own_ref, fine_ref, early0_ref, qkv_ref, proj_ref,
    out_ref, send_ref, late0_ref, x_ref, a_ref, stacked, spread_from,
):
    @pl.when(flags_ref[1] == 0)
    def _():
        expand_first(fine_ref, late0_ref, stacked, spread_from)

    for z in range(WZ):
        for a in range(WLAT):
            put(x_ref, z * WLAT + a, 24, LINES, left_ref[z, 3 + a].astype(f32))
            put(x_ref, 288 + z * WLAT + a, 24, LINES, own_ref[z, 3 + a].astype(f32))
    attended = attend_fine(x_ref, early_or_late(flags_ref, early0_ref, late0_ref), qkv_ref, proj_ref)
    out_ref[...] = attended
    put(a_ref, 0, 288, 1, attended.astype(f32))
    lines = [a_ref[t, pl.ds(z * WLAT + a, 24, stride=LINES), :] for t in range(2) for z in range(WZ) for a in range(3)]
    send_ref[...] = pack_lines(lines[:6], [line[:, :64] for line in lines[6:]]).astype(bf16)


def second_rows_kernel(
    flags_ref, left_ref, own_ref, corner_ref, below_ref, first_ref, early1_ref, late1_ref, qkv_ref, proj_ref, up_ref,
    down_ref, out_ref, x_ref, a_ref, w_ref,
):
    below, corner = below_ref[...].astype(f32), corner_ref[...].astype(f32)
    for z in range(WZ):
        for a in range(WLAT):
            at = z * WLAT + a
            if a < 3:
                put(x_ref, at, 24, LINES, left_ref[z, 9 + a].astype(f32))
                put(x_ref, 288 + at, 24, LINES, own_ref[z, 9 + a].astype(f32))
            else:
                put(x_ref, 72 + at, 18, LINES, unpack_line(corner, z * 3 + a - 3, 18))
                put(x_ref, 288 + at, 18, LINES, unpack_line(below, z * 3 + a - 3, 18))
    put(a_ref, 0, 288, 1, first_ref[...].astype(f32))
    bias = early_or_late(flags_ref, early1_ref, late1_ref)
    put(a_ref, 288, 288, 1, attend_fine(x_ref, bias, qkv_ref, proj_ref).astype(f32))
    for t in range(2):
        for rho in range(3, 12):
            for z in range(WZ):
                at = rho // WLAT * 288 + z * WLAT + rho % WLAT
                to = ((rho - 3) * WZ + z) * 24
                w_ref[t, to : to + 24, :] = a_ref[t, pl.ds(at, 24, stride=LINES), :]
    for i in range(3):
        x = get(w_ref, i * 144, 144, 1, 192)
        out_ref[i * 144 : (i + 1) * 144, :] = fine_feed_forward(x, up_ref, down_ref).astype(bf16)


def coarse_kernel(
    flags_ref, y_ref, got_ref, fine_up_ref, fine_down_ref, merge_ref, early2_ref, late2_ref, qkv_ref, proj_ref, up_ref, down_ref,
    keep_ref, lower_ref, corner_ref, left_ref, w_ref, p_ref, o_ref,
):
    got = got_ref[...].astype(f32)
    got = jnp.concatenate([unpack_line(got, z * 3 + a, 24) for a in range(3) for z in range(WZ)], axis=0)
    put(w_ref, 0, 432, 1, y_ref[...].astype(f32))
    put(w_ref, 432, 144, 1, fine_feed_forward(got, fine_up_ref, fine_down_ref))
    parts = []
    for pa in range(2):
        for pb in range(2):
            for t in range(2):
                for z in range(WZ):
                    for i in range(WLAT):
                        at = ((2 * i + pa) * WZ + z) * 24 + pb
                        line = w_ref[t, pl.ds(at, WLON, stride=2), :]
                        p_ref[t, pl.ds(len(parts) * CELLS + z * WLAT + i, WLON, stride=LINES), :] = line
            parts.append(get(p_ref, len(parts) * CELLS, CELLS, 1, 192))
    mean = sum(jnp.sum(part, axis=-1, keepdims=True) for part in parts) * (1.0 / 768)
    parts = [part - mean for part in parts]
    variance = sum(jnp.sum(part * part, axis=-1, keepdims=True) for part in parts) * (1.0 / 768)
    scale = lax.rsqrt(variance + EPSILON)
    merged = sum(
        dot((part * scale).astype(bf16), merge_ref[i * 192 : (i + 1) * 192, :]) for i, part in enumerate(parts)
    )
    merged = merged.astype(bf16).astype(f32)
    normed = normalise(merged)
    qkv = dot(normed, qkv_ref[...]).astype(bf16)
    product = merged
    bias = early_or_late(flags_ref, early2_ref, late2_ref)
    for g in range(3):
        q = qkv[:, g * 128 : (g + 1) * 128].astype(f32)
        k = qkv[:, 384 + g * 128 : 384 + (g + 1) * 128]
        v = qkv[:, 768 + g * 128 : 768 + (g + 1) * 128]
        mixed = attend_group(q, k, v, bias(g * 4, (g + 1) * 4, 0, CELLS), 4)
        product = product + dot(mixed.astype(bf16), proj_ref[g * 128 : (g + 1) * 128, :])
    attended = product.astype(bf16).astype(f32)
    put(o_ref, 0, CELLS, 1, feed_forward(attended, up_ref, down_ref))
    for i in range(3):
        for j in range(WLON):
            for ref, row in ((left_ref, i), (corner_ref, 3 + i)) if j < 6 else ((keep_ref, i), (lower_ref, 3 + i)):
                ref[i, j % 6] = get(o_ref, j * LINES + row, WZ, WLAT, 384).astype(bf16)


def call(kernel, outs, scratch, operands, flops, smem=0):
    specs = [pl.BlockSpec(memory_space=pltpu.SMEM)] * smem
    specs += [pl.BlockSpec(memory_space=pltpu.VMEM)] * (len(operands) - smem)
    return pl.pallas_call(
        kernel,
        out_shape=[jax.ShapeDtypeStruct(shape, dtype) for shape, dtype in outs],
        in_specs=specs,
        out_specs=[pl.BlockSpec(memory_space=pltpu.VMEM)] * len(outs),
        scratch_shapes=[pltpu.VMEM(shape, dtype) for shape, dtype in scratch],
        compiler_params=pltpu.CompilerParams(vmem_limit_bytes=VMEM_LIMIT),
        cost_estimate=pl.CostEstimate(
            flops=flops,
            bytes_accessed=sum(a.size * a.dtype.itemsize for a in operands),
            transcendentals=0,
        ),
    )(*operands)


def body(
    fields,
    fine_bias,
    fine_qkv,
    fine_proj,
    fine_up,
    fine_down,
    merge_weight,
    coarse_bias,
    coarse_qkv,
    coarse_proj,
    coarse_up,
    coarse_down,
):
    lat, lats = lax.axis_index("lat"), lax.axis_size("lat")
    lon, lons = lax.axis_index("lon"), lax.axis_size("lon")
    flags = jnp.stack([lat == lats - 1, (lat < lats // 2) & (lon < lons // 2)]).astype(jnp.int32)
    fine_tables = fine_bias.transpose(0, 2, 3, 1, 4)
    coarse_tables = coarse_bias.transpose(0, 2, 3, 1, 4)
    fine_down = fine_down.T
    expansion = [((6 * 32, CELLS), f32), ((6 * 16, LINES * 32), f32)]
    biases = [((6, CELLS, CELLS), f32), ((12, CELLS, CELLS), f32)]
    left = from_behind(fields, 1, 0)
    sources = [fields, fine_tables, coarse_tables, fine_qkv, fine_proj]
    hbm, vmem, smem = (pl.BlockSpec(memory_space=space) for space in (pltpu.HBM, pltpu.VMEM, pltpu.SMEM))
    below, corner, own, fine_tables, coarse_tables, fine_qkv, fine_proj, bias0, bias1, bias2 = pl.pallas_call(
        prepare_kernel,
        out_shape=[jax.ShapeDtypeStruct((162, 128), bf16)] * 2
        + [jax.ShapeDtypeStruct(source.shape, source.dtype) for source in sources]
        + [jax.ShapeDtypeStruct(shape, dtype) for shape, dtype in [((6, CELLS, CELLS), f32)] + biases],
        in_specs=[smem] + [hbm] * 5,
        out_specs=[vmem] * 10,
        scratch_shapes=[pltpu.VMEM((162, 128), f32)]
        + [pltpu.VMEM(shape, dtype) for shape, dtype in expansion]
        + [pltpu.SemaphoreType.DMA((6,))],
        compiler_params=pltpu.CompilerParams(vmem_limit_bytes=VMEM_LIMIT),
    )(flags, *(pltpu.with_memory_space_constraint(source, pltpu.HBM) for source in sources))
    corner = from_behind(corner, 1, -1)
    below = from_behind(below, 0, -1)
    first, edge = call(
        first_rows_kernel,
        [((288, 192), bf16), ((216, 128), bf16)],
        [((6, CELLS, CELLS), f32), tiles_of(576, 192), tiles_of(288, 192)] + expansion,
        [flags, left, own, fine_tables, bias0, fine_qkv, fine_proj],
        1_000_000_000,
        smem=1,
    )
    got = from_behind(edge, 0, -1)
    late1, late2 = call(
        other_bias_kernel, biases, expansion, [flags, fine_tables, coarse_tables, first], 2_000_000_000, smem=1
    )
    (finished,) = call(
        second_rows_kernel,
        [((432, 192), bf16)],
        [tiles_of(576, 192), tiles_of(576, 192), tiles_of(432, 192)],
        [flags, left, own, corner, below, first, bias1, late1, fine_qkv, fine_proj, fine_up, fine_down],
        3_000_000_000,
        smem=1,
    )
    quarter = ((3, 6, WZ, 384), bf16)
    keep, lower, far_corner, upper_left = call(
        coarse_kernel,
        [quarter] * 4,
        [tiles_of(576, 192), tiles_of(576, 192), tiles_of(CELLS, 384)],
        [flags, finished, got, fine_up, fine_down, merge_weight, bias2, late2]
        + [coarse_qkv, coarse_proj, coarse_up, coarse_down],
        4_000_000_000,
        smem=1,
    )
    above = from_behind(lower, 0, 1)
    corner = from_behind(far_corner, -1, 1)
    right = from_behind(upper_left, -1, 0)
    rows = [jnp.concatenate([above, corner], axis=1), jnp.concatenate([keep, right], axis=1)]
    return jnp.concatenate(rows, axis=0).transpose(2, 0, 1, 3)


def solution(mesh):
    return jax.shard_map(
        body,
        mesh=mesh,
        in_specs=(
            P(None, "lat", "lon", None),
            P("lat", None, None, None, None),
            P(),
            P(),
            P(),
            P(),
            P(),
            P("lat", None, None, None, None),
            P(),
            P(),
            P(),
            P(),
        ),
        out_specs=P(None, "lat", "lon", None),
        check_vma=False,
    )
```

```python
import functools

import jax
import jax.numpy as jnp
from jax import lax
from jax.experimental import pallas as pl
from jax.experimental.pallas import tpu as pltpu
from jax.sharding import PartitionSpec as P

HD = 32
WZ = 2
WLAT = 6
WLON = 12
CELLS = WZ * WLAT * WLON
LINES = WZ * WLAT
SPAN = 2 * WLON - 1
EPSILON = 1e-05
MASKED = -1e30
VMEM_LIMIT = 40 * 1024 * 1024

f32 = jnp.float32
bf16 = jnp.bfloat16


def from_behind(shard, lon, lat):
    lons, lats = lax.axis_size("lon"), lax.axis_size("lat")
    pairs = [
        (o * lats + a, (o + lon) % lons * lats + (a + lat) % lats) for o in range(lons) for a in range(lats)
    ]
    return lax.ppermute(shard, ("lon", "lat"), pairs)


def normalise(values):
    centred = values - jnp.mean(values, axis=-1, keepdims=True)
    variance = jnp.mean(centred * centred, axis=-1, keepdims=True)
    return (centred * lax.rsqrt(variance + EPSILON)).astype(bf16)


def dot(a, b):
    return jnp.dot(a, b, preferred_element_type=f32)


def dot_nt(a, b):
    return lax.dot_general(a, b, (((1,), (1,)), ((), ())), preferred_element_type=f32)


def gelu(x):
    return 0.5 * x * (1.0 + lax.erf(x * (2.0**-0.5)))


def feed_forward(x, up_ref, down_ref):
    hidden = gelu(dot(normalise(x), up_ref[...])).astype(bf16)
    return (x + dot(hidden, down_ref[...])).astype(bf16).astype(f32)


def fine_feed_forward(x, up_ref, down_ref):
    hidden = gelu(dot(normalise(x), up_ref[...])).astype(bf16)
    return (x + dot_nt(hidden, down_ref[...])).astype(bf16).astype(f32)


def three_parts(x):
    high = x.astype(bf16)
    rest = x - high.astype(f32)
    middle = rest.astype(bf16)
    low = (rest - middle.astype(f32)).astype(bf16)
    return high, middle, low


def iota(shape, axis):
    return lax.broadcasted_iota(jnp.int32, shape, axis)


def expand_bias(tables, outs, stacked, spread_from):
    stacked[...] = jnp.zeros_like(stacked)
    row = iota((LINES * 16, CELLS), 0)
    key, query = row // 16, row % 16
    z_key, z_query = 1 - key // WLAT, 1 - query // WLAT
    column = ((z_query * WZ + z_key) * WLAT + query % WLAT) * WLAT + key % WLAT
    pick = ((iota((LINES * 16, CELLS), 1) == column) & (query < LINES)).astype(f32).astype(bf16)
    row = iota((LINES * 32, 384), 0)
    lane = iota((LINES * 32, 384), 1)
    spread = (lane == (SPAN - 1 - row % 32) * LINES + row // 32) & (row % 32 < SPAN)
    spread = spread.astype(f32).astype(bf16)
    row, lane = iota((6 * 16, 384), 0) % 16, iota((6 * 16, 384), 1) % LINES
    levels_differ = row // WLAT != lane // WLAT
    rows_differ = (row % WLAT >= WLAT // 2) != (lane % WLAT >= WLAT // 2)
    slot = iota((16, 128), 1) // 32
    for (table_of, last), out_of in zip(tables, outs, strict=True):
        for head in range(6):
            stacked[head * 32 : head * 32 + SPAN, :] = table_of(head)
        picked = sum(dot_nt(pick, part) for part in three_parts(stacked[...]))
        picked = [picked[:, :128], jnp.concatenate([picked[:, 128:], jnp.zeros((LINES * 16, 64), f32)], axis=-1)]
        rolled = [[half] + [pltpu.roll(half, 32 * r, 1) for r in range(1, 4)] for half in picked]
        for head in range(6):
            for group in range(3):
                block = None
                for at in range(4):
                    key = group * 4 + at
                    piece = rolled[head // 4][(at - head) % 4][key * 16 : (key + 1) * 16]
                    block = piece if block is None else jnp.where(slot == at, piece, block)
                spread_from[head * 16 : (head + 1) * 16, group * 128 : (group + 1) * 128] = block
        flat = sum(dot(part, spread) for part in three_parts(spread_from[...]))
        apart = levels_differ if last is None else levels_differ | (rows_differ & (last > 0))
        flat = jnp.where(apart, MASKED, flat)
        for o in range(WLON):
            start = (WLON - 1 - o) * LINES
            piece = flat[:, start : start + CELLS]
            for head in range(6):
                out_of(head, o * LINES, piece[head * 16 : head * 16 + LINES])


def writer(out_ref, base):
    def write(head, at, piece):
        out_ref[base + head, at : at + LINES, :] = piece

    return write


def reader(table_ref, row, base):
    return lambda head: table_ref[row, base + head, :, 0, :]


def attend_group(q, k, v, bias, heads):
    queries, width = q.shape
    of_head = iota((queries, width), 1) // HD
    big = jnp.concatenate([jnp.where(of_head == h, q, 0.0) for h in range(heads)], axis=0)
    scores = dot_nt(big.astype(bf16), k) * HD ** (-0.5) + bias.reshape(heads * queries, CELLS)
    top = jnp.max(scores, axis=-1, keepdims=True)
    weights = jnp.exp(scores - top)
    total = jnp.sum(weights, axis=-1, keepdims=True)
    mixed = dot(weights.astype(bf16), v) * (1.0 / total)
    out = jnp.zeros((queries, width), f32)
    for h in range(heads):
        out = jnp.where(of_head == h, mixed[h * queries : (h + 1) * queries], out)
    return out


def tiles_of(rows, width):
    return ((-(-width // 128), rows, 128), f32)


def put(ref, at, rows, stride, values):
    width = values.shape[-1]
    for t in range(ref.shape[0]):
        piece = values[:, t * 128 : min((t + 1) * 128, width)]
        if piece.shape[-1] < 128:
            piece = jnp.concatenate([piece, jnp.zeros((rows, 128 - piece.shape[-1]), f32)], axis=-1)
        ref[t, pl.ds(at, rows, stride=stride), :] = piece


def get(ref, at, rows, stride, width):
    pieces = [ref[t, pl.ds(at, rows, stride=stride), :] for t in range(ref.shape[0])]
    return jnp.concatenate(pieces, axis=-1)[:, :width]


def pack_lines(first, second):
    return jnp.concatenate(first + [jnp.concatenate([second[i], second[3 + i]], axis=-1) for i in range(3)], axis=0)


def unpack_line(packed, i, size):
    first = packed[i * size : (i + 1) * size]
    at = (6 + i % 3) * size
    second = packed[at : at + size, i // 3 * 64 : i // 3 * 64 + 64]
    return jnp.concatenate([first, second], axis=-1)


def expand_first(fine_ref, bias0_ref, stacked, spread_from):
    expand_bias([(reader(fine_ref, 0, 0), None)], [writer(bias0_ref, 0)], stacked, spread_from)


def expand_others(last, fine_ref, coarse_ref, bias1_ref, bias2_ref, stacked, spread_from):
    tables = [(reader(fine_ref, 1, 0), last), (reader(coarse_ref, 0, 0), last), (reader(coarse_ref, 0, 6), last)]
    expand_bias(tables, [writer(bias1_ref, 0), writer(bias2_ref, 0), writer(bias2_ref, 6)], stacked, spread_from)


def prepare_kernel(
    flags_ref, fields_hbm, fine_hbm, coarse_hbm, qkv_hbm, proj_hbm, below_ref, corner_ref, own_ref, fine_ref,
    coarse_ref, qkv_ref, proj_ref, bias0_ref, bias1_ref, bias2_ref, line_ref, stacked, spread_from, sems,
):
    moves = [
        (fields_hbm.at[:, 0:3], own_ref.at[:, 0:3]),
        (fine_hbm, fine_ref),
        (coarse_hbm, coarse_ref),
        (fields_hbm.at[:, 3:12], own_ref.at[:, 3:12]),
        (qkv_hbm, qkv_ref),
        (proj_hbm, proj_ref),
    ]
    copies = [pltpu.make_async_copy(source, to, sems.at[i]) for i, (source, to) in enumerate(moves)]
    for copy in copies:
        copy.start()
    copies[0].wait()
    lines = [own_ref[z, a].astype(f32) for z in range(WZ) for a in range(3)]
    packed = pack_lines([line[:, :128] for line in lines], [line[:, 128:] for line in lines])
    for ref, start in ((below_ref, 0), (corner_ref, 6)):
        for i in range(9):
            line_ref[i * 18 : (i + 1) * 18, :] = packed[i * 24 + start : i * 24 + start + 18]
        ref[...] = line_ref[...].astype(bf16)

    for copy in copies[1:]:
        copy.wait()

    @pl.when(flags_ref[1] > 0)
    def _():
        expand_first(fine_ref, bias0_ref, stacked, spread_from)
        expand_others(flags_ref[0], fine_ref, coarse_ref, bias1_ref, bias2_ref, stacked, spread_from)


def other_bias_kernel(flags_ref, fine_ref, coarse_ref, after_ref, bias1_ref, bias2_ref, stacked, spread_from):
    @pl.when(flags_ref[1] == 0)
    def _():
        expand_others(flags_ref[0], fine_ref, coarse_ref, bias1_ref, bias2_ref, stacked, spread_from)


def attend_fine(x_ref, m_ref, qkv_ref, proj_ref, with_bias):
    normed = normalise(get(x_ref, 72, 432, 1, 192))
    q = dot(normed, qkv_ref[:, 0:192]).astype(bf16).astype(f32)
    k = dot(normed, qkv_ref[:, 192:384]).astype(bf16)
    v = dot(normed, qkv_ref[:, 384:576]).astype(bf16)

    def attend(bias_ref):
        to = 0
        for window, start, stop in ((0, 72, 144), (1, 0, 144), (2, 0, 72)):
            at, rows = window * CELLS, stop - start
            q_rows = q[at + start : at + stop]
            k_rows, v_rows = k[at : at + CELLS], v[at : at + CELLS]
            for t, lanes, heads in ((0, slice(0, 128), slice(0, 4)), (1, slice(128, 192), slice(4, 6))):
                mixed = attend_group(
                    q_rows[:, lanes], k_rows[:, lanes], v_rows[:, lanes], bias_ref[heads, start:stop, :],
                    heads.stop - heads.start,
                )
                m_ref[t, to : to + rows, 0 : mixed.shape[-1]] = mixed
            to += rows

    with_bias(attend)
    product = dot(m_ref[0].astype(bf16), proj_ref[0:128, :]) + dot(m_ref[1, :, 0:64].astype(bf16), proj_ref[128:192, :])
    return (get(x_ref, 144, 288, 1, 192) + product).astype(bf16)


def early_or_late(flags_ref, early_ref, late_ref):
    def with_bias(attend):
        @pl.when(flags_ref[1] > 0)
        def _():
            attend(early_ref)

        @pl.when(flags_ref[1] == 0)
        def _():
            attend(late_ref)

    return with_bias


def merge_tokens(parts, merge_ref):
    mean = sum(jnp.sum(part, axis=-1, keepdims=True) for part in parts) * (1.0 / 768)
    parts = [part - mean for part in parts]
    variance = sum(jnp.sum(part * part, axis=-1, keepdims=True) for part in parts) * (1.0 / 768)
    scale = lax.rsqrt(variance + EPSILON)
    merged = sum(
        dot((part * scale).astype(bf16), merge_ref[i * 192 : (i + 1) * 192, :]) for i, part in enumerate(parts)
    )
    return merged.astype(bf16)


def first_rows_kernel(
    flags_ref, left_ref, own_ref, fine_ref, early0_ref, qkv_ref, proj_ref, up_hbm, down_hbm, merge_hbm,
    out_ref, send_ref, up_ref, down_ref, merge_ref,
    late0_ref, x_ref, a_ref, m_ref, e_ref, stacked, spread_from, sems,
):
    moves = [(up_hbm, up_ref), (down_hbm, down_ref), (merge_hbm, merge_ref)]
    copies = [pltpu.make_async_copy(source, to, sems.at[i]) for i, (source, to) in enumerate(moves)]
    for copy in copies:
        copy.start()
    for z in range(WZ):
        for a in range(WLAT):
            put(x_ref, z * WLAT + a, 24, LINES, left_ref[z, 3 + a].astype(f32))
            put(x_ref, 288 + z * WLAT + a, 24, LINES, own_ref[z, 3 + a].astype(f32))

    @pl.when(flags_ref[1] == 0)
    def _():
        expand_first(fine_ref, late0_ref, stacked, spread_from)

    attended = attend_fine(x_ref, m_ref, qkv_ref, proj_ref, early_or_late(flags_ref, early0_ref, late0_ref))
    out_ref[...] = attended
    put(a_ref, 0, 288, 1, attended.astype(f32))
    for copy in copies:
        copy.wait()
    edge = [get(a_ref, z * WLAT + a, 24, LINES, 192) for a in range(3) for z in range(WZ)]
    put(e_ref, 0, 144, 1, fine_feed_forward(jnp.concatenate(edge, axis=0), up_ref, down_ref))
    parts = [get(e_ref, 48 + pa * 48 + pb, 24, 2, 192) for pa in range(2) for pb in range(2)]
    merged = merge_tokens(parts, merge_ref).astype(f32)
    row = get(e_ref, 0, 48, 1, 192)
    pieces = [row[:, :128], jnp.concatenate([row[:24, 128:], row[24:, 128:]], axis=-1)]
    pieces += [merged[:, t * 128 : (t + 1) * 128] for t in range(3)]
    send_ref[...] = jnp.concatenate(pieces, axis=0).astype(bf16)


def second_rows_kernel(
    flags_ref, left_ref, own_ref, corner_ref, below_ref, first_ref, early1_ref, late1_ref, qkv_ref, proj_ref, up_ref,
    down_ref, merge_ref, out_ref, last_ref, x_ref, a_ref, w_ref, m_ref,
):
    below, corner = below_ref[...].astype(f32), corner_ref[...].astype(f32)
    for z in range(WZ):
        for a in range(WLAT):
            at = z * WLAT + a
            if a < 3:
                put(x_ref, at, 24, LINES, left_ref[z, 9 + a].astype(f32))
                put(x_ref, 288 + at, 24, LINES, own_ref[z, 9 + a].astype(f32))
            else:
                put(x_ref, 72 + at, 18, LINES, unpack_line(corner, z * 3 + a - 3, 18))
                put(x_ref, 288 + at, 18, LINES, unpack_line(below, z * 3 + a - 3, 18))
    put(a_ref, 0, 288, 1, first_ref[...].astype(f32))
    attended = attend_fine(x_ref, m_ref, qkv_ref, proj_ref, early_or_late(flags_ref, early1_ref, late1_ref))
    put(a_ref, 288, 288, 1, attended.astype(f32))
    for t in range(2):
        for rho in range(3, 12):
            for z in range(WZ):
                at = rho // WLAT * 288 + z * WLAT + rho % WLAT
                to = ((rho - 3) * WZ + z) * 24
                w_ref[t, to : to + 24, :] = a_ref[t, pl.ds(at, 24, stride=LINES), :]
    for i in range(3):
        put(w_ref, i * 144, 144, 1, fine_feed_forward(get(w_ref, i * 144, 144, 1, 192), up_ref, down_ref))
    parts = [
        jnp.concatenate([get(w_ref, (2 * i + pa) * 48 + pb, 24, 2, 192) for i in range(4)], axis=0)
        for pa in range(2)
        for pb in range(2)
    ]
    out_ref[...] = merge_tokens(parts, merge_ref)
    last_ref[...] = get(w_ref, 384, 48, 1, 192).astype(bf16)


def coarse_kernel(
    flags_ref, rows_ref, last_ref, got_ref, merge_ref, early2_ref, late2_ref, qkv_ref, proj_ref, up_ref, down_ref,
    keep_ref, lower_ref, corner_ref, left_ref, r_ref, o_ref, m_ref,
):
    got = got_ref[...].astype(f32)
    put(r_ref, 0, 48, 1, last_ref[...].astype(f32))
    second = jnp.concatenate([got[48:72, :64], got[48:72, 64:]], axis=0)
    put(r_ref, 48, 48, 1, jnp.concatenate([got[:48], second], axis=-1))
    parts = [get(r_ref, pa * 48 + pb, 24, 2, 192) for pa in range(2) for pb in range(2)]
    fifth = merge_tokens(parts, merge_ref).astype(f32)
    sixth = jnp.concatenate([got[72 + t * 24 : 96 + t * 24] for t in range(3)], axis=-1)
    rows = jnp.concatenate([rows_ref[...].astype(f32), fifth, sixth], axis=0)
    for i in range(WLAT):
        for z in range(WZ):
            at = (i * WZ + z) * WLON
            put(o_ref, z * WLAT + i, WLON, LINES, rows[at : at + WLON])
    merged = get(o_ref, 0, CELLS, 1, 384)
    normed = normalise(merged)
    qkv = dot(normed, qkv_ref[...]).astype(bf16)

    def attend(bias_ref):
        for g in range(3):
            q = qkv[:, g * 128 : (g + 1) * 128].astype(f32)
            k = qkv[:, 384 + g * 128 : 384 + (g + 1) * 128]
            v = qkv[:, 768 + g * 128 : 768 + (g + 1) * 128]
            m_ref[:, g * 128 : (g + 1) * 128] = attend_group(q, k, v, bias_ref[g * 4 : (g + 1) * 4], 4).astype(bf16)

    early_or_late(flags_ref, early2_ref, late2_ref)(attend)
    product = merged + dot(m_ref[...], proj_ref[...])
    attended = product.astype(bf16).astype(f32)
    put(o_ref, 0, CELLS, 1, feed_forward(attended, up_ref, down_ref))
    for i in range(3):
        for j in range(WLON):
            for ref, row in ((left_ref, i), (corner_ref, 3 + i)) if j < 6 else ((keep_ref, i), (lower_ref, 3 + i)):
                ref[i, j % 6] = get(o_ref, j * LINES + row, WZ, WLAT, 384).astype(bf16)


def call(kernel, outs, scratch, operands, flops, smem=0):
    specs = [pl.BlockSpec(memory_space=pltpu.SMEM)] * smem
    specs += [pl.BlockSpec(memory_space=pltpu.VMEM)] * (len(operands) - smem)
    return pl.pallas_call(
        kernel,
        out_shape=[jax.ShapeDtypeStruct(shape, dtype) for shape, dtype in outs],
        in_specs=specs,
        out_specs=[pl.BlockSpec(memory_space=pltpu.VMEM)] * len(outs),
        scratch_shapes=[pltpu.VMEM(shape, dtype) for shape, dtype in scratch],
        compiler_params=pltpu.CompilerParams(vmem_limit_bytes=VMEM_LIMIT),
        cost_estimate=pl.CostEstimate(
            flops=flops,
            bytes_accessed=sum(a.size * a.dtype.itemsize for a in operands),
            transcendentals=0,
        ),
    )(*operands)


def body(
    fields,
    fine_bias,
    fine_qkv,
    fine_proj,
    fine_up,
    fine_down,
    merge_weight,
    coarse_bias,
    coarse_qkv,
    coarse_proj,
    coarse_up,
    coarse_down,
):
    lat, lats = lax.axis_index("lat"), lax.axis_size("lat")
    lon, lons = lax.axis_index("lon"), lax.axis_size("lon")
    early = (lat < lats // 4) | ((lat < lats // 2) & (lon < lons // 2))
    flags = jnp.stack([lat == lats - 1, early]).astype(jnp.int32)
    fine_tables = fine_bias.transpose(0, 2, 3, 1, 4)
    coarse_tables = coarse_bias.transpose(0, 2, 3, 1, 4)
    fine_down = fine_down.T
    expansion = [((6 * 32, CELLS), f32), ((6 * 16, LINES * 32), f32)]
    biases = [((6, CELLS, CELLS), f32), ((12, CELLS, CELLS), f32)]
    left = from_behind(fields, 1, 0)
    sources = [fields, fine_tables, coarse_tables, fine_qkv, fine_proj]
    hbm, vmem, smem = (pl.BlockSpec(memory_space=space) for space in (pltpu.HBM, pltpu.VMEM, pltpu.SMEM))
    below, corner, own, fine_tables, coarse_tables, fine_qkv, fine_proj, bias0, bias1, bias2 = pl.pallas_call(
        prepare_kernel,
        out_shape=[jax.ShapeDtypeStruct((162, 128), bf16)] * 2
        + [jax.ShapeDtypeStruct(source.shape, source.dtype) for source in sources]
        + [jax.ShapeDtypeStruct(shape, dtype) for shape, dtype in [((6, CELLS, CELLS), f32)] + biases],
        in_specs=[smem] + [hbm] * 5,
        out_specs=[vmem] * 10,
        scratch_shapes=[pltpu.VMEM((162, 128), f32)]
        + [pltpu.VMEM(shape, dtype) for shape, dtype in expansion]
        + [pltpu.SemaphoreType.DMA((6,))],
        compiler_params=pltpu.CompilerParams(vmem_limit_bytes=VMEM_LIMIT),
    )(flags, *(pltpu.with_memory_space_constraint(source, pltpu.HBM) for source in sources))
    corner = from_behind(corner, 1, -1)
    below = from_behind(below, 0, -1)
    weights = [fine_up, fine_down, merge_weight]
    first, edge, fine_up, fine_down, merge_weight = pl.pallas_call(
        first_rows_kernel,
        out_shape=[jax.ShapeDtypeStruct((288, 192), bf16), jax.ShapeDtypeStruct((144, 128), bf16)]
        + [jax.ShapeDtypeStruct(weight.shape, weight.dtype) for weight in weights],
        in_specs=[smem] + [vmem] * 6 + [hbm] * 3,
        out_specs=[vmem] * 5,
        scratch_shapes=[
            pltpu.VMEM(shape, dtype)
            for shape, dtype in [((6, CELLS, CELLS), f32), tiles_of(576, 192), tiles_of(288, 192), tiles_of(288, 192)]
            + [tiles_of(144, 192)]
            + expansion
        ]
        + [pltpu.SemaphoreType.DMA((3,))],
        compiler_params=pltpu.CompilerParams(vmem_limit_bytes=VMEM_LIMIT),
    )(
        *[flags, left, own, fine_tables, bias0, fine_qkv, fine_proj],
        *(pltpu.with_memory_space_constraint(weight, pltpu.HBM) for weight in weights),
    )
    got = from_behind(edge, 0, -1)
    late1, late2 = call(
        other_bias_kernel, biases, expansion, [flags, fine_tables, coarse_tables, first], 2_000_000_000, smem=1
    )
    rows, row = call(
        second_rows_kernel,
        [((96, 384), bf16), ((48, 192), bf16)],
        [tiles_of(576, 192), tiles_of(576, 192), tiles_of(432, 192), tiles_of(288, 192)],
        [flags, left, own, corner, below, first, bias1, late1, fine_qkv, fine_proj, fine_up, fine_down, merge_weight],
        3_000_000_000,
        smem=1,
    )
    quarter = ((3, 6, WZ, 384), bf16)
    keep, lower, far_corner, upper_left = call(
        coarse_kernel,
        [quarter] * 4,
        [tiles_of(96, 192), tiles_of(CELLS, 384), ((CELLS, 384), bf16)],
        [flags, rows, row, got, merge_weight, bias2, late2, coarse_qkv, coarse_proj, coarse_up, coarse_down],
        4_000_000_000,
        smem=1,
    )
    above = from_behind(lower, 0, 1)
    corner = from_behind(far_corner, -1, 1)
    right = from_behind(upper_left, -1, 0)
    rows = [jnp.concatenate([above, corner], axis=1), jnp.concatenate([keep, right], axis=1)]
    return jnp.concatenate(rows, axis=0).transpose(2, 0, 1, 3)


def solution(mesh):
    return jax.shard_map(
        body,
        mesh=mesh,
        in_specs=(
            P(None, "lat", "lon", None),
            P("lat", None, None, None, None),
            P(),
            P(),
            P(),
            P(),
            P(),
            P("lat", None, None, None, None),
            P(),
            P(),
            P(),
            P(),
        ),
        out_specs=P(None, "lat", "lon", None),
        check_vma=False,
    )
```

```python
import functools

import jax
import jax.numpy as jnp
from jax import lax
from jax.experimental import pallas as pl
from jax.experimental.pallas import tpu as pltpu
from jax.sharding import PartitionSpec as P

HD = 32
WZ = 2
WLAT = 6
WLON = 12
CELLS = WZ * WLAT * WLON
LINES = WZ * WLAT
SPAN = 2 * WLON - 1
EPSILON = 1e-05
MASKED = -1e30
VMEM_LIMIT = 40 * 1024 * 1024

f32 = jnp.float32
bf16 = jnp.bfloat16


def from_behind(shard, lon, lat):
    lons, lats = lax.axis_size("lon"), lax.axis_size("lat")
    pairs = [
        (o * lats + a, (o + lon) % lons * lats + (a + lat) % lats) for o in range(lons) for a in range(lats)
    ]
    return lax.ppermute(shard, ("lon", "lat"), pairs)


def normalise(values):
    centred = values - jnp.mean(values, axis=-1, keepdims=True)
    variance = jnp.mean(centred * centred, axis=-1, keepdims=True)
    return (centred * lax.rsqrt(variance + EPSILON)).astype(bf16)


def dot(a, b):
    return jnp.dot(a, b, preferred_element_type=f32)


def dot_nt(a, b):
    return lax.dot_general(a, b, (((1,), (1,)), ((), ())), preferred_element_type=f32)


def gelu(x):
    return 0.5 * x * (1.0 + lax.erf(x * (2.0**-0.5)))


def feed_forward(x, up_ref, down_ref):
    hidden = gelu(dot(normalise(x), up_ref[...])).astype(bf16)
    return (x + dot(hidden, down_ref[...])).astype(bf16).astype(f32)


def fine_feed_forward(x, up_ref, down_ref):
    hidden = gelu(dot(normalise(x), up_ref[...])).astype(bf16)
    return (x + dot_nt(hidden, down_ref[...])).astype(bf16).astype(f32)


def two_parts(x):
    high = x.astype(bf16)
    return high, (x - high.astype(f32)).astype(bf16)


def iota(shape, axis):
    return lax.broadcasted_iota(jnp.int32, shape, axis)


def expand_bias(tables, outs, stacked, spread_from):
    stacked[...] = jnp.zeros_like(stacked)
    row = iota((LINES * 16, CELLS), 0)
    key, query = row // 16, row % 16
    z_key, z_query = 1 - key // WLAT, 1 - query // WLAT
    column = ((z_query * WZ + z_key) * WLAT + query % WLAT) * WLAT + key % WLAT
    pick = ((iota((LINES * 16, CELLS), 1) == column) & (query < LINES)).astype(f32).astype(bf16)
    row = iota((LINES * 32, 384), 0)
    lane = iota((LINES * 32, 384), 1)
    spread = (lane == (SPAN - 1 - row % 32) * LINES + row // 32) & (row % 32 < SPAN)
    spread = spread.astype(f32).astype(bf16)
    row, lane = iota((6 * LINES, 384), 0) % LINES, iota((6 * LINES, 384), 1) % LINES
    levels_differ = row // WLAT != lane // WLAT
    rows_differ = (row % WLAT >= WLAT // 2) != (lane % WLAT >= WLAT // 2)
    slot = iota((16, 128), 1) // 32
    for (table_of, last), out_of in zip(tables, outs, strict=True):
        for head in range(6):
            stacked[head * 32 : head * 32 + SPAN, :] = table_of(head)
        picked = sum(dot_nt(pick, part) for part in two_parts(stacked[...]))
        picked = [picked[:, :128], jnp.concatenate([picked[:, 128:], jnp.zeros((LINES * 16, 64), f32)], axis=-1)]
        rolled = [[half] + [pltpu.roll(half, 32 * r, 1) for r in range(1, 4)] for half in picked]
        for head in range(6):
            for group in range(3):
                block = None
                for at in range(4):
                    key = group * 4 + at
                    piece = rolled[head // 4][(at - head) % 4][key * 16 : (key + 1) * 16]
                    block = piece if block is None else jnp.where(slot == at, piece, block)
                spread_from[head * LINES : (head + 1) * LINES, group * 128 : (group + 1) * 128] = block[:LINES]
        flat = sum(dot(part, spread) for part in two_parts(spread_from[...]))
        apart = levels_differ if last is None else levels_differ | (rows_differ & (last > 0))
        flat = jnp.where(apart, MASKED, flat)
        for o in range(WLON):
            start = (WLON - 1 - o) * LINES
            piece = flat[:, start : start + CELLS]
            for head in range(6):
                out_of(head, o * LINES, piece[head * LINES : (head + 1) * LINES])


def writer(out_ref, base):
    def write(head, at, piece):
        out_ref[base + head, at : at + LINES, :] = piece

    return write


def reader(table_ref, row, base):
    return lambda head: table_ref[row, base + head, :, 0, :]


def attend_group(q, k, v, bias, heads):
    queries, width = q.shape
    of_head = iota((queries, width), 1) // HD
    big = jnp.concatenate([jnp.where(of_head == h, q, 0.0) for h in range(heads)], axis=0)
    scores = dot_nt(big.astype(bf16), k) * HD ** (-0.5) + bias.reshape(heads * queries, CELLS)
    top = jnp.max(scores, axis=-1, keepdims=True)
    weights = jnp.exp(scores - top)
    total = jnp.sum(weights, axis=-1, keepdims=True)
    mixed = dot(weights.astype(bf16), v) * (1.0 / total)
    out = jnp.zeros((queries, width), f32)
    for h in range(heads):
        out = jnp.where(of_head == h, mixed[h * queries : (h + 1) * queries], out)
    return out


def tiles_of(rows, width):
    return ((-(-width // 128), rows, 128), f32)


def put(ref, at, rows, stride, values):
    width = values.shape[-1]
    for t in range(ref.shape[0]):
        piece = values[:, t * 128 : min((t + 1) * 128, width)]
        if piece.shape[-1] < 128:
            piece = jnp.concatenate([piece, jnp.zeros((rows, 128 - piece.shape[-1]), f32)], axis=-1)
        ref[t, pl.ds(at, rows, stride=stride), :] = piece


def get(ref, at, rows, stride, width):
    pieces = [ref[t, pl.ds(at, rows, stride=stride), :] for t in range(ref.shape[0])]
    return jnp.concatenate(pieces, axis=-1)[:, :width]


def pack_lines(first, second):
    return jnp.concatenate(first + [jnp.concatenate([second[i], second[3 + i]], axis=-1) for i in range(3)], axis=0)


def unpack_line(packed, i, size):
    first = packed[i * size : (i + 1) * size]
    at = (6 + i % 3) * size
    second = packed[at : at + size, i // 3 * 64 : i // 3 * 64 + 64]
    return jnp.concatenate([first, second], axis=-1)


def expand_first(fine_ref, bias0_ref, stacked, spread_from):
    expand_bias([(reader(fine_ref, 0, 0), None)], [writer(bias0_ref, 0)], stacked, spread_from)


def expand_others(last, fine_ref, coarse_ref, bias1_ref, bias2_ref, stacked, spread_from):
    tables = [(reader(fine_ref, 1, 0), last), (reader(coarse_ref, 0, 0), last), (reader(coarse_ref, 0, 6), last)]
    expand_bias(tables, [writer(bias1_ref, 0), writer(bias2_ref, 0), writer(bias2_ref, 6)], stacked, spread_from)


def prepare_kernel(
    flags_ref, fields_hbm, fine_hbm, coarse_hbm, qkv_hbm, proj_hbm, below_ref, corner_ref, own_ref, fine_ref,
    coarse_ref, qkv_ref, proj_ref, bias0_ref, bias1_ref, bias2_ref, line_ref, stacked, spread_from, sems,
):
    moves = [
        (fields_hbm.at[:, 0:3], own_ref.at[:, 0:3]),
        (fine_hbm, fine_ref),
        (coarse_hbm, coarse_ref),
        (fields_hbm.at[:, 3:12], own_ref.at[:, 3:12]),
        (qkv_hbm, qkv_ref),
        (proj_hbm, proj_ref),
    ]
    copies = [pltpu.make_async_copy(source, to, sems.at[i]) for i, (source, to) in enumerate(moves)]
    for copy in copies:
        copy.start()
    copies[0].wait()
    lines = [own_ref[z, a].astype(f32) for z in range(WZ) for a in range(3)]
    packed = pack_lines([line[:, :128] for line in lines], [line[:, 128:] for line in lines])
    for ref, start in ((below_ref, 0), (corner_ref, 6)):
        for i in range(9):
            line_ref[i * 18 : (i + 1) * 18, :] = packed[i * 24 + start : i * 24 + start + 18]
        ref[...] = line_ref[...].astype(bf16)

    for copy in copies[1:]:
        copy.wait()

    @pl.when(flags_ref[1] > 0)
    def _():
        expand_first(fine_ref, bias0_ref, stacked, spread_from)
        expand_others(flags_ref[0], fine_ref, coarse_ref, bias1_ref, bias2_ref, stacked, spread_from)


def other_bias_kernel(
    flags_ref, fine_ref, coarse_ref, early1_ref, early2_ref, after_ref, bias1_ref, bias2_ref, stacked, spread_from
):
    @pl.when(flags_ref[1] > 0)
    def _():
        bias1_ref[...] = early1_ref[...]
        bias2_ref[...] = early2_ref[...]

    @pl.when(flags_ref[1] == 0)
    def _():
        expand_others(flags_ref[0], fine_ref, coarse_ref, bias1_ref, bias2_ref, stacked, spread_from)


def attend_fine(x_ref, bias_ref, qkv_ref, proj_ref):
    normed = normalise(get(x_ref, 72, 432, 1, 192))
    q = dot(normed, qkv_ref[:, 0:192]).astype(bf16).astype(f32)
    k = dot(normed, qkv_ref[:, 192:384]).astype(bf16)
    v = dot(normed, qkv_ref[:, 384:576]).astype(bf16)
    left, right = [], []
    for window, start, stop in ((0, 72, 144), (1, 0, 144), (2, 0, 72)):
        at = window * CELLS
        q_rows = q[at + start : at + stop]
        k_rows, v_rows = k[at : at + CELLS], v[at : at + CELLS]
        bias = bias_ref[:, start:stop, :]
        left.append(attend_group(q_rows[:, :128], k_rows[:, :128], v_rows[:, :128], bias[:4], 4))
        right.append(attend_group(q_rows[:, 128:], k_rows[:, 128:], v_rows[:, 128:], bias[4:], 2))
    left = jnp.concatenate(left, axis=0).astype(bf16)
    right = jnp.concatenate(right, axis=0).astype(bf16)
    product = dot(left, proj_ref[0:128, :]) + dot(right, proj_ref[128:192, :])
    return (get(x_ref, 144, 288, 1, 192) + product).astype(bf16)


def first_rows_kernel(
    flags_ref, left_ref, own_ref, fine_ref, early0_ref, qkv_ref, proj_ref,
    out_ref, send_ref, bias0_ref, x_ref, a_ref, stacked, spread_from,
):
    @pl.when(flags_ref[1] == 0)
    def _():
        expand_first(fine_ref, bias0_ref, stacked, spread_from)

    @pl.when(flags_ref[1] > 0)
    def _():
        bias0_ref[...] = early0_ref[...]

    for z in range(WZ):
        for a in range(WLAT):
            put(x_ref, z * WLAT + a, 24, LINES, left_ref[z, 3 + a].astype(f32))
            put(x_ref, 288 + z * WLAT + a, 24, LINES, own_ref[z, 3 + a].astype(f32))
    attended = attend_fine(x_ref, bias0_ref, qkv_ref, proj_ref)
    out_ref[...] = attended
    put(a_ref, 0, 288, 1, attended.astype(f32))
    lines = [a_ref[t, pl.ds(z * WLAT + a, 24, stride=LINES), :] for t in range(2) for z in range(WZ) for a in range(3)]
    send_ref[...] = pack_lines(lines[:6], [line[:, :64] for line in lines[6:]]).astype(bf16)


def second_rows_kernel(
    left_ref, own_ref, corner_ref, below_ref, first_ref, bias1_ref, qkv_ref, proj_ref, up_ref, down_ref,
    out_ref, x_ref, a_ref, w_ref,
):
    below, corner = below_ref[...].astype(f32), corner_ref[...].astype(f32)
    for z in range(WZ):
        for a in range(WLAT):
            at = z * WLAT + a
            if a < 3:
                put(x_ref, at, 24, LINES, left_ref[z, 9 + a].astype(f32))
                put(x_ref, 288 + at, 24, LINES, own_ref[z, 9 + a].astype(f32))
            else:
                put(x_ref, 72 + at, 18, LINES, unpack_line(corner, z * 3 + a - 3, 18))
                put(x_ref, 288 + at, 18, LINES, unpack_line(below, z * 3 + a - 3, 18))
    put(a_ref, 0, 288, 1, first_ref[...].astype(f32))
    put(a_ref, 288, 288, 1, attend_fine(x_ref, bias1_ref, qkv_ref, proj_ref).astype(f32))
    for t in range(2):
        for rho in range(3, 12):
            for z in range(WZ):
                at = rho // WLAT * 288 + z * WLAT + rho % WLAT
                to = ((rho - 3) * WZ + z) * 24
                w_ref[t, to : to + 24, :] = a_ref[t, pl.ds(at, 24, stride=LINES), :]
    for i in range(3):
        x = get(w_ref, i * 144, 144, 1, 192)
        out_ref[i * 144 : (i + 1) * 144, :] = fine_feed_forward(x, up_ref, down_ref).astype(bf16)


def coarse_kernel(
    y_ref, got_ref, fine_up_ref, fine_down_ref, merge_ref, bias_ref, qkv_ref, proj_ref, up_ref, down_ref,
    keep_ref, lower_ref, corner_ref, left_ref, w_ref, p_ref, o_ref,
):
    got = got_ref[...].astype(f32)
    got = jnp.concatenate([unpack_line(got, z * 3 + a, 24) for a in range(3) for z in range(WZ)], axis=0)
    put(w_ref, 0, 432, 1, y_ref[...].astype(f32))
    put(w_ref, 432, 144, 1, fine_feed_forward(got, fine_up_ref, fine_down_ref))
    parts = []
    for pa in range(2):
        for pb in range(2):
            for t in range(2):
                for z in range(WZ):
                    for i in range(WLAT):
                        at = ((2 * i + pa) * WZ + z) * 24 + pb
                        line = w_ref[t, pl.ds(at, WLON, stride=2), :]
                        p_ref[t, pl.ds(len(parts) * CELLS + z * WLAT + i, WLON, stride=LINES), :] = line
            parts.append(get(p_ref, len(parts) * CELLS, CELLS, 1, 192))
    mean = sum(jnp.sum(part, axis=-1, keepdims=True) for part in parts) * (1.0 / 768)
    parts = [part - mean for part in parts]
    variance = sum(jnp.sum(part * part, axis=-1, keepdims=True) for part in parts) * (1.0 / 768)
    scale = lax.rsqrt(variance + EPSILON)
    merged = sum(
        dot((part * scale).astype(bf16), merge_ref[i * 192 : (i + 1) * 192, :]) for i, part in enumerate(parts)
    )
    merged = merged.astype(bf16).astype(f32)
    normed = normalise(merged)
    qkv = dot(normed, qkv_ref[...]).astype(bf16)
    product = merged
    for g in range(3):
        q = qkv[:, g * 128 : (g + 1) * 128].astype(f32)
        k = qkv[:, 384 + g * 128 : 384 + (g + 1) * 128]
        v = qkv[:, 768 + g * 128 : 768 + (g + 1) * 128]
        mixed = attend_group(q, k, v, bias_ref[g * 4 : (g + 1) * 4], 4)
        product = product + dot(mixed.astype(bf16), proj_ref[g * 128 : (g + 1) * 128, :])
    attended = product.astype(bf16).astype(f32)
    put(o_ref, 0, CELLS, 1, feed_forward(attended, up_ref, down_ref))
    for i in range(3):
        for j in range(WLON):
            for ref, row in ((left_ref, i), (corner_ref, 3 + i)) if j < 6 else ((keep_ref, i), (lower_ref, 3 + i)):
                ref[i, j % 6] = get(o_ref, j * LINES + row, WZ, WLAT, 384).astype(bf16)


def call(kernel, outs, scratch, operands, flops, smem=0):
    specs = [pl.BlockSpec(memory_space=pltpu.SMEM)] * smem
    specs += [pl.BlockSpec(memory_space=pltpu.VMEM)] * (len(operands) - smem)
    return pl.pallas_call(
        kernel,
        out_shape=[jax.ShapeDtypeStruct(shape, dtype) for shape, dtype in outs],
        in_specs=specs,
        out_specs=[pl.BlockSpec(memory_space=pltpu.VMEM)] * len(outs),
        scratch_shapes=[pltpu.VMEM(shape, dtype) for shape, dtype in scratch],
        compiler_params=pltpu.CompilerParams(vmem_limit_bytes=VMEM_LIMIT),
        cost_estimate=pl.CostEstimate(
            flops=flops,
            bytes_accessed=sum(a.size * a.dtype.itemsize for a in operands),
            transcendentals=0,
        ),
    )(*operands)


def body(
    fields,
    fine_bias,
    fine_qkv,
    fine_proj,
    fine_up,
    fine_down,
    merge_weight,
    coarse_bias,
    coarse_qkv,
    coarse_proj,
    coarse_up,
    coarse_down,
):
    lat, lats = lax.axis_index("lat"), lax.axis_size("lat")
    lon, lons = lax.axis_index("lon"), lax.axis_size("lon")
    flags = jnp.stack([lat == lats - 1, (lat < lats // 2) & (lon < lons // 2)]).astype(jnp.int32)
    fine_tables = fine_bias.transpose(0, 2, 3, 1, 4)
    coarse_tables = coarse_bias.transpose(0, 2, 3, 1, 4)
    fine_down = fine_down.T
    expansion = [((6 * 32, CELLS), f32), ((6 * LINES, LINES * 32), f32)]
    biases = [((6, CELLS, CELLS), f32), ((12, CELLS, CELLS), f32)]
    left = from_behind(fields, 1, 0)
    sources = [fields, fine_tables, coarse_tables, fine_qkv, fine_proj]
    hbm, vmem, smem = (pl.BlockSpec(memory_space=space) for space in (pltpu.HBM, pltpu.VMEM, pltpu.SMEM))
    below, corner, own, fine_tables, coarse_tables, fine_qkv, fine_proj, bias0, bias1, bias2 = pl.pallas_call(
        prepare_kernel,
        out_shape=[jax.ShapeDtypeStruct((162, 128), bf16)] * 2
        + [jax.ShapeDtypeStruct(source.shape, source.dtype) for source in sources]
        + [jax.ShapeDtypeStruct(shape, dtype) for shape, dtype in [((6, CELLS, CELLS), f32)] + biases],
        in_specs=[smem] + [hbm] * 5,
        out_specs=[vmem] * 10,
        scratch_shapes=[pltpu.VMEM((162, 128), f32)]
        + [pltpu.VMEM(shape, dtype) for shape, dtype in expansion]
        + [pltpu.SemaphoreType.DMA((6,))],
        compiler_params=pltpu.CompilerParams(vmem_limit_bytes=VMEM_LIMIT),
    )(flags, *(pltpu.with_memory_space_constraint(source, pltpu.HBM) for source in sources))
    corner = from_behind(corner, 1, -1)
    below = from_behind(below, 0, -1)
    first, edge = call(
        first_rows_kernel,
        [((288, 192), bf16), ((216, 128), bf16)],
        [((6, CELLS, CELLS), f32), tiles_of(576, 192), tiles_of(288, 192)] + expansion,
        [flags, left, own, fine_tables, bias0, fine_qkv, fine_proj],
        1_000_000_000,
        smem=1,
    )
    got = from_behind(edge, 0, -1)
    bias1, bias2 = call(
        other_bias_kernel,
        biases,
        expansion,
        [flags, fine_tables, coarse_tables, bias1, bias2, first],
        2_000_000_000,
        smem=1,
    )
    (finished,) = call(
        second_rows_kernel,
        [((432, 192), bf16)],
        [tiles_of(576, 192), tiles_of(576, 192), tiles_of(432, 192)],
        [left, own, corner, below, first, bias1, fine_qkv, fine_proj, fine_up, fine_down],
        3_000_000_000,
    )
    quarter = ((3, 6, WZ, 384), bf16)
    keep, lower, far_corner, upper_left = call(
        coarse_kernel,
        [quarter] * 4,
        [tiles_of(576, 192), tiles_of(576, 192), tiles_of(CELLS, 384)],
        [finished, got, fine_up, fine_down, merge_weight, bias2, coarse_qkv, coarse_proj, coarse_up, coarse_down],
        4_000_000_000,
    )
    above = from_behind(lower, 0, 1)
    corner = from_behind(far_corner, -1, 1)
    right = from_behind(upper_left, -1, 0)
    rows = [jnp.concatenate([above, corner], axis=1), jnp.concatenate([keep, right], axis=1)]
    return jnp.concatenate(rows, axis=0).transpose(2, 0, 1, 3)


def solution(mesh):
    return jax.shard_map(
        body,
        mesh=mesh,
        in_specs=(
            P(None, "lat", "lon", None),
            P("lat", None, None, None, None),
            P(),
            P(),
            P(),
            P(),
            P(),
            P("lat", None, None, None, None),
            P(),
            P(),
            P(),
            P(),
        ),
        out_specs=P(None, "lat", "lon", None),
        check_vma=False,
    )
```

```python
import functools

import jax
import jax.numpy as jnp
from jax import lax
from jax.experimental import pallas as pl
from jax.experimental.pallas import tpu as pltpu
from jax.sharding import PartitionSpec as P

HD = 32
WZ = 2
WLAT = 6
WLON = 12
CELLS = WZ * WLAT * WLON
LINES = WZ * WLAT
SPAN = 2 * WLON - 1
EPSILON = 1e-05
MASKED = -1e30
VMEM_LIMIT = 40 * 1024 * 1024

f32 = jnp.float32
bf16 = jnp.bfloat16


def from_behind(shard, lon, lat):
    lons, lats = lax.axis_size("lon"), lax.axis_size("lat")
    pairs = [
        (o * lats + a, (o + lon) % lons * lats + (a + lat) % lats) for o in range(lons) for a in range(lats)
    ]
    return lax.ppermute(shard, ("lon", "lat"), pairs)


def normalise(values):
    centred = values - jnp.mean(values, axis=-1, keepdims=True)
    variance = jnp.mean(centred * centred, axis=-1, keepdims=True)
    return (centred * lax.rsqrt(variance + EPSILON)).astype(bf16)


def dot(a, b):
    return jnp.dot(a, b, preferred_element_type=f32)


def dot_nt(a, b):
    return lax.dot_general(a, b, (((1,), (1,)), ((), ())), preferred_element_type=f32)


def gelu(x):
    return 0.5 * x * (1.0 + lax.erf(x * (2.0**-0.5)))


def feed_forward(x, up_ref, down_ref):
    hidden = gelu(dot(normalise(x), up_ref[...])).astype(bf16)
    return (x + dot(hidden, down_ref[...])).astype(bf16).astype(f32)


def fine_feed_forward(x, up_ref, down_ref):
    hidden = gelu(dot(normalise(x), up_ref[...])).astype(bf16)
    return (x + dot_nt(hidden, down_ref[...])).astype(bf16).astype(f32)


def two_parts(x):
    high = x.astype(bf16)
    return high, (x - high.astype(f32)).astype(bf16)


def iota(shape, axis):
    return lax.broadcasted_iota(jnp.int32, shape, axis)


def expand_bias(tables, outs, stacked, spread_from):
    stacked[...] = jnp.zeros_like(stacked)
    row = iota((LINES * 16, CELLS), 0)
    key, query = row // 16, row % 16
    z_key, z_query = 1 - key // WLAT, 1 - query // WLAT
    column = ((z_query * WZ + z_key) * WLAT + query % WLAT) * WLAT + key % WLAT
    pick = ((iota((LINES * 16, CELLS), 1) == column) & (query < LINES)).astype(f32).astype(bf16)
    row = iota((LINES * 32, 384), 0)
    lane = iota((LINES * 32, 384), 1)
    spread = (lane == (SPAN - 1 - row % 32) * LINES + row // 32) & (row % 32 < SPAN)
    spread = spread.astype(f32).astype(bf16)
    row, lane = iota((6 * LINES, 384), 0) % LINES, iota((6 * LINES, 384), 1) % LINES
    levels_differ = row // WLAT != lane // WLAT
    rows_differ = (row % WLAT >= WLAT // 2) != (lane % WLAT >= WLAT // 2)
    slot, kept = iota((16, 128), 1) // 32, iota((6 * LINES, 128), 1)
    for (table_of, last), out_of in zip(tables, outs, strict=True):
        for head in range(6):
            stacked[head * 32 : head * 32 + SPAN, :] = table_of(head)
        picked = sum(dot_nt(pick, part) for part in two_parts(stacked[...]))
        picked = [picked[:, :128], jnp.concatenate([picked[:, 128:], jnp.zeros((LINES * 16, 64), f32)], axis=-1)]
        rolled = [[half] + [pltpu.roll(half, 32 * r, 1) for r in range(1, 4)] for half in picked]
        for head in range(6):
            for group in range(3):
                block = None
                for at in range(4):
                    key = group * 4 + at
                    piece = rolled[head // 4][(at - head) % 4][key * 16 : (key + 1) * 16]
                    block = piece if block is None else jnp.where(slot == at, piece, block)
                spread_from[head * LINES : (head + 1) * LINES, group * 128 : (group + 1) * 128] = block[:LINES]
        flat = sum(dot(part, spread) for part in two_parts(spread_from[...]))
        apart = levels_differ if last is None else levels_differ | (rows_differ & last)
        flat = jnp.where(apart, MASKED, flat)
        for o in range(WLON):
            start = (WLON - 1 - o) * LINES
            tile, shift = divmod(start, 128)
            parts = [flat[:, t * 128 : (t + 1) * 128] for t in range(tile, min(tile + 3, 3))]
            if shift:
                parts = [pltpu.roll(part, 128 - shift, 1) for part in parts]
                parts = [jnp.where(kept < 128 - shift, a, b) for a, b in zip(parts, parts[1:] + parts[-1:], strict=True)]
            piece = jnp.concatenate([parts[0], parts[1][:, : CELLS - 128]], axis=-1)
            for head in range(6):
                out_of(head, o * LINES, piece[head * LINES : (head + 1) * LINES])


def writer(out_ref, base):
    def write(head, at, piece):
        out_ref[base + head, at : at + LINES, :] = piece

    return write


def reader(table_ref, row, base):
    return lambda head: table_ref[row, base + head, :, 0, :]


def attend_group(q, k, v, bias, heads):
    queries, width = q.shape
    of_head = iota((queries, width), 1) // HD
    big = jnp.concatenate([jnp.where(of_head == h, q, 0.0) for h in range(heads)], axis=0)
    scores = dot_nt(big.astype(bf16), k) * HD ** (-0.5) + bias.reshape(heads * queries, CELLS)
    top = jnp.max(scores, axis=-1, keepdims=True)
    weights = jnp.exp(scores - top)
    total = jnp.sum(weights, axis=-1, keepdims=True)
    mixed = dot(weights.astype(bf16), v) * (1.0 / total)
    out = jnp.zeros((queries, width), f32)
    for h in range(heads):
        out = jnp.where(of_head == h, mixed[h * queries : (h + 1) * queries], out)
    return out


def tiles_of(rows, width):
    return ((-(-width // 128), rows, 128), f32)


def put(ref, at, rows, stride, values):
    width = values.shape[-1]
    for t in range(ref.shape[0]):
        piece = values[:, t * 128 : min((t + 1) * 128, width)]
        if piece.shape[-1] < 128:
            piece = jnp.concatenate([piece, jnp.zeros((rows, 128 - piece.shape[-1]), f32)], axis=-1)
        ref[t, pl.ds(at, rows, stride=stride), :] = piece


def get(ref, at, rows, stride, width):
    pieces = [ref[t, pl.ds(at, rows, stride=stride), :] for t in range(ref.shape[0])]
    return jnp.concatenate(pieces, axis=-1)[:, :width]


def pack_lines(first, second):
    return jnp.concatenate(first + [jnp.concatenate([second[i], second[3 + i]], axis=-1) for i in range(3)], axis=0)


def unpack_line(packed, i, size):
    first = packed[i * size : (i + 1) * size]
    at = (6 + i % 3) * size
    second = packed[at : at + size, i // 3 * 64 : i // 3 * 64 + 64]
    return jnp.concatenate([first, second], axis=-1)


def expand_first(fine_ref, bias0_ref, stacked, spread_from):
    expand_bias([(reader(fine_ref, 0, 0), None)], [writer(bias0_ref, 0)], stacked, spread_from)


def expand_others(last, fine_ref, coarse_ref, bias1_ref, bias2_ref, stacked, spread_from):
    tables = [(reader(fine_ref, 1, 0), last), (reader(coarse_ref, 0, 0), last), (reader(coarse_ref, 0, 6), last)]
    expand_bias(tables, [writer(bias1_ref, 0), writer(bias2_ref, 0), writer(bias2_ref, 6)], stacked, spread_from)


def place():
    lat, lats = lax.axis_index("lat"), lax.axis_size("lat")
    lon, lons = lax.axis_index("lon"), lax.axis_size("lon")
    return lat == lats - 1, (lat < lats // 2) & (lon < lons // 2)


def prepare_kernel(
    fields_hbm, fine_hbm, coarse_hbm, qkv_hbm, proj_hbm, below_ref, corner_ref, own_ref, fine_ref,
    coarse_ref, qkv_ref, proj_ref, bias0_ref, bias1_ref, bias2_ref, line_ref, stacked, spread_from, sems,
):
    last, early = place()
    moves = [
        (fields_hbm.at[:, 0:3], own_ref.at[:, 0:3]),
        (fine_hbm, fine_ref),
        (coarse_hbm, coarse_ref),
        (fields_hbm.at[:, 3:12], own_ref.at[:, 3:12]),
        (qkv_hbm, qkv_ref),
        (proj_hbm, proj_ref),
    ]
    copies = [pltpu.make_async_copy(source, to, sems.at[i]) for i, (source, to) in enumerate(moves)]
    for copy in copies:
        copy.start()
    copies[0].wait()
    lines = [own_ref[z, a].astype(f32) for z in range(WZ) for a in range(3)]
    packed = pack_lines([line[:, :128] for line in lines], [line[:, 128:] for line in lines])
    for ref, start in ((below_ref, 0), (corner_ref, 6)):
        for i in range(9):
            line_ref[i * 18 : (i + 1) * 18, :] = packed[i * 24 + start : i * 24 + start + 18]
        ref[...] = line_ref[...].astype(bf16)

    for copy in copies[1:]:
        copy.wait()

    @pl.when(early)
    def _():
        expand_first(fine_ref, bias0_ref, stacked, spread_from)
        expand_others(last, fine_ref, coarse_ref, bias1_ref, bias2_ref, stacked, spread_from)


def other_bias_kernel(
    fine_ref, coarse_ref, early1_ref, early2_ref, after_ref, bias1_ref, bias2_ref, stacked, spread_from
):
    last, early = place()

    @pl.when(early)
    def _():
        bias1_ref[...] = early1_ref[...]
        bias2_ref[...] = early2_ref[...]

    @pl.when(jnp.logical_not(early))
    def _():
        expand_others(last, fine_ref, coarse_ref, bias1_ref, bias2_ref, stacked, spread_from)


def attend_fine(x_ref, bias_ref, qkv_ref, proj_ref):
    normed = normalise(get(x_ref, 72, 432, 1, 192))
    q = dot(normed, qkv_ref[:, 0:192]).astype(bf16).astype(f32)
    k = dot(normed, qkv_ref[:, 192:384]).astype(bf16)
    v = dot(normed, qkv_ref[:, 384:576]).astype(bf16)
    left, right = [], []
    for window, start, stop in ((0, 72, 144), (1, 0, 144), (2, 0, 72)):
        at = window * CELLS
        q_rows = q[at + start : at + stop]
        k_rows, v_rows = k[at : at + CELLS], v[at : at + CELLS]
        bias = bias_ref[:, start:stop, :]
        left.append(attend_group(q_rows[:, :128], k_rows[:, :128], v_rows[:, :128], bias[:4], 4))
        right.append(attend_group(q_rows[:, 128:], k_rows[:, 128:], v_rows[:, 128:], bias[4:], 2))
    left = jnp.concatenate(left, axis=0).astype(bf16)
    right = jnp.concatenate(right, axis=0).astype(bf16)
    product = dot(left, proj_ref[0:128, :]) + dot(right, proj_ref[128:192, :])
    return (get(x_ref, 144, 288, 1, 192) + product).astype(bf16)


def first_rows_kernel(
    left_ref, own_ref, fine_ref, early0_ref, qkv_ref, proj_ref,
    out_ref, send_ref, bias0_ref, x_ref, a_ref, stacked, spread_from,
):
    _, early = place()

    @pl.when(jnp.logical_not(early))
    def _():
        expand_first(fine_ref, bias0_ref, stacked, spread_from)

    @pl.when(early)
    def _():
        bias0_ref[...] = early0_ref[...]

    for z in range(WZ):
        for a in range(WLAT):
            put(x_ref, z * WLAT + a, 24, LINES, left_ref[z, 3 + a].astype(f32))
            put(x_ref, 288 + z * WLAT + a, 24, LINES, own_ref[z, 3 + a].astype(f32))
    attended = attend_fine(x_ref, bias0_ref, qkv_ref, proj_ref)
    out_ref[...] = attended
    put(a_ref, 0, 288, 1, attended.astype(f32))
    lines = [a_ref[t, pl.ds(z * WLAT + a, 24, stride=LINES), :] for t in range(2) for z in range(WZ) for a in range(3)]
    send_ref[...] = pack_lines(lines[:6], [line[:, :64] for line in lines[6:]]).astype(bf16)


def second_rows_kernel(
    left_ref, own_ref, corner_ref, below_ref, first_ref, bias1_ref, qkv_ref, proj_ref, up_ref, down_ref,
    out_ref, x_ref, a_ref, w_ref,
):
    below, corner = below_ref[...].astype(f32), corner_ref[...].astype(f32)
    for z in range(WZ):
        for a in range(WLAT):
            at = z * WLAT + a
            if a < 3:
                put(x_ref, at, 24, LINES, left_ref[z, 9 + a].astype(f32))
                put(x_ref, 288 + at, 24, LINES, own_ref[z, 9 + a].astype(f32))
            else:
                put(x_ref, 72 + at, 18, LINES, unpack_line(corner, z * 3 + a - 3, 18))
                put(x_ref, 288 + at, 18, LINES, unpack_line(below, z * 3 + a - 3, 18))
    put(a_ref, 0, 288, 1, first_ref[...].astype(f32))
    put(a_ref, 288, 288, 1, attend_fine(x_ref, bias1_ref, qkv_ref, proj_ref).astype(f32))
    for t in range(2):
        for rho in range(3, 12):
            for z in range(WZ):
                at = rho // WLAT * 288 + z * WLAT + rho % WLAT
                to = ((rho - 3) * WZ + z) * 24
                w_ref[t, to : to + 24, :] = a_ref[t, pl.ds(at, 24, stride=LINES), :]
    for i in range(3):
        x = get(w_ref, i * 144, 144, 1, 192)
        out_ref[i * 144 : (i + 1) * 144, :] = fine_feed_forward(x, up_ref, down_ref).astype(bf16)


def coarse_kernel(
    y_ref, got_ref, fine_up_ref, fine_down_ref, merge_ref, bias_ref, qkv_ref, proj_ref, up_ref, down_ref,
    keep_ref, lower_ref, corner_ref, left_ref, w_ref, p_ref, o_ref,
):
    got = got_ref[...].astype(f32)
    got = jnp.concatenate([unpack_line(got, z * 3 + a, 24) for a in range(3) for z in range(WZ)], axis=0)
    put(w_ref, 0, 432, 1, y_ref[...].astype(f32))
    put(w_ref, 432, 144, 1, fine_feed_forward(got, fine_up_ref, fine_down_ref))
    parts = []
    for pa in range(2):
        for pb in range(2):
            for t in range(2):
                for z in range(WZ):
                    for i in range(WLAT):
                        at = ((2 * i + pa) * WZ + z) * 24 + pb
                        line = w_ref[t, pl.ds(at, WLON, stride=2), :]
                        p_ref[t, pl.ds(len(parts) * CELLS + z * WLAT + i, WLON, stride=LINES), :] = line
            parts.append(get(p_ref, len(parts) * CELLS, CELLS, 1, 192))
    mean = sum(jnp.sum(part, axis=-1, keepdims=True) for part in parts) * (1.0 / 768)
    parts = [part - mean for part in parts]
    variance = sum(jnp.sum(part * part, axis=-1, keepdims=True) for part in parts) * (1.0 / 768)
    scale = lax.rsqrt(variance + EPSILON)
    merged = sum(
        dot((part * scale).astype(bf16), merge_ref[i * 192 : (i + 1) * 192, :]) for i, part in enumerate(parts)
    )
    merged = merged.astype(bf16).astype(f32)
    normed = normalise(merged)
    qkv = dot(normed, qkv_ref[...]).astype(bf16)
    product = merged
    for g in range(3):
        q = qkv[:, g * 128 : (g + 1) * 128].astype(f32)
        k = qkv[:, 384 + g * 128 : 384 + (g + 1) * 128]
        v = qkv[:, 768 + g * 128 : 768 + (g + 1) * 128]
        mixed = attend_group(q, k, v, bias_ref[g * 4 : (g + 1) * 4], 4)
        product = product + dot(mixed.astype(bf16), proj_ref[g * 128 : (g + 1) * 128, :])
    attended = product.astype(bf16).astype(f32)
    put(o_ref, 0, CELLS, 1, feed_forward(attended, up_ref, down_ref))
    for i in range(3):
        for j in range(WLON):
            for ref, row in ((left_ref, i), (corner_ref, 3 + i)) if j < 6 else ((keep_ref, i), (lower_ref, 3 + i)):
                ref[i, j % 6] = get(o_ref, j * LINES + row, WZ, WLAT, 384).astype(bf16)


def call(kernel, outs, scratch, operands, flops):
    specs = [pl.BlockSpec(memory_space=pltpu.VMEM)] * len(operands)
    return pl.pallas_call(
        kernel,
        out_shape=[jax.ShapeDtypeStruct(shape, dtype) for shape, dtype in outs],
        in_specs=specs,
        out_specs=[pl.BlockSpec(memory_space=pltpu.VMEM)] * len(outs),
        scratch_shapes=[pltpu.VMEM(shape, dtype) for shape, dtype in scratch],
        compiler_params=pltpu.CompilerParams(vmem_limit_bytes=VMEM_LIMIT),
        cost_estimate=pl.CostEstimate(
            flops=flops,
            bytes_accessed=sum(a.size * a.dtype.itemsize for a in operands),
            transcendentals=0,
        ),
    )(*operands)


def body(
    fields,
    fine_bias,
    fine_qkv,
    fine_proj,
    fine_up,
    fine_down,
    merge_weight,
    coarse_bias,
    coarse_qkv,
    coarse_proj,
    coarse_up,
    coarse_down,
):
    fine_tables = fine_bias.transpose(0, 2, 3, 1, 4)
    coarse_tables = coarse_bias.transpose(0, 2, 3, 1, 4)
    fine_down = fine_down.T
    expansion = [((6 * 32, CELLS), f32), ((6 * LINES, LINES * 32), f32)]
    biases = [((6, CELLS, CELLS), f32), ((12, CELLS, CELLS), f32)]
    left = from_behind(fields, 1, 0)
    sources = [fields, fine_tables, coarse_tables, fine_qkv, fine_proj]
    hbm, vmem = (pl.BlockSpec(memory_space=space) for space in (pltpu.HBM, pltpu.VMEM))
    below, corner, own, fine_tables, coarse_tables, fine_qkv, fine_proj, bias0, bias1, bias2 = pl.pallas_call(
        prepare_kernel,
        out_shape=[jax.ShapeDtypeStruct((162, 128), bf16)] * 2
        + [jax.ShapeDtypeStruct(source.shape, source.dtype) for source in sources]
        + [jax.ShapeDtypeStruct(shape, dtype) for shape, dtype in [((6, CELLS, CELLS), f32)] + biases],
        in_specs=[hbm] * 5,
        out_specs=[vmem] * 10,
        scratch_shapes=[pltpu.VMEM((162, 128), f32)]
        + [pltpu.VMEM(shape, dtype) for shape, dtype in expansion]
        + [pltpu.SemaphoreType.DMA((6,))],
        compiler_params=pltpu.CompilerParams(vmem_limit_bytes=VMEM_LIMIT),
    )(*(pltpu.with_memory_space_constraint(source, pltpu.HBM) for source in sources))
    corner = from_behind(corner, 1, -1)
    below = from_behind(below, 0, -1)
    first, edge = call(
        first_rows_kernel,
        [((288, 192), bf16), ((216, 128), bf16)],
        [((6, CELLS, CELLS), f32), tiles_of(576, 192), tiles_of(288, 192)] + expansion,
        [left, own, fine_tables, bias0, fine_qkv, fine_proj],
        1_000_000_000,
    )
    got = from_behind(edge, 0, -1)
    bias1, bias2 = call(
        other_bias_kernel,
        biases,
        expansion,
        [fine_tables, coarse_tables, bias1, bias2, first],
        2_000_000_000,
    )
    (finished,) = call(
        second_rows_kernel,
        [((432, 192), bf16)],
        [tiles_of(576, 192), tiles_of(576, 192), tiles_of(432, 192)],
        [left, own, corner, below, first, bias1, fine_qkv, fine_proj, fine_up, fine_down],
        3_000_000_000,
    )
    quarter = ((3, 6, WZ, 384), bf16)
    keep, lower, far_corner, upper_left = call(
        coarse_kernel,
        [quarter] * 4,
        [tiles_of(576, 192), tiles_of(576, 192), tiles_of(CELLS, 384)],
        [finished, got, fine_up, fine_down, merge_weight, bias2, coarse_qkv, coarse_proj, coarse_up, coarse_down],
        4_000_000_000,
    )
    above = from_behind(lower, 0, 1)
    corner = from_behind(far_corner, -1, 1)
    right = from_behind(upper_left, -1, 0)
    rows = [jnp.concatenate([above, corner], axis=1), jnp.concatenate([keep, right], axis=1)]
    return jnp.concatenate(rows, axis=0).transpose(2, 0, 1, 3)


def solution(mesh):
    return jax.shard_map(
        body,
        mesh=mesh,
        in_specs=(
            P(None, "lat", "lon", None),
            P("lat", None, None, None, None),
            P(),
            P(),
            P(),
            P(),
            P(),
            P("lat", None, None, None, None),
            P(),
            P(),
            P(),
            P(),
        ),
        out_specs=P(None, "lat", "lon", None),
        check_vma=False,
    )
```

```python
import functools

import jax
import jax.numpy as jnp
from jax import lax
from jax.experimental import pallas as pl
from jax.experimental.pallas import tpu as pltpu
from jax.sharding import PartitionSpec as P

HD = 32
WZ = 2
WLAT = 6
WLON = 12
CELLS = WZ * WLAT * WLON
LINES = WZ * WLAT
SPAN = 2 * WLON - 1
EPSILON = 1e-05
MASKED = -1e30
VMEM_LIMIT = 40 * 1024 * 1024

f32 = jnp.float32
bf16 = jnp.bfloat16


def from_behind(shard, lon, lat, bands=lambda a: True):
    lons, lats = lax.axis_size("lon"), lax.axis_size("lat")
    pairs = [
        (o * lats + a, (o + lon) % lons * lats + (a + lat) % lats)
        for o in range(lons)
        for a in range(lats)
        if bands(a)
    ]
    return lax.ppermute(shard, ("lon", "lat"), pairs)


def normalise(values):
    centred = values - jnp.mean(values, axis=-1, keepdims=True)
    variance = jnp.mean(centred * centred, axis=-1, keepdims=True)
    return (centred * lax.rsqrt(variance + EPSILON)).astype(bf16)


def dot(a, b):
    return jnp.dot(a, b, preferred_element_type=f32)


def dot_nt(a, b):
    return lax.dot_general(a, b, (((1,), (1,)), ((), ())), preferred_element_type=f32)


def gelu(x):
    return 0.5 * x * (1.0 + lax.erf(x * (2.0**-0.5)))


def feed_forward(x, up_ref, down_ref):
    hidden = gelu(dot(normalise(x), up_ref[...])).astype(bf16)
    return (x + dot(hidden, down_ref[...])).astype(bf16).astype(f32)


def fine_feed_forward(x, up_ref, down_ref):
    hidden = gelu(dot(normalise(x), up_ref[...])).astype(bf16)
    return (x + dot_nt(hidden, down_ref[...])).astype(bf16).astype(f32)


def two_parts(x):
    high = x.astype(bf16)
    return high, (x - high.astype(f32)).astype(bf16)


def iota(shape, axis):
    return lax.broadcasted_iota(jnp.int32, shape, axis)


def expand_bias(tables, outs, stacked, spread_from):
    stacked[...] = jnp.zeros_like(stacked)
    row = iota((LINES * 16, CELLS), 0)
    key, query = row // 16, row % 16
    z_key, z_query = 1 - key // WLAT, 1 - query // WLAT
    column = ((z_query * WZ + z_key) * WLAT + query % WLAT) * WLAT + key % WLAT
    pick = ((iota((LINES * 16, CELLS), 1) == column) & (query < LINES)).astype(f32).astype(bf16)
    row = iota((LINES * 32, 384), 0)
    lane = iota((LINES * 32, 384), 1)
    spread = (lane == (SPAN - 1 - row % 32) * LINES + row // 32) & (row % 32 < SPAN)
    spread = spread.astype(f32).astype(bf16)
    row, lane = iota((6 * LINES, 384), 0) % LINES, iota((6 * LINES, 384), 1) % LINES
    levels_differ = row // WLAT != lane // WLAT
    rows_differ = (row % WLAT >= WLAT // 2) != (lane % WLAT >= WLAT // 2)
    slot, kept = iota((16, 128), 1) // 32, iota((6 * LINES, 128), 1)
    for (table_of, last), out_of in zip(tables, outs, strict=True):
        for head in range(6):
            stacked[head * 32 : head * 32 + SPAN, :] = table_of(head)
        picked = sum(dot_nt(pick, part) for part in two_parts(stacked[...]))
        picked = [picked[:, :128], jnp.concatenate([picked[:, 128:], jnp.zeros((LINES * 16, 64), f32)], axis=-1)]
        rolled = [[half] + [pltpu.roll(half, 32 * r, 1) for r in range(1, 4)] for half in picked]
        for head in range(6):
            for group in range(3):
                block = None
                for at in range(4):
                    key = group * 4 + at
                    piece = rolled[head // 4][(at - head) % 4][key * 16 : (key + 1) * 16]
                    block = piece if block is None else jnp.where(slot == at, piece, block)
                spread_from[head * LINES : (head + 1) * LINES, group * 128 : (group + 1) * 128] = block[:LINES]
        flat = sum(dot(part, spread) for part in two_parts(spread_from[...]))
        apart = levels_differ if last is None else levels_differ | (rows_differ & last)
        flat = jnp.where(apart, MASKED, flat)
        for o in range(WLON):
            start = (WLON - 1 - o) * LINES
            tile, shift = divmod(start, 128)
            parts = [flat[:, t * 128 : (t + 1) * 128] for t in range(tile, min(tile + 3, 3))]
            if shift:
                parts = [pltpu.roll(part, 128 - shift, 1) for part in parts]
                parts = [jnp.where(kept < 128 - shift, a, b) for a, b in zip(parts, parts[1:] + parts[-1:], strict=True)]
            piece = jnp.concatenate([parts[0], parts[1][:, : CELLS - 128]], axis=-1)
            for head in range(6):
                out_of(head, o * LINES, piece[head * LINES : (head + 1) * LINES])


def writer(out_ref, base):
    def write(head, at, piece):
        out_ref[base + head, at : at + LINES, :] = piece

    return write


def reader(table_ref, row, base):
    return lambda head: table_ref[row, base + head, :, 0, :]


def attend_group(q, k, v, bias, heads):
    queries, width = q.shape
    of_head = iota((queries, width), 1) // HD
    big = jnp.concatenate([jnp.where(of_head == h, q, 0.0) for h in range(heads)], axis=0)
    scores = dot_nt(big.astype(bf16), k) * HD ** (-0.5) + bias.reshape(heads * queries, CELLS)
    top = jnp.max(scores, axis=-1, keepdims=True)
    weights = jnp.exp(scores - top)
    total = jnp.sum(weights, axis=-1, keepdims=True)
    mixed = dot(weights.astype(bf16), v) * (1.0 / total)
    out = jnp.zeros((queries, width), f32)
    for h in range(heads):
        out = jnp.where(of_head == h, mixed[h * queries : (h + 1) * queries], out)
    return out


def tiles_of(rows, width):
    return ((-(-width // 128), rows, 128), f32)


def put(ref, at, rows, stride, values):
    width = values.shape[-1]
    for t in range(ref.shape[0]):
        piece = values[:, t * 128 : min((t + 1) * 128, width)]
        if piece.shape[-1] < 128:
            piece = jnp.concatenate([piece, jnp.zeros((rows, 128 - piece.shape[-1]), f32)], axis=-1)
        ref[t, pl.ds(at, rows, stride=stride), :] = piece


def get(ref, at, rows, stride, width):
    pieces = [ref[t, pl.ds(at, rows, stride=stride), :] for t in range(ref.shape[0])]
    return jnp.concatenate(pieces, axis=-1)[:, :width]


def pack_lines(first, second):
    return jnp.concatenate(first + [jnp.concatenate([second[i], second[3 + i]], axis=-1) for i in range(3)], axis=0)


def unpack_line(packed, i, size):
    first = packed[i * size : (i + 1) * size]
    at = (6 + i % 3) * size
    second = packed[at : at + size, i // 3 * 64 : i // 3 * 64 + 64]
    return jnp.concatenate([first, second], axis=-1)


def expand_first(fine_ref, bias0_ref, stacked, spread_from):
    expand_bias([(reader(fine_ref, 0, 0), None)], [writer(bias0_ref, 0)], stacked, spread_from)


def expand_others(last, fine_ref, coarse_ref, bias1_ref, bias2_ref, stacked, spread_from):
    tables = [(reader(fine_ref, 1, 0), last), (reader(coarse_ref, 0, 0), last), (reader(coarse_ref, 0, 6), last)]
    expand_bias(tables, [writer(bias1_ref, 0), writer(bias2_ref, 0), writer(bias2_ref, 6)], stacked, spread_from)


def place():
    lat, lats = lax.axis_index("lat"), lax.axis_size("lat")
    lon, lons = lax.axis_index("lon"), lax.axis_size("lon")
    early = ((lat < lats // 2) & (lon < lons // 2)) | ((lat == 0) & (lon >= lons - lons // 8))
    return lat == lats - 1, early


def prepare_kernel(
    fields_hbm, fine_hbm, coarse_hbm, qkv_hbm, proj_hbm, below_ref, corner_ref, own_ref, fine_ref,
    coarse_ref, qkv_ref, proj_ref, bias0_ref, bias1_ref, bias2_ref, line_ref, stacked, spread_from, sems,
):
    last, early = place()
    moves = [
        (fields_hbm.at[:, 0:3], own_ref.at[:, 0:3]),
        (fine_hbm, fine_ref),
        (coarse_hbm, coarse_ref),
        (fields_hbm.at[:, 3:12], own_ref.at[:, 3:12]),
        (qkv_hbm, qkv_ref),
        (proj_hbm, proj_ref),
    ]
    copies = [pltpu.make_async_copy(source, to, sems.at[i]) for i, (source, to) in enumerate(moves)]
    for copy in copies:
        copy.start()
    copies[0].wait()
    lines = [own_ref[z, a].astype(f32) for z in range(WZ) for a in range(3)]
    packed = pack_lines([line[:, :128] for line in lines], [line[:, 128:] for line in lines])
    for ref, start in ((below_ref, 0), (corner_ref, 6)):
        for i in range(9):
            line_ref[i * 18 : (i + 1) * 18, :] = packed[i * 24 + start : i * 24 + start + 18]
        ref[...] = line_ref[...].astype(bf16)

    for copy in copies[1:]:
        copy.wait()

    @pl.when(early)
    def _():
        expand_first(fine_ref, bias0_ref, stacked, spread_from)
        expand_others(last, fine_ref, coarse_ref, bias1_ref, bias2_ref, stacked, spread_from)


def other_bias_kernel(
    fine_ref, coarse_ref, early1_ref, early2_ref, after_ref, bias1_ref, bias2_ref, stacked, spread_from
):
    last, early = place()

    @pl.when(early)
    def _():
        bias1_ref[...] = early1_ref[...]
        bias2_ref[...] = early2_ref[...]

    @pl.when(jnp.logical_not(early))
    def _():
        expand_others(last, fine_ref, coarse_ref, bias1_ref, bias2_ref, stacked, spread_from)


def attend_fine(x_ref, bias_ref, qkv_ref, proj_ref):
    normed = normalise(get(x_ref, 72, 432, 1, 192))
    q = dot(normed, qkv_ref[:, 0:192]).astype(bf16).astype(f32)
    k = dot(normed, qkv_ref[:, 192:384]).astype(bf16)
    v = dot(normed, qkv_ref[:, 384:576]).astype(bf16)
    left, right = [], []
    for window, start, stop in ((0, 72, 144), (1, 0, 144), (2, 0, 72)):
        at = window * CELLS
        q_rows = q[at + start : at + stop]
        k_rows, v_rows = k[at : at + CELLS], v[at : at + CELLS]
        bias = bias_ref[:, start:stop, :]
        left.append(attend_group(q_rows[:, :128], k_rows[:, :128], v_rows[:, :128], bias[:4], 4))
        right.append(attend_group(q_rows[:, 128:], k_rows[:, 128:], v_rows[:, 128:], bias[4:], 2))
    left = jnp.concatenate(left, axis=0).astype(bf16)
    right = jnp.concatenate(right, axis=0).astype(bf16)
    product = dot(left, proj_ref[0:128, :]) + dot(right, proj_ref[128:192, :])
    return (get(x_ref, 144, 288, 1, 192) + product).astype(bf16)


def first_rows_kernel(
    left_ref, own_ref, fine_ref, early0_ref, qkv_ref, proj_ref, up_hbm, down_hbm,
    out_ref, send_ref, up_ref, down_ref, bias0_ref, x_ref, a_ref, stacked, spread_from, sems,
):
    moves = [(up_hbm, up_ref), (down_hbm, down_ref)]
    copies = [pltpu.make_async_copy(source, to, sems.at[i]) for i, (source, to) in enumerate(moves)]
    for copy in copies:
        copy.start()
    _, early = place()

    @pl.when(jnp.logical_not(early))
    def _():
        expand_first(fine_ref, bias0_ref, stacked, spread_from)

    @pl.when(early)
    def _():
        bias0_ref[...] = early0_ref[...]

    for z in range(WZ):
        for a in range(WLAT):
            put(x_ref, z * WLAT + a, 24, LINES, left_ref[z, 3 + a].astype(f32))
            put(x_ref, 288 + z * WLAT + a, 24, LINES, own_ref[z, 3 + a].astype(f32))
    attended = attend_fine(x_ref, bias0_ref, qkv_ref, proj_ref)
    out_ref[...] = attended
    put(a_ref, 0, 288, 1, attended.astype(f32))
    lines = [a_ref[t, pl.ds(z * WLAT + a, 24, stride=LINES), :] for t in range(2) for z in range(WZ) for a in range(3)]
    send_ref[...] = pack_lines(lines[:6], [line[:, :64] for line in lines[6:]]).astype(bf16)
    for copy in copies:
        copy.wait()


def second_rows_kernel(
    left_ref, own_ref, corner_ref, below_ref, first_ref, bias1_ref, qkv_ref, proj_ref, up_ref, down_ref,
    out_ref, x_ref, a_ref, w_ref,
):
    below, corner = below_ref[...].astype(f32), corner_ref[...].astype(f32)
    for z in range(WZ):
        for a in range(WLAT):
            at = z * WLAT + a
            if a < 3:
                put(x_ref, at, 24, LINES, left_ref[z, 9 + a].astype(f32))
                put(x_ref, 288 + at, 24, LINES, own_ref[z, 9 + a].astype(f32))
            else:
                put(x_ref, 72 + at, 18, LINES, unpack_line(corner, z * 3 + a - 3, 18))
                put(x_ref, 288 + at, 18, LINES, unpack_line(below, z * 3 + a - 3, 18))
    put(a_ref, 0, 288, 1, first_ref[...].astype(f32))
    put(a_ref, 288, 288, 1, attend_fine(x_ref, bias1_ref, qkv_ref, proj_ref).astype(f32))
    for t in range(2):
        for rho in range(3, 12):
            for z in range(WZ):
                at = rho // WLAT * 288 + z * WLAT + rho % WLAT
                to = ((rho - 3) * WZ + z) * 24
                w_ref[t, to : to + 24, :] = a_ref[t, pl.ds(at, 24, stride=LINES), :]
    for i in range(3):
        x = get(w_ref, i * 144, 144, 1, 192)
        out_ref[i * 144 : (i + 1) * 144, :] = fine_feed_forward(x, up_ref, down_ref).astype(bf16)


def coarse_kernel(
    y_ref, got_ref, fine_up_ref, fine_down_ref, merge_ref, bias_ref, qkv_ref, proj_ref, up_ref, down_ref,
    keep_ref, lower_ref, left_ref, corner_ref, again_ref, w_ref, p_ref, o_ref,
):
    got = got_ref[...].astype(f32)
    got = jnp.concatenate([unpack_line(got, z * 3 + a, 24) for a in range(3) for z in range(WZ)], axis=0)
    put(w_ref, 0, 432, 1, y_ref[...].astype(f32))
    put(w_ref, 432, 144, 1, fine_feed_forward(got, fine_up_ref, fine_down_ref))
    parts = []
    for pa in range(2):
        for pb in range(2):
            for t in range(2):
                for z in range(WZ):
                    for i in range(WLAT):
                        at = ((2 * i + pa) * WZ + z) * 24 + pb
                        line = w_ref[t, pl.ds(at, WLON, stride=2), :]
                        p_ref[t, pl.ds(len(parts) * CELLS + z * WLAT + i, WLON, stride=LINES), :] = line
            parts.append(get(p_ref, len(parts) * CELLS, CELLS, 1, 192))
    mean = sum(jnp.sum(part, axis=-1, keepdims=True) for part in parts) * (1.0 / 768)
    parts = [part - mean for part in parts]
    variance = sum(jnp.sum(part * part, axis=-1, keepdims=True) for part in parts) * (1.0 / 768)
    scale = lax.rsqrt(variance + EPSILON)
    merged = sum(
        dot((part * scale).astype(bf16), merge_ref[i * 192 : (i + 1) * 192, :]) for i, part in enumerate(parts)
    )
    merged = merged.astype(bf16).astype(f32)
    normed = normalise(merged)
    qkv = dot(normed, qkv_ref[...]).astype(bf16)
    product = merged
    for g in range(3):
        q = qkv[:, g * 128 : (g + 1) * 128].astype(f32)
        k = qkv[:, 384 + g * 128 : 384 + (g + 1) * 128]
        v = qkv[:, 768 + g * 128 : 768 + (g + 1) * 128]
        mixed = attend_group(q, k, v, bias_ref[g * 4 : (g + 1) * 4], 4)
        product = product + dot(mixed.astype(bf16), proj_ref[g * 128 : (g + 1) * 128, :])
    attended = product.astype(bf16).astype(f32)
    put(o_ref, 0, CELLS, 1, feed_forward(attended, up_ref, down_ref))
    for i in range(3):
        for j in range(WLON):
            for refs, row in (((left_ref, again_ref), i), ((corner_ref,), 3 + i)) if j < 6 else (((keep_ref,), i), ((lower_ref,), 3 + i)):
                cell = get(o_ref, j * LINES + row, WZ, WLAT, 384).astype(bf16)
                for ref in refs:
                    ref[i, j % 6] = cell


def call(kernel, outs, scratch, operands, flops):
    specs = [pl.BlockSpec(memory_space=pltpu.VMEM)] * len(operands)
    return pl.pallas_call(
        kernel,
        out_shape=[jax.ShapeDtypeStruct(shape, dtype) for shape, dtype in outs],
        in_specs=specs,
        out_specs=[pl.BlockSpec(memory_space=pltpu.VMEM)] * len(outs),
        scratch_shapes=[pltpu.VMEM(shape, dtype) for shape, dtype in scratch],
        compiler_params=pltpu.CompilerParams(vmem_limit_bytes=VMEM_LIMIT),
        cost_estimate=pl.CostEstimate(
            flops=flops,
            bytes_accessed=sum(a.size * a.dtype.itemsize for a in operands),
            transcendentals=0,
        ),
    )(*operands)


def body(
    fields,
    fine_bias,
    fine_qkv,
    fine_proj,
    fine_up,
    fine_down,
    merge_weight,
    coarse_bias,
    coarse_qkv,
    coarse_proj,
    coarse_up,
    coarse_down,
):
    lats = lax.axis_size("lat")
    fine_tables = fine_bias.transpose(0, 2, 3, 1, 4)
    coarse_tables = coarse_bias.transpose(0, 2, 3, 1, 4)
    fine_down = fine_down.T
    expansion = [((6 * 32, CELLS), f32), ((6 * LINES, LINES * 32), f32)]
    biases = [((6, CELLS, CELLS), f32), ((12, CELLS, CELLS), f32)]
    left = from_behind(fields, 1, 0)
    sources = [fields, fine_tables, coarse_tables, fine_qkv, fine_proj]
    hbm, vmem = (pl.BlockSpec(memory_space=space) for space in (pltpu.HBM, pltpu.VMEM))
    below, corner, own, fine_tables, coarse_tables, fine_qkv, fine_proj, bias0, bias1, bias2 = pl.pallas_call(
        prepare_kernel,
        out_shape=[jax.ShapeDtypeStruct((162, 128), bf16)] * 2
        + [jax.ShapeDtypeStruct(source.shape, source.dtype) for source in sources]
        + [jax.ShapeDtypeStruct(shape, dtype) for shape, dtype in [((6, CELLS, CELLS), f32)] + biases],
        in_specs=[hbm] * 5,
        out_specs=[vmem] * 10,
        scratch_shapes=[pltpu.VMEM((162, 128), f32)]
        + [pltpu.VMEM(shape, dtype) for shape, dtype in expansion]
        + [pltpu.SemaphoreType.DMA((6,))],
        compiler_params=pltpu.CompilerParams(vmem_limit_bytes=VMEM_LIMIT),
    )(*(pltpu.with_memory_space_constraint(source, pltpu.HBM) for source in sources))
    corner = from_behind(corner, 1, -1)
    below = from_behind(below, 0, -1)
    weights = [fine_up, fine_down]
    first, edge, fine_up, fine_down = pl.pallas_call(
        first_rows_kernel,
        out_shape=[jax.ShapeDtypeStruct((288, 192), bf16), jax.ShapeDtypeStruct((216, 128), bf16)]
        + [jax.ShapeDtypeStruct(weight.shape, weight.dtype) for weight in weights],
        in_specs=[vmem] * 6 + [hbm] * 2,
        out_specs=[vmem] * 4,
        scratch_shapes=[
            pltpu.VMEM(shape, dtype)
            for shape, dtype in [((6, CELLS, CELLS), f32), tiles_of(576, 192), tiles_of(288, 192)] + expansion
        ]
        + [pltpu.SemaphoreType.DMA((2,))],
        compiler_params=pltpu.CompilerParams(vmem_limit_bytes=VMEM_LIMIT),
    )(
        *[left, own, fine_tables, bias0, fine_qkv, fine_proj],
        *(pltpu.with_memory_space_constraint(weight, pltpu.HBM) for weight in weights),
    )
    got = from_behind(edge, 0, -1)
    bias1, bias2 = call(
        other_bias_kernel,
        biases,
        expansion,
        [fine_tables, coarse_tables, bias1, bias2, first],
        2_000_000_000,
    )
    (finished,) = call(
        second_rows_kernel,
        [((432, 192), bf16)],
        [tiles_of(576, 192), tiles_of(576, 192), tiles_of(432, 192)],
        [left, own, corner, below, first, bias1, fine_qkv, fine_proj, fine_up, fine_down],
        3_000_000_000,
    )
    quarter = ((3, 6, WZ, 384), bf16)
    keep, lower, first_left, far_corner, other_left = call(
        coarse_kernel,
        [quarter] * 5,
        [tiles_of(576, 192), tiles_of(576, 192), tiles_of(CELLS, 384)],
        [finished, got, fine_up, fine_down, merge_weight, bias2, coarse_qkv, coarse_proj, coarse_up, coarse_down],
        4_000_000_000,
    )
    above = from_behind(lower, 0, 1)
    band = lats // 2 + 1
    right = from_behind(first_left, -1, 0, lambda a: a == band)
    corner = from_behind(far_corner, -1, 1)
    other = from_behind(other_left, -1, 0, lambda a: a != band)
    above, right, corner, other = lax.optimization_barrier((above, right, corner, other))
    right = right + other
    rows = [jnp.concatenate([above, corner], axis=1), jnp.concatenate([keep, right], axis=1)]
    return jnp.concatenate(rows, axis=0).transpose(2, 0, 1, 3)


def solution(mesh):
    return jax.shard_map(
        body,
        mesh=mesh,
        in_specs=(
            P(None, "lat", "lon", None),
            P("lat", None, None, None, None),
            P(),
            P(),
            P(),
            P(),
            P(),
            P("lat", None, None, None, None),
            P(),
            P(),
            P(),
            P(),
        ),
        out_specs=P(None, "lat", "lon", None),
        check_vma=False,
    )
```
